32 devices in a mesh: section: 2 (over x), dp: 16 (over z, y, core).
Axes of the slice: x: 2, y: 2, z: 4, core: 2. Of those that a mesh axis runs over, the one named last changes fastest.
Arguments:
- inputs: bfloat16 [2, 4096, 512], P('section', 'dp'), may hold values from -6 to 6
- lengths: int32 [32, 2, 16], P('dp'), may hold values from 0 to 128, as said below
- w_qkv: bfloat16 [2, 512, 1536], P('section'), may hold values from -0.25 to 0.25
- w_attn_out: bfloat16 [2, 512, 512], P('section'), may hold values from -0.5 to 0.5
- w_cross: bfloat16 [2, 512, 1024], P('section'), may hold values from -0.25 to 0.25
- w_up: bfloat16 [2, 512, 2048], P('section'), may hold values from -0.25 to 0.25
- w_down: bfloat16 [2, 2048, 512], P('section'), may hold values from -0.125 to 0.125
- cotangent: bfloat16 [2, 4096, 512], P('section', 'dp'), may hold values from -6 to 6
Outputs:
- outputs: bfloat16 [2, 4096, 512], P('section', 'dp')
- input_grad: bfloat16 [2, 4096, 512], P('section', 'dp')
- grad_qkv: float32 [2, 512, 1536], P('section')
- grad_attn_out: float32 [2, 512, 512], P('section')
- grad_cross: float32 [2, 512, 1024], P('section')
- grad_up: float32 [2, 512, 2048], P('section')
- grad_down: float32 [2, 2048, 512], P('section')
The draws below stay inside these ranges and needn't reach their ends.
Inputs may be any that keep to these rules, and one draw needn't show every extreme that they name: For each micro-batch g, lengths[g, 0, :] and lengths[g, 1, :] each sum to 128; a slot's source length is 0 exactly when its target length is 0; some micro-batch holds a single pair of 128 source and 128 target tokens.
All inputs are finite; a program needn't handle non-finite values.
Results may differ from the reference program's by a relative error of at most 0.018.
Values may be sent and summed in bfloat16 or wider, within the bound.
No kernel may reach another device: no remote copies, remote signals or barrier semaphores. Data moves between devices by JAX's collectives and lax.ppermute only.
A program may use at most 256 MiB of HBM per device.

```python
import jax
import jax.numpy as jnp
from jax import lax

D = 512
HEADS = 8
HEAD_DIM = 64
FF = 2048
ROWS = 128
SLOTS = 16
MB = 2
GROUPS = 32
TOKENS = 4096
N_DP = 16


def draw_lengths(key, part):
    key = jax.random.fold_in(key, 7)
    key_short, key_long, key_forced = jax.random.split(key, 3)
    pair_sum = 2 * ROWS // SLOTS
    first_len = jax.random.randint(key_short, (GROUPS, 2, SLOTS // 2), 1, pair_sum)
    short_rows = jnp.stack([first_len, pair_sum - first_len], axis=-1).reshape(GROUPS, 2, SLOTS)
    forced = jax.random.randint(key_forced, (), 0, GROUPS)
    is_long = (jax.random.randint(key_long, (GROUPS,), 0, 8) == 0) | (jnp.arange(GROUPS) == forced)
    long_row = jnp.where(jnp.arange(SLOTS) == 0, ROWS, 0)
    return jnp.where(is_long[:, None, None], long_row[None, None, :], short_rows).astype(jnp.int32)


def steps_of(stream_key, shape, cuts, least, high):
    def one(axis_at, parts):
        heights = jax.random.uniform(jax.random.fold_in(jax.random.fold_in(stream_key, 6), axis_at), (parts,), jnp.float32, least / len(cuts), high / len(cuts))
        return jnp.repeat(jnp.exp(heights), shape[axis_at] // parts).reshape((-1,) + (1,) * (len(shape) - axis_at - 1))

    loudness = one(*cuts[0])
    for cut in cuts[1:]:
        loudness = loudness * one(*cut)
    return loudness


def bell_draw(rng, dims, width, reach, cuts=(), held_as=jnp.bfloat16):
    entries = width * jax.random.normal(rng, dims, jnp.float32)
    if cuts:
        entries = entries * steps_of(rng, dims, cuts, -0.22, 0.18)
    return jnp.clip(entries, -reach, reach).astype(held_as)


def setup_inputs(seed: int = 0) -> dict:
    seeds = jax.random.split(jax.random.key(seed), 9)
    return {
        "inputs": bell_draw(seeds[0], (2, TOKENS, D), 1.0, 6.0, ((0, 2), (1, 16))),
        "lengths": draw_lengths(jax.random.fold_in(seeds[8], 71), 0),
        "w_qkv": bell_draw(seeds[2], (2, D, 3 * D), D ** -0.5, 0.25, ((0, 2),)),
        "w_attn_out": bell_draw(seeds[3], (2, D, D), (D // 4) ** -0.5, 0.5, ((0, 2),)),
        "w_cross": bell_draw(seeds[4], (2, D, 2 * D), D ** -0.5, 0.25, ((0, 2),)),
        "w_up": bell_draw(seeds[5], (2, D, FF), D ** -0.5, 0.25, ((0, 2),)),
        "w_down": bell_draw(seeds[6], (2, FF, D), FF ** -0.5, 0.125, ((0, 2),)),
        "cotangent": bell_draw(seeds[7], (2, TOKENS, D), 1.0, 6.0, ((0, 2), (1, 16))),
    }


exact_mode = lax.Precision.HIGHEST

@jax.custom_vjp
def low(v):
    return lax.optimization_barrier(v.astype(jnp.bfloat16)).astype(jnp.float32)

@jax.custom_vjp
def low_back(v):
    return v

def low_keep(v):
    return (low(v), None)

def low_pass(kept, grad):
    return (grad,)

def back_keep(v):
    return (v, None)

def back_low(kept, grad):
    return (low(grad),)
low.defvjp(low_keep, low_pass)
low_back.defvjp(back_keep, back_low)

def product(left, right):
    return jnp.dot(left, right, precision=exact_mode)

def segments(pair_lengths, position):
    pair_ends = jnp.cumsum(pair_lengths)
    return lax.optimization_barrier(jnp.sum((position[:, None] >= pair_ends[None, :]).astype(jnp.int32), axis=1))

def attention(query_in, keys_in, values_in, mask_in):
    rows_query = query_in.shape[0]
    rows_keys = keys_in.shape[0]
    query_heads = query_in.reshape(rows_query, HEADS, HEAD_DIM)
    keys_heads = keys_in.reshape(rows_keys, HEADS, HEAD_DIM)
    values_heads = values_in.reshape(rows_keys, HEADS, HEAD_DIM)
    scores = low_back(jnp.einsum('qhd,khd->hqk', query_heads, keys_heads, precision=exact_mode) * HEAD_DIM ** (-0.5))
    scores = jnp.where(mask_in[None], scores, -1e+30)
    probs = jax.nn.softmax(scores, axis=-1)
    mixed_heads = jnp.einsum('hqk,khd->qhd', low(probs), values_heads, precision=exact_mode)
    return low_back(low(mixed_heads.reshape(rows_query, HEADS * HEAD_DIM)))

def feed_forward(residual, w_grow, w_shrink):
    hidden = low_back(product(low(residual), w_grow))
    active = low(jax.nn.gelu(hidden))
    return low_back(product(active, w_shrink))

def pair_forward(source, target, pair_lengths, w_qkv, w_attn_out, w_cross, w_up, w_down):
    position = jnp.arange(ROWS)
    seg_src = segments(pair_lengths[0], position)
    seg_tgt = segments(pair_lengths[1], position)
    own_src = seg_src[:, None] == seg_src[None, :]
    own_tgt = (seg_tgt[:, None] == seg_tgt[None, :]) & (position[:, None] >= position[None, :])
    across = seg_tgt[:, None] == seg_src[None, :]
    enc_proj = low_back(low(product(source, w_qkv[0])))
    enc_mix = attention(enc_proj[:, :D], enc_proj[:, D:2 * D], enc_proj[:, 2 * D:], own_src)
    enc_mid = source + low_back(product(enc_mix, w_attn_out[0]))
    memory = enc_mid + feed_forward(enc_mid, w_up[0], w_down[0])
    link_keys = low_back(low(product(low(memory), w_cross[0])))
    dec_proj = low_back(low(product(target, w_qkv[1])))
    dec_mix = attention(dec_proj[:, :D], dec_proj[:, D:2 * D], dec_proj[:, 2 * D:], own_tgt)
    dec_mid = target + low_back(product(dec_mix, w_attn_out[1]))
    cross_query = low_back(low(product(low(dec_mid), w_cross[1][:, :D])))
    cross_mix = attention(cross_query, link_keys[:, :D], link_keys[:, D:], across)
    dec_cross = dec_mid + low_back(product(cross_mix, w_cross[1][:, D:]))
    decoded = dec_cross + feed_forward(dec_cross, w_up[1], w_down[1])
    return (memory, decoded)

def reference(inputs, lengths, w_qkv, w_attn_out, w_cross, w_up, w_down, cotangent):
    groups = N_DP * MB
    source = inputs[0].astype(jnp.float32).reshape(groups, ROWS, D)
    target = inputs[1].astype(jnp.float32).reshape(groups, ROWS, D)
    weights = tuple((weight.astype(jnp.float32) for weight in (w_qkv, w_attn_out, w_cross, w_up, w_down)))

    def forward(source, target, weight_qkv, weight_out, weight_cross, weight_up, weight_down):

        def single(packed):
            return pair_forward(packed[0], packed[1], packed[2], weight_qkv, weight_out, weight_cross, weight_up, weight_down)
        return lax.map(jax.checkpoint(single), (source, target, lengths))
    (memory, decoded), pullback = jax.vjp(forward, source, target, *weights)
    later_grad = cotangent[0].astype(jnp.float32).reshape(groups, ROWS, D)
    final_grad = cotangent[1].astype(jnp.float32).reshape(groups, ROWS, D)
    gradients = pullback((later_grad, final_grad))
    outputs = jnp.stack([memory.reshape(-1, D), decoded.reshape(-1, D)]).astype(jnp.bfloat16)
    input_grad = jnp.stack([gradients[0].reshape(-1, D), gradients[1].reshape(-1, D)]).astype(jnp.bfloat16)
    return (outputs, input_grad, gradients[2], gradients[3], gradients[4], gradients[5], gradients[6])
```

```python
import functools

import jax
import jax.numpy as jnp
from jax import lax
from jax.experimental import pallas as pl
from jax.experimental.pallas import tpu as pltpu
from jax.sharding import PartitionSpec as P

D = 512
HEADS = 8
HEAD_DIM = 64
FF = 2048
ROWS = 128
SLOTS = 16
MB = 2
PAIRS = HEADS // 2
LANES = 2 * HEAD_DIM
HALF = D // 2
SCALE = HEAD_DIM ** (-0.5)
GELU_IN = 0.7978845608028654
GELU_CUBE = 0.044715
LOW = jnp.bfloat16
F32 = jnp.float32
VMEM_LIMIT = 48 * 1024 * 1024

CROSS_AT, UP_AT, DOWN_AT, OUT_AT, QKV_AT = 0, 2, 6, 10, 11
BLOCKS = 14
EARLY = 10
LATE = BLOCKS - EARLY


def mm(left, right):
    return jnp.dot(left, right, preferred_element_type=F32)


def mm_nt(left, right):
    return lax.dot_general(left, right, (((1,), (1,)), ((), ())), preferred_element_type=F32)


def mm_tn(left, right):
    return lax.dot_general(left, right, (((0,), (0,)), ((), ())), preferred_element_type=F32)


def gelu(hidden):
    inner = GELU_IN * (hidden + GELU_CUBE * (hidden * hidden * hidden))
    return hidden * (0.5 * (1.0 + jnp.tanh(inner)))


def gelu_slope(hidden):
    square = hidden * hidden
    inner = GELU_IN * (hidden + GELU_CUBE * (square * hidden))
    bent = jnp.tanh(inner)
    inner_slope = GELU_IN * (1.0 + (3.0 * GELU_CUBE) * square)
    return 0.5 * (1.0 + bent) + 0.5 * hidden * (1.0 - bent * bent) * inner_slope


def segments(lengths_ref, micro, which, dim):
    position = lax.broadcasted_iota(jnp.int32, (ROWS, ROWS), dim)
    end = jnp.int32(0)
    seg = jnp.zeros((ROWS, ROWS), jnp.int32)
    for slot in range(SLOTS):
        end = end + lengths_ref[micro, which, slot]
        seg = seg + (position >= end).astype(jnp.int32)
    return seg


def low_lanes():
    return lax.broadcasted_iota(jnp.int32, (ROWS, LANES), 1) < HEAD_DIM


def two_heads(pair, lanes):
    nothing = jnp.zeros_like(pair)
    return jnp.concatenate(
        [jnp.where(lanes, pair, nothing), jnp.where(lanes, nothing, pair)], axis=0
    )


def softmax(scores):
    highest = jnp.max(scores, axis=1, keepdims=True)
    raised = jnp.exp(scores - highest)
    return raised * (1.0 / jnp.sum(raised, axis=1, keepdims=True))


def attend(read_q, read_k, read_v, mask, write_probs, write_mix):
    lanes = low_lanes()
    for pair in range(PAIRS):
        query = (read_q(pair).astype(F32) * SCALE).astype(LOW)
        scores = mm_nt(query, two_heads(read_k(pair), lanes))
        probs = jnp.concatenate(
            [
                softmax(jnp.where(mask, scores[:, :ROWS], -1e30)),
                softmax(jnp.where(mask, scores[:, ROWS:], -1e30)),
            ],
            axis=1,
        )
        write_probs(pair, probs)
        write_mix(pair, mm(probs.astype(LOW), two_heads(read_v(pair), lanes)).astype(LOW))


def attend_back(read_q, read_k, read_v, read_probs, read_grad, write):
    lanes = low_lanes()
    for pair in range(PAIRS):
        query = (read_q(pair).astype(F32) * SCALE).astype(LOW)
        probs = read_probs(pair)
        grad = read_grad(pair)
        grad_probs = mm_nt(grad, two_heads(read_v(pair), lanes))
        product = probs * grad_probs
        slopes = []
        for head in range(2):
            cut = slice(head * ROWS, (head + 1) * ROWS)
            total = jnp.sum(product[:, cut], axis=1, keepdims=True)
            slopes.append((probs[:, cut] * (grad_probs[:, cut] - total)).astype(LOW))
        probs_low = probs.astype(LOW)
        grad_q = mm(jnp.concatenate(slopes, axis=1), two_heads(read_k(pair), lanes)) * SCALE
        grad_k = mm_tn(jnp.concatenate(slopes, axis=0), two_heads(query, lanes))
        grad_v = mm_tn(
            jnp.concatenate([probs_low[:, :ROWS], probs_low[:, ROWS:]], axis=0),
            two_heads(grad, lanes),
        )
        write(pair, grad_q.astype(LOW), grad_k.astype(LOW), grad_v.astype(LOW))


def columns(ref, start):
    def read(pair):
        return ref[:, start + pair * LANES : start + (pair + 1) * LANES]

    return read


def fetch(source, target, sem):
    copy = pltpu.make_async_copy(source, target, sem)
    copy.start()
    return copy


def forward_kernel(
    micro,
    section_ref,
    lengths_ref,
    tokens_ref,
    w_qkv,
    w_out,
    w_cross,
    w_up,
    w_down,
    proj,
    mix,
    mid_low,
    wide,
    act,
    memory,
    link,
    probs,
    qkv_v,
    out_v,
    cross_v,
    up_v,
    down_v,
    sems,
):
    first = section_ref[0] == 0
    get_qkv = fetch(w_qkv.at[0], qkv_v, sems.at[0])
    get_out = fetch(w_out.at[0], out_v, sems.at[1])
    get_cross = pltpu.make_async_copy(w_cross.at[0], cross_v, sems.at[2])
    get_up = pltpu.make_async_copy(w_up.at[0], up_v, sems.at[3])
    get_down = pltpu.make_async_copy(w_down.at[0], down_v, sems.at[4])

    @pl.when(first)
    def _():
        get_up.start()
        get_down.start()

    get_cross.start()

    tokens = tokens_ref[0, micro * ROWS : (micro + 1) * ROWS, :]
    seg_q_src = segments(lengths_ref, micro, 0, 0)
    seg_k_src = segments(lengths_ref, micro, 0, 1)
    seg_q_tgt = segments(lengths_ref, micro, 1, 0)
    seg_k_tgt = segments(lengths_ref, micro, 1, 1)
    later = lax.broadcasted_iota(jnp.int32, (ROWS, ROWS), 0) >= lax.broadcasted_iota(
        jnp.int32, (ROWS, ROWS), 1
    )
    source_mask = (seg_q_src == seg_k_src).astype(jnp.int32)
    target_mask = ((seg_q_tgt == seg_k_tgt) & later).astype(jnp.int32)
    mask = jnp.where(first, source_mask, target_mask) != 0

    get_qkv.wait()
    for part in range(3):
        cut = slice(part * D, (part + 1) * D)
        proj[:, cut] = mm(tokens, qkv_v[:, cut]).astype(LOW)

    def write_probs(pair, value):
        probs[pair] = value

    def write_mix(pair, value):
        mix[:, pair * LANES : (pair + 1) * LANES] = value

    attend(columns(proj, 0), columns(proj, D), columns(proj, 2 * D), mask, write_probs, write_mix)
    get_out.wait()
    mid = tokens.astype(F32) + mm(mix[...], out_v[...])
    mid_low[...] = mid.astype(LOW)

    @pl.when(first)
    def _():
        get_up.wait()
        get_down.wait()
        total = mid
        for part in range(4):
            cut = slice(part * D, (part + 1) * D)
            hidden = mm(mid_low[...], up_v[:, cut])
            wide[:, cut] = hidden
            act[:, cut] = gelu(hidden).astype(LOW)
            total = total + mm(act[:, cut], down_v[cut, :])
        memory[...] = total.astype(LOW)
        get_cross.wait()
        for part in range(2):
            cut = slice(part * D, (part + 1) * D)
            link[:, cut] = mm(memory[...], cross_v[:, cut]).astype(LOW)

    @pl.when(jnp.logical_not(first))
    def _():
        wide[:, :D] = mid
        get_cross.wait()
        link[:, :D] = mm(mid_low[...], cross_v[:, :D]).astype(LOW)


def whole():
    return pl.BlockSpec(memory_space=pltpu.VMEM)


def in_smem():
    return pl.BlockSpec(memory_space=pltpu.SMEM)


def anywhere():
    return pl.BlockSpec(memory_space=pl.ANY)


def forward_stage(micro, section, lengths, tokens, weights):
    shapes = (
        ((ROWS, 3 * D), LOW),
        ((ROWS, D), LOW),
        ((ROWS, D), LOW),
        ((ROWS, FF), F32),
        ((ROWS, FF), LOW),
        ((ROWS, D), LOW),
        ((ROWS, 2 * D), LOW),
        ((PAIRS, ROWS, 2 * ROWS), F32),
    )
    return pl.pallas_call(
        functools.partial(forward_kernel, micro),
        out_shape=[jax.ShapeDtypeStruct(s, t) for s, t in shapes],
        in_specs=[in_smem(), in_smem(), whole()] + [anywhere()] * 5,
        out_specs=[pl.BlockSpec(memory_space=pltpu.VMEM)] * len(shapes),
        scratch_shapes=[
            pltpu.VMEM((D, 3 * D), LOW),
            pltpu.VMEM((D, D), LOW),
            pltpu.VMEM((D, 2 * D), LOW),
            pltpu.VMEM((D, FF), LOW),
            pltpu.VMEM((FF, D), LOW),
            pltpu.SemaphoreType.DMA((5,)),
        ],
        compiler_params=pltpu.CompilerParams(vmem_limit_bytes=VMEM_LIMIT),
        cost_estimate=pl.CostEstimate(
            flops=2 * ROWS * D * 7168, bytes_accessed=10_000_000, transcendentals=400_000
        ),
        name="forward_stage",
    )(section, lengths, tokens, *weights)


def middle_kernel(
    micro,
    section_ref,
    lengths_ref,
    mid_ref,
    query_ref,
    link_ref,
    cotangent_ref,
    w_cross,
    w_up,
    w_down,
    decoded,
    link_grad,
    cross_low,
    cross_mix,
    act,
    grad_hidden,
    cross_grad_low,
    query_grad,
    cross_grad,
    cross_v,
    up_v,
    down_v,
    hidden_v,
    probs_v,
    mixed_v,
    mid_v,
    query_v,
    sems,
):
    @pl.when(section_ref[0] != 0)
    def _():
        get_query = fetch(query_ref.at[:, pl.ds(0, D)], query_v, sems.at[3])
        get_mid = fetch(mid_ref.at[:, pl.ds(0, D)], mid_v, sems.at[4])
        get_cross = fetch(w_cross.at[0], cross_v, sems.at[0])
        get_up = fetch(w_up.at[0], up_v, sems.at[1])
        get_down = fetch(w_down.at[0], down_v, sems.at[2])
        mask = segments(lengths_ref, micro, 1, 0) == segments(lengths_ref, micro, 0, 1)

        def write_probs(pair, value):
            probs_v[pair] = value

        def write_mix(pair, value):
            cross_mix[:, pair * LANES : (pair + 1) * LANES] = value

        read_q, read_k, read_v = columns(query_v, 0), columns(link_ref, 0), columns(link_ref, D)
        get_query.wait()
        attend(read_q, read_k, read_v, mask, write_probs, write_mix)
        get_mid.wait()
        get_cross.wait()
        after = mid_v[...] + mm(cross_mix[...], cross_v[:, D:])
        cross_low[...] = after.astype(LOW)
        get_up.wait()
        get_down.wait()
        total = after
        for part in range(4):
            cut = slice(part * D, (part + 1) * D)
            hidden = mm(cross_low[...], up_v[:, cut])
            hidden_v[:, cut] = hidden
            act[:, cut] = gelu(hidden).astype(LOW)
            total = total + mm(act[:, cut], down_v[cut, :])
        decoded[...] = total.astype(LOW)
        grad_low = cotangent_ref[0, micro * ROWS : (micro + 1) * ROWS, :]
        grad = grad_low.astype(F32)
        for part in range(4):
            cut = slice(part * D, (part + 1) * D)
            grad_act = mm_nt(grad_low, down_v[cut, :])
            grad_hidden[:, cut] = (gelu_slope(hidden_v[:, cut]) * grad_act).astype(LOW)
            grad = grad + mm_nt(grad_hidden[:, cut], up_v[:, cut])
        cross_grad[...] = grad
        cross_grad_low[...] = grad.astype(LOW)
        mixed_v[...] = mm_nt(cross_grad_low[...], cross_v[:, D:]).astype(LOW)

        def write(pair, grad_q, grad_k, grad_v):
            query_grad[:, pair * LANES : (pair + 1) * LANES] = grad_q
            link_grad[:, pair * LANES : (pair + 1) * LANES] = grad_k
            link_grad[:, D + pair * LANES : D + (pair + 1) * LANES] = grad_v

        attend_back(read_q, read_k, read_v, lambda pair: probs_v[pair], columns(mixed_v, 0), write)


def middle_stage(micro, section, lengths, mid, query, link, cotangent, w_cross, w_up, w_down):
    shapes = (
        ((ROWS, D), LOW),
        ((ROWS, 2 * D), LOW),
        ((ROWS, D), LOW),
        ((ROWS, D), LOW),
        ((ROWS, FF), LOW),
        ((ROWS, FF), LOW),
        ((ROWS, D), LOW),
        ((ROWS, D), LOW),
        ((ROWS, D), F32),
    )
    return pl.pallas_call(
        functools.partial(middle_kernel, micro),
        out_shape=[jax.ShapeDtypeStruct(s, t) for s, t in shapes],
        in_specs=[
            in_smem(),
            in_smem(),
            anywhere(),
            anywhere(),
            whole(),
            whole(),
            anywhere(),
            anywhere(),
            anywhere(),
        ],
        out_specs=[pl.BlockSpec(memory_space=pltpu.VMEM)] * len(shapes),
        scratch_shapes=[
            pltpu.VMEM((D, 2 * D), LOW),
            pltpu.VMEM((D, FF), LOW),
            pltpu.VMEM((FF, D), LOW),
            pltpu.VMEM((ROWS, FF), F32),
            pltpu.VMEM((PAIRS, ROWS, 2 * ROWS), F32),
            pltpu.VMEM((ROWS, D), LOW),
            pltpu.VMEM((ROWS, D), F32),
            pltpu.VMEM((ROWS, D), LOW),
            pltpu.SemaphoreType.DMA((5,)),
        ],
        compiler_params=pltpu.CompilerParams(vmem_limit_bytes=VMEM_LIMIT),
        cost_estimate=pl.CostEstimate(
            flops=2 * ROWS * D * 10000, bytes_accessed=8_000_000, transcendentals=600_000
        ),
        name="middle_stage",
    )(section, lengths, mid, query, link, cotangent, w_cross, w_up, w_down)


def put_block(core, keep, send, at, left_ref, left_at, right):
    own = pl.ds(pl.multiple_of(left_at + core * HALF, HALF), HALF)
    other = pl.ds(pl.multiple_of(left_at + (1 - core) * HALF, HALF), HALF)
    send[at] = mm_tn(left_ref[:, other], right).astype(LOW)
    keep[at] = mm_tn(left_ref[:, own], right)


def early_kernel(
    section_ref,
    core_ref,
    cotangent_ref,
    memory0,
    memory1,
    lg0,
    lg1,
    mid0,
    mid1,
    wide0,
    wide1,
    act0,
    act1,
    cl0,
    cl1,
    cm0,
    cm1,
    dact0,
    dact1,
    gh0,
    gh1,
    cgl0,
    cgl1,
    qg0,
    qg1,
    cg0,
    cg1,
    w_cross,
    w_up,
    w_down,
    keep,
    send,
    residual,
    a_v,
    b_v,
    z_v,
    g_v,
    act_v,
    gh_v,
    wide_v,
    lg_v,
    cross_v,
    up_v,
    down_v,
    sems,
):
    core = core_ref[0]
    first = section_ref[0] == 0
    get_cross = fetch(w_cross.at[0], cross_v, sems.at[0])

    def both(pair_refs, target, at):
        return [
            fetch(ref, target.at[pl.ds(i * ROWS, ROWS)], sems.at[at + i])
            for i, ref in enumerate(pair_refs)
        ]

    @pl.when(first)
    def _():
        gets_lg = both((lg0, lg1), lg_v, 1)
        gets_mem = both((memory0, memory1), a_v, 3)
        get_down = fetch(w_down.at[0], down_v, sems.at[5])
        gets_wide = both((wide0, wide1), wide_v, 6)
        gets_act = both((act0, act1), act_v, 8)
        get_up = fetch(w_up.at[0], up_v, sems.at[10])
        gets_z = both((mid0, mid1), z_v, 11)
        for copy in gets_lg:
            copy.wait()
        get_cross.wait()
        grad = cotangent_ref[0].astype(F32) + mm_nt(lg_v[...], cross_v[...])
        g_v[...] = grad.astype(LOW)
        for copy in gets_mem:
            copy.wait()
        for part in range(2):
            put_block(core, keep, send, CROSS_AT + part, a_v, 0, lg_v[:, part * D : (part + 1) * D])
        get_down.wait()
        for copy in gets_wide + gets_act + gets_z:
            copy.wait()
        get_up.wait()
        for part in range(4):
            cut = slice(part * D, (part + 1) * D)
            grad_act = mm_nt(g_v[...], down_v[cut, :])
            gh_v[:, cut] = (gelu_slope(wide_v[:, cut]) * grad_act).astype(LOW)
            grad = grad + mm_nt(gh_v[:, cut], up_v[:, cut])
            put_block(core, keep, send, UP_AT + part, z_v, 0, gh_v[:, cut])
            put_block(core, keep, send, DOWN_AT + part, act_v, part * D, g_v[...])
        residual[...] = grad

    @pl.when(jnp.logical_not(first))
    def _():
        gets = both((dact0, dact1), act_v, 1) + both((gh0, gh1), gh_v, 3)
        gets_z = both((cl0, cl1), z_v, 5)
        gets_q = both((qg0, qg1), lg_v.at[:, :D], 7) + both((cgl0, cgl1), lg_v.at[:, D:], 9)
        gets_a = both((mid0, mid1), a_v, 11) + both((cm0, cm1), b_v, 13)
        gets_c = both((cg0, cg1), wide_v.at[:, :D], 15)
        for copy in gets_q + gets_a + gets_c:
            copy.wait()
        get_cross.wait()
        put_block(core, keep, send, CROSS_AT, a_v, 0, lg_v[:, :D])
        put_block(core, keep, send, CROSS_AT + 1, b_v, 0, lg_v[:, D:])
        residual[...] = wide_v[:, :D] + mm_nt(lg_v[:, :D], cross_v[:, :D])
        for copy in gets + gets_z:
            copy.wait()
        for part in range(4):
            cut = slice(part * D, (part + 1) * D)
            put_block(core, keep, send, UP_AT + part, z_v, 0, gh_v[:, cut])
            put_block(core, keep, send, DOWN_AT + part, act_v, part * D, cotangent_ref[0])


def early_stage(section, core, cotangent, ones, twos, weights):
    operands = [section, core, cotangent]
    for name in ("memory", "lg", "mid_low", "wide", "act"):
        operands += [one[name] for one in ones]
    for name in (
        "cross_low",
        "cross_mix",
        "act",
        "grad_hidden",
        "cross_grad_low",
        "query_grad",
        "cross_grad",
    ):
        operands += [two[name] for two in twos]
    operands += list(weights)
    return pl.pallas_call(
        early_kernel,
        out_shape=[
            jax.ShapeDtypeStruct((EARLY, HALF, D), F32),
            jax.ShapeDtypeStruct((EARLY, HALF, D), LOW),
            jax.ShapeDtypeStruct((MB * ROWS, D), F32),
        ],
        in_specs=[in_smem(), in_smem(), whole()] + [anywhere()] * (len(operands) - 3),
        out_specs=[pl.BlockSpec(memory_space=pltpu.VMEM)] * 3,
        scratch_shapes=[
            pltpu.VMEM((MB * ROWS, D), LOW),
            pltpu.VMEM((MB * ROWS, D), LOW),
            pltpu.VMEM((MB * ROWS, D), LOW),
            pltpu.VMEM((MB * ROWS, D), LOW),
            pltpu.VMEM((MB * ROWS, FF), LOW),
            pltpu.VMEM((MB * ROWS, FF), LOW),
            pltpu.VMEM((MB * ROWS, FF), F32),
            pltpu.VMEM((MB * ROWS, 2 * D), LOW),
            pltpu.VMEM((D, 2 * D), LOW),
            pltpu.VMEM((D, FF), LOW),
            pltpu.VMEM((FF, D), LOW),
            pltpu.SemaphoreType.DMA((17,)),
        ],
        compiler_params=pltpu.CompilerParams(vmem_limit_bytes=VMEM_LIMIT),
        cost_estimate=pl.CostEstimate(
            flops=2 * 256 * D * 10000, bytes_accessed=20_000_000, transcendentals=500_000
        ),
        name="early_stage",
    )(*operands)


def late_kernel(
    section_ref,
    core_ref,
    tokens_ref,
    residual_ref,
    mix0,
    mix1,
    proj0,
    proj1,
    probs0,
    probs1,
    memory0,
    memory1,
    decoded0,
    decoded1,
    w_qkv,
    w_out,
    keep,
    send,
    outputs,
    input_grad,
    mix_v,
    proj_v,
    probs_v,
    final_v,
    g_v,
    mixed_v,
    gp_v,
    qkv_v,
    out_v,
    sems,
):
    core = core_ref[0]
    first = section_ref[0] == 0
    get_out = fetch(w_out.at[0], out_v, sems.at[0])
    gets_probs = [fetch(r, probs_v.at[i], sems.at[1 + i]) for i, r in enumerate((probs0, probs1))]
    gets_proj = [fetch(r, proj_v.at[i], sems.at[3 + i]) for i, r in enumerate((proj0, proj1))]

    def both(pair_refs, target, at):
        return [
            fetch(ref, target.at[pl.ds(i * ROWS, ROWS)], sems.at[at + i])
            for i, ref in enumerate(pair_refs)
        ]

    gets_mix = both((mix0, mix1), mix_v, 5)
    get_qkv = fetch(w_qkv.at[0], qkv_v, sems.at[7])

    @pl.when(first)
    def _():
        for copy in both((memory0, memory1), final_v, 8):
            copy.wait()

    @pl.when(jnp.logical_not(first))
    def _():
        for copy in both((decoded0, decoded1), final_v, 8):
            copy.wait()

    outputs[0] = final_v[...]
    g_v[...] = residual_ref[...].astype(LOW)
    get_out.wait()
    mixed_v[...] = mm_nt(g_v[...], out_v[...]).astype(LOW)
    for copy in gets_probs + gets_proj:
        copy.wait()
    for micro in range(MB):
        rows = slice(micro * ROWS, (micro + 1) * ROWS)

        def write(pair, grad_q, grad_k, grad_v, rows=rows):
            for part, value in enumerate((grad_q, grad_k, grad_v)):
                at = part * D + pair * LANES
                gp_v[rows, at : at + LANES] = value

        attend_back(
            columns(proj_v.at[micro], 0),
            columns(proj_v.at[micro], D),
            columns(proj_v.at[micro], 2 * D),
            lambda pair, micro=micro: probs_v[micro, pair],
            columns(mixed_v.at[pl.ds(micro * ROWS, ROWS)], 0),
            write,
        )
    for copy in gets_mix:
        copy.wait()
    put_block(core, keep, send, 0, mix_v, 0, g_v[...])
    for part in range(3):
        put_block(core, keep, send, 1 + part, tokens_ref.at[0], 0, gp_v[:, part * D : (part + 1) * D])
    get_qkv.wait()
    input_grad[0] = (residual_ref[...] + mm_nt(gp_v[...], qkv_v[...])).astype(LOW)


def late_stage(section, core, tokens, residual, ones, twos, w_qkv, w_out):
    operands = [section, core, tokens, residual]
    for name in ("mix", "proj", "probs", "memory"):
        operands += [one[name] for one in ones]
    operands += [two["decoded"] for two in twos]
    operands += [w_qkv, w_out]
    return pl.pallas_call(
        late_kernel,
        out_shape=[
            jax.ShapeDtypeStruct((LATE, HALF, D), F32),
            jax.ShapeDtypeStruct((LATE, HALF, D), LOW),
            jax.ShapeDtypeStruct((1, MB * ROWS, D), LOW),
            jax.ShapeDtypeStruct((1, MB * ROWS, D), LOW),
        ],
        in_specs=[in_smem(), in_smem(), whole(), whole()] + [anywhere()] * (len(operands) - 4),
        out_specs=[pl.BlockSpec(memory_space=pltpu.VMEM)] * 4,
        scratch_shapes=[
            pltpu.VMEM((MB * ROWS, D), LOW),
            pltpu.VMEM((MB, ROWS, 3 * D), LOW),
            pltpu.VMEM((MB, PAIRS, ROWS, 2 * ROWS), F32),
            pltpu.VMEM((MB * ROWS, D), LOW),
            pltpu.VMEM((MB * ROWS, D), LOW),
            pltpu.VMEM((MB * ROWS, D), LOW),
            pltpu.VMEM((MB * ROWS, 3 * D), LOW),
            pltpu.VMEM((D, 3 * D), LOW),
            pltpu.VMEM((D, D), LOW),
            pltpu.SemaphoreType.DMA((10,)),
        ],
        compiler_params=pltpu.CompilerParams(vmem_limit_bytes=VMEM_LIMIT),
        cost_estimate=pl.CostEstimate(
            flops=2 * 256 * D * 5000, bytes_accessed=12_000_000, transcendentals=1000
        ),
        name="late_stage",
    )(*operands)


def chip_sum_kernel(keep_a, got_a, keep_b, got_b, total):
    total[:EARLY] = (keep_a[...] + got_a[...].astype(F32)).astype(LOW)
    total[EARLY:] = (keep_b[...] + got_b[...].astype(F32)).astype(LOW)


def chip_sum(keep_a, got_a, keep_b, got_b):
    return pl.pallas_call(
        chip_sum_kernel,
        out_shape=jax.ShapeDtypeStruct((BLOCKS, HALF, D), LOW),
        in_specs=[pl.BlockSpec(memory_space=pltpu.VMEM)] * 4,
        out_specs=pl.BlockSpec(memory_space=pltpu.VMEM),
        compiler_params=pltpu.CompilerParams(vmem_limit_bytes=VMEM_LIMIT),
        name="chip_sum",
    )(keep_a, got_a, keep_b, got_b)


def unpack_kernel(core_ref, own, other, g_qkv, g_out, g_cross, g_up, g_down, slots, sems):
    core = core_ref[0]
    places = (
        [(g_cross.at[0, :, pl.ds(p * D, D)]) for p in range(2)]
        + [(g_up.at[0, :, pl.ds(p * D, D)]) for p in range(4)]
        + [(g_down.at[0, pl.ds(p * D, D), :]) for p in range(4)]
        + [g_out.at[0]]
        + [(g_qkv.at[0, :, pl.ds(p * D, D)]) for p in range(3)]
    )
    depth = slots.shape[0]
    here = pl.ds(pl.multiple_of(core * HALF, HALF), HALF)
    there = pl.ds(pl.multiple_of((1 - core) * HALF, HALF), HALF)
    copies = []
    for block, place in enumerate(places):
        slot = block % depth
        if block >= depth:
            copies[block - depth].wait()
        slots[slot, here, :] = own[block].astype(F32)
        slots[slot, there, :] = other[block].astype(F32)
        copies.append(fetch(slots.at[slot], place, sems.at[slot]))
    for copy in copies[-depth:]:
        copy.wait()


def unpack(core, own, other):
    shapes = ((1, D, 3 * D), (1, D, D), (1, D, 2 * D), (1, D, FF), (1, FF, D))
    return pl.pallas_call(
        unpack_kernel,
        out_shape=[jax.ShapeDtypeStruct(s, F32) for s in shapes],
        in_specs=[in_smem(), whole(), whole()],
        out_specs=[anywhere()] * 5,
        scratch_shapes=[pltpu.VMEM((4, D, D), F32), pltpu.SemaphoreType.DMA((4,))],
        compiler_params=pltpu.CompilerParams(vmem_limit_bytes=VMEM_LIMIT),
        name="unpack",
    )(core, own, other)


def ring_groups(count):
    chips = count // 2
    across = 2 if chips % 2 == 0 else 1
    along = chips // across
    order = [z * across for z in range(along)]
    if across == 2:
        order += [z * across + 1 for z in reversed(range(along))]
    return [[2 * chip + core for chip in order] for core in range(2)]


def swap_cores(value, count):
    return lax.ppermute(value, "dp", [(i, i ^ 1) for i in range(count)])


def on_device(inputs, lengths, w_qkv, w_attn_out, w_cross, w_up, w_down, cotangent):
    count = lax.axis_size("dp")
    section = lax.axis_index("section").astype(jnp.int32).reshape(1)
    core = (lax.axis_index("dp") % 2).astype(jnp.int32).reshape(1)
    weights = (w_qkv, w_attn_out, w_cross, w_up, w_down)
    names_one = ("proj", "mix", "mid_low", "wide", "act", "memory", "link", "probs")
    names_two = (
        "decoded",
        "link_grad",
        "cross_low",
        "cross_mix",
        "act",
        "grad_hidden",
        "cross_grad_low",
        "query_grad",
        "cross_grad",
    )
    ones, twos = [], []
    for micro in range(MB):
        one = dict(
            zip(names_one, forward_stage(micro, section, lengths, inputs, weights))
        )
        one["arrived"] = lax.ppermute(one["link"], "section", [(0, 1)])
        ones.append(one)
    for micro in range(MB):
        one = ones[micro]
        two = dict(
            zip(
                names_two,
                middle_stage(
                    micro,
                    section,
                    lengths,
                    one["wide"],
                    one["link"],
                    one["arrived"],
                    cotangent,
                    w_cross,
                    w_up,
                    w_down,
                ),
            )
        )
        one["lg"] = lax.ppermute(two["link_grad"], "section", [(1, 0)])
        twos.append(two)
    keep_a, send_a, residual = early_stage(
        section, core, cotangent, ones, twos, (w_cross, w_up, w_down)
    )
    got_a = swap_cores(send_a, count)
    keep_b, send_b, outputs, input_grad = late_stage(
        section, core, inputs, residual, ones, twos, w_qkv, w_attn_out
    )
    got_b = swap_cores(send_b, count)
    total = chip_sum(keep_a, got_a, keep_b, got_b).reshape(BLOCKS * HALF, D)
    groups = ring_groups(count)
    piece = lax.psum_scatter(
        total, "dp", scatter_dimension=0, tiled=True, axis_index_groups=groups
    )
    own = lax.all_gather(piece, "dp", axis=0, tiled=True, axis_index_groups=groups)
    other = swap_cores(own, count)
    grads = unpack(
        core, own.reshape(BLOCKS, HALF, D), other.reshape(BLOCKS, HALF, D)
    )
    return (outputs, input_grad, *grads)


def solution(mesh):
    return jax.shard_map(
        on_device,
        mesh=mesh,
        in_specs=(
            P("section", "dp", None),
            P("dp", None, None),
            P("section", None, None),
            P("section", None, None),
            P("section", None, None),
            P("section", None, None),
            P("section", None, None),
            P("section", "dp", None),
        ),
        out_specs=(
            P("section", "dp", None),
            P("section", "dp", None),
            P("section", None, None),
            P("section", None, None),
            P("section", None, None),
            P("section", None, None),
            P("section", None, None),
        ),
        check_vma=False,
    )
```

```python
import functools

import jax
import jax.numpy as jnp
from jax import lax
from jax.experimental import pallas as pl
from jax.experimental.pallas import tpu as pltpu
from jax.sharding import PartitionSpec as P

D = 512
HEADS = 8
HEAD_DIM = 64
FF = 2048
ROWS = 128
SLOTS = 16
MB = 2
PAIRS = HEADS // 2
LANES = 2 * HEAD_DIM
HALF = D // 2
SCALE = HEAD_DIM ** (-0.5)
GELU_IN = 0.7978845608028654
GELU_CUBE = 0.044715
LOW = jnp.bfloat16
F32 = jnp.float32
SPLIT = True

CROSS_AT, UP_AT, DOWN_AT, OUT_AT, QKV_AT = 0, 2, 6, 10, 11
BLOCKS = 14
EARLY = 10
LATE = BLOCKS - EARLY


def mm(left, right):
    return jnp.dot(left, right, preferred_element_type=F32)


def mm_nt(left, right):
    return lax.dot_general(left, right, (((1,), (1,)), ((), ())), preferred_element_type=F32)


def mm_tn(left, right):
    return lax.dot_general(left, right, (((0,), (0,)), ((), ())), preferred_element_type=F32)


def gelu(hidden):
    inner = GELU_IN * (hidden + GELU_CUBE * (hidden * hidden * hidden))
    return hidden * (0.5 * (1.0 + jnp.tanh(inner)))


def gelu_slope(hidden):
    square = hidden * hidden
    inner = GELU_IN * (hidden + GELU_CUBE * (square * hidden))
    bent = jnp.tanh(inner)
    inner_slope = GELU_IN * (1.0 + (3.0 * GELU_CUBE) * square)
    return 0.5 * (1.0 + bent) + 0.5 * hidden * (1.0 - bent * bent) * inner_slope


def segments(lengths_ref, micro, which, dim):
    position = lax.broadcasted_iota(jnp.int32, (ROWS, ROWS), dim)
    end = jnp.int32(0)
    seg = jnp.zeros((ROWS, ROWS), jnp.int32)
    for slot in range(SLOTS):
        end = end + lengths_ref[micro, which, slot]
        seg = seg + (position >= end).astype(jnp.int32)
    return seg


def low_lanes():
    return lax.broadcasted_iota(jnp.int32, (ROWS, LANES), 1) < HEAD_DIM


def two_heads(pair, lanes):
    nothing = jnp.zeros_like(pair)
    return jnp.concatenate(
        [jnp.where(lanes, pair, nothing), jnp.where(lanes, nothing, pair)], axis=0
    )


def softmax(scores):
    highest = jnp.max(scores, axis=1, keepdims=True)
    raised = jnp.exp(scores - highest)
    return raised * (1.0 / jnp.sum(raised, axis=1, keepdims=True))


def attend(read_q, read_k, read_v, mask, write_probs, write_mix):
    lanes = low_lanes()
    for pair in range(PAIRS):
        query = (read_q(pair).astype(F32) * SCALE).astype(LOW)
        scores = mm_nt(query, two_heads(read_k(pair), lanes))
        probs = jnp.concatenate(
            [
                softmax(jnp.where(mask, scores[:, :ROWS], -1e30)),
                softmax(jnp.where(mask, scores[:, ROWS:], -1e30)),
            ],
            axis=1,
        )
        write_probs(pair, probs)
        write_mix(pair, mm(probs.astype(LOW), two_heads(read_v(pair), lanes)).astype(LOW))


def attend_back(read_q, read_k, read_v, read_probs, read_grad, write):
    lanes = low_lanes()
    for pair in range(PAIRS):
        query = (read_q(pair).astype(F32) * SCALE).astype(LOW)
        probs = read_probs(pair)
        grad = read_grad(pair)
        grad_probs = mm_nt(grad, two_heads(read_v(pair), lanes))
        product = probs * grad_probs
        slopes = []
        for head in range(2):
            cut = slice(head * ROWS, (head + 1) * ROWS)
            total = jnp.sum(product[:, cut], axis=1, keepdims=True)
            slopes.append((probs[:, cut] * (grad_probs[:, cut] - total)).astype(LOW))
        probs_low = probs.astype(LOW)
        grad_q = mm(jnp.concatenate(slopes, axis=1), two_heads(read_k(pair), lanes)) * SCALE
        grad_k = mm_tn(jnp.concatenate(slopes, axis=0), two_heads(query, lanes))
        grad_v = mm_tn(
            jnp.concatenate([probs_low[:, :ROWS], probs_low[:, ROWS:]], axis=0),
            two_heads(grad, lanes),
        )
        write(pair, grad_q.astype(LOW), grad_k.astype(LOW), grad_v.astype(LOW))


def columns(ref, rows, start):
    def read(pair):
        return ref[rows, start + pair * LANES : start + (pair + 1) * LANES]

    return read


def fetch(source, target, sem):
    copy = pltpu.make_async_copy(source, target, sem)
    copy.start()
    return copy


STATE = {
    "proj": ((MB * ROWS, 3 * D), LOW),
    "mix": ((MB * ROWS, D), LOW),
    "probs": ((MB, PAIRS, ROWS, 2 * ROWS), F32),
    "wide": ((MB * ROWS, FF), F32),
    "act": ((MB * ROWS, FF), LOW),
    "narrow": ((MB * ROWS, D), LOW),
    "result": ((MB * ROWS, D), LOW),
    "mid_low": ((MB * ROWS, D), LOW),
    "query": ((MB * ROWS, D), LOW),
    "across": ((MB * ROWS, ROWS), F32),
}
BACK = {
    "cross_mix": ((MB * ROWS, D), LOW),
    "grad_hidden": ((MB * ROWS, FF), LOW),
    "grad_low": ((MB * ROWS, D), LOW),
    "query_grad": ((MB * ROWS, D), LOW),
    "grad": ((MB * ROWS, D), F32),
}
WEIGHTS = {
    "w_qkv": ((D, 3 * D), LOW),
    "w_out": ((D, D), LOW),
    "w_cross": ((D, 2 * D), LOW),
    "w_up": ((D, FF), LOW),
    "w_down": ((FF, D), LOW),
}
HELD = {"tokens": ((MB * ROWS, D), LOW), "cotangent": ((MB * ROWS, D), LOW)}


def shaped(table):
    return [pltpu.VMEM(shape, kind) for shape, kind in table.values()]


def same_shape(arrays):
    return [pltpu.VMEM(value.shape, value.dtype) for value in arrays]


def held(arrays):
    return [pltpu.with_memory_space_constraint(value, pltpu.VMEM) for value in arrays]


def left(arrays):
    return [pltpu.with_memory_space_constraint(value, pltpu.HBM) for value in arrays]


def in_vmem():
    return pl.BlockSpec(memory_space=pltpu.VMEM)


def in_smem():
    return pl.BlockSpec(memory_space=pltpu.SMEM)


def in_hbm():
    return pl.BlockSpec(memory_space=pltpu.HBM)


def call(kernel, name, place, reads, keeps, makes, scratch=(), vmem_mib=16, cost=(0, 0)):
    kept = list(keeps)
    out_shape = same_shape(keeps.values()) + shaped(makes)
    read_count, kept_count, made_count = len(reads), len(kept), len(makes)

    def body(place_ref, *refs):
        refs = list(refs)
        named = dict(zip(reads, refs[:read_count]))
        refs = refs[read_count + kept_count :]
        named.update(zip(kept, refs[:kept_count]))
        named.update(zip(makes, refs[kept_count : kept_count + made_count]))
        kernel(place_ref, named, *refs[kept_count + made_count :])

    results = pl.pallas_call(
        body,
        out_shape=out_shape,
        in_specs=[in_smem()] + [in_vmem()] * (read_count + kept_count),
        out_specs=[in_vmem()] * len(out_shape),
        scratch_shapes=list(scratch),
        input_output_aliases={1 + read_count + i: i for i in range(kept_count)},
        compiler_params=pltpu.CompilerParams(vmem_limit_bytes=vmem_mib * 1024 * 1024),
        cost_estimate=pl.CostEstimate(flops=cost[0], bytes_accessed=cost[1], transcendentals=0),
        name=name,
    )(place, *held(reads.values()), *held(keeps.values()))
    return dict(zip(list(kept) + list(makes), results))


def forward_step(micro, first, lengths_ref, ref, link, ready):
    rows = slice(micro * ROWS, (micro + 1) * ROWS)
    ready("lengths")
    seg_q_tgt = segments(lengths_ref, micro, 1, 0)
    seg_k_src = segments(lengths_ref, micro, 0, 1)
    ref["across"][rows, :] = (seg_q_tgt == seg_k_src).astype(F32)
    later = lax.broadcasted_iota(jnp.int32, (ROWS, ROWS), 0) >= lax.broadcasted_iota(
        jnp.int32, (ROWS, ROWS), 1
    )
    source_mask = (segments(lengths_ref, micro, 0, 0) == seg_k_src).astype(jnp.int32)
    target_mask = ((seg_q_tgt == segments(lengths_ref, micro, 1, 1)) & later).astype(jnp.int32)
    mask = jnp.where(first, source_mask, target_mask) != 0
    ready("tokens")
    tokens = ref["tokens"][rows, :]
    proj, mix, probs = ref["proj"], ref["mix"], ref["probs"]
    ready("w_qkv")
    for part in range(3):
        cut = slice(part * D, (part + 1) * D)
        proj[rows, cut] = mm(tokens, ref["w_qkv"][:, cut]).astype(LOW)

    def write_probs(pair, value):
        probs[micro, pair] = value

    def write_mix(pair, value):
        mix[rows, pair * LANES : (pair + 1) * LANES] = value

    attend(
        columns(proj, rows, 0),
        columns(proj, rows, D),
        columns(proj, rows, 2 * D),
        mask,
        write_probs,
        write_mix,
    )
    ready("w_out")
    mid = tokens.astype(F32) + mm(mix[rows, :], ref["w_out"][...])

    @pl.when(first)
    def _():
        narrow, act, result = ref["narrow"], ref["act"], ref["result"]
        narrow[rows, :] = mid.astype(LOW)
        ready("w_up")
        ready("w_down")
        total = mid
        for part in range(4):
            cut = slice(part * D, (part + 1) * D)
            hidden = mm(narrow[rows, :], ref["w_up"][:, cut])
            ref["wide"][rows, cut] = hidden
            act[rows, cut] = gelu(hidden).astype(LOW)
            total = total + mm(act[rows, cut], ref["w_down"][cut, :])
        result[rows, :] = total.astype(LOW)
        ready("w_cross")
        for part in range(2):
            cut = slice(part * D, (part + 1) * D)
            link[:, cut] = mm(result[rows, :], ref["w_cross"][:, cut]).astype(LOW)

    @pl.when(jnp.logical_not(first))
    def _():
        ref["mid_low"][rows, :] = mid.astype(LOW)
        ref["wide"][rows, :D] = mid
        ready("w_up")
        ready("w_down")
        ready("w_cross")
        ref["query"][rows, :] = mm(ref["mid_low"][rows, :], ref["w_cross"][:, :D]).astype(LOW)


FETCHED = ("lengths", "tokens", "w_qkv", "w_out", "w_up", "w_down", "w_cross", "cotangent")


def first_kernel(place_ref, *refs):
    inputs = refs[: len(FETCHED)]
    outs = list(WEIGHTS) + list(HELD) + list(STATE)
    ref = dict(zip(outs, refs[len(FETCHED) :]))
    link, lengths_ref, sems = refs[len(FETCHED) + len(outs) :]
    copies = {}
    for at, (name, source) in enumerate(zip(FETCHED, inputs)):
        if name == "lengths":
            copies[name] = fetch(source, lengths_ref, sems.at[at])
        else:
            copies[name] = fetch(source.at[0], ref[name], sems.at[at])
    forward_step(0, place_ref[0] == 0, lengths_ref, ref, link, lambda name: copies[name].wait())
    copies["cotangent"].wait()


def first_stage(place, lengths, tokens, cotangent, weights):
    given = {"lengths": lengths, "tokens": tokens, "cotangent": cotangent, **weights}
    makes = {**WEIGHTS, **HELD, **STATE, "link": ((ROWS, 2 * D), LOW)}
    results = pl.pallas_call(
        first_kernel,
        out_shape=shaped(makes),
        in_specs=[in_smem()] + [in_hbm()] * len(FETCHED),
        out_specs=[in_vmem()] * len(makes),
        scratch_shapes=[
            pltpu.SMEM((MB, 2, SLOTS), jnp.int32),
            pltpu.SemaphoreType.DMA((len(FETCHED),)),
        ],
        compiler_params=pltpu.CompilerParams(vmem_limit_bytes=16 * 1024 * 1024),
        cost_estimate=pl.CostEstimate(
            flops=2 * ROWS * D * 7168, bytes_accessed=10_000_000, transcendentals=0
        ),
        name="first_stage",
    )(place, *left([given[name] for name in FETCHED]))
    return dict(zip(makes, results))


def second_stage(place, lengths, state):
    reads = {name: state[name] for name in list(WEIGHTS) + ["tokens"]}
    keeps = {name: state[name] for name in STATE}

    def body(place_ref, lengths_hbm, *refs):
        refs = list(refs)
        ref = dict(zip(reads, refs[: len(reads)]))
        refs = refs[len(reads) + len(keeps) :]
        ref.update(zip(keeps, refs[: len(keeps)]))
        link, lengths_ref, sems = refs[len(keeps) :]
        copy = fetch(lengths_hbm, lengths_ref, sems.at[0])
        forward_step(
            1,
            place_ref[0] == 0,
            lengths_ref,
            ref,
            link,
            lambda name: copy.wait() if name == "lengths" else None,
        )

    results = pl.pallas_call(
        body,
        out_shape=same_shape(keeps.values()) + [pltpu.VMEM((ROWS, 2 * D), LOW)],
        in_specs=[in_smem(), in_hbm()] + [in_vmem()] * (len(reads) + len(keeps)),
        out_specs=[in_vmem()] * (len(keeps) + 1),
        scratch_shapes=[
            pltpu.SMEM((MB, 2, SLOTS), jnp.int32),
            pltpu.SemaphoreType.DMA((1,)),
        ],
        input_output_aliases={2 + len(reads) + i: i for i in range(len(keeps))},
        compiler_params=pltpu.CompilerParams(vmem_limit_bytes=16 * 1024 * 1024),
        cost_estimate=pl.CostEstimate(
            flops=2 * ROWS * D * 7168, bytes_accessed=10_000_000, transcendentals=0
        ),
        name="second_stage",
    )(place, *left([lengths]), *held(reads.values()), *held(keeps.values()))
    return dict(zip(list(keeps) + ["link"], results))


def middle_step(micros, ref, link_grad, links, hidden_v, probs_v, mixed_v):
    rows = slice(micros[0] * ROWS, (micros[-1] + 1) * ROWS)
    readers = []
    for at, micro in enumerate(micros):
        mine = slice(micro * ROWS, (micro + 1) * ROWS)
        mask = ref["across"][mine, :] != 0.0
        whole = slice(0, ROWS)
        reads = (
            columns(ref["query"], mine, 0),
            columns(links[at], whole, 0),
            columns(links[at], whole, D),
        )

        def write_probs(pair, value, at=at):
            probs_v[at, pair] = value

        def write_mix(pair, value, mine=mine):
            ref["cross_mix"][mine, pair * LANES : (pair + 1) * LANES] = value

        attend(*reads, mask, write_probs, write_mix)
        readers.append((mine, reads))
    w_back = ref["w_cross"][:, D:]
    after = ref["wide"][rows, :D] + mm(ref["cross_mix"][rows, :], w_back)
    narrow, act = ref["narrow"], ref["act"]
    narrow[rows, :] = after.astype(LOW)
    total = after
    for part in range(4):
        cut = slice(part * D, (part + 1) * D)
        hidden = mm(narrow[rows, :], ref["w_up"][:, cut])
        hidden_v[:, cut] = hidden
        act[rows, cut] = gelu(hidden).astype(LOW)
        total = total + mm(act[rows, cut], ref["w_down"][cut, :])
    ref["result"][rows, :] = total.astype(LOW)
    cotangent = ref["cotangent"][rows, :]
    grad = cotangent.astype(F32)
    for part in range(4):
        cut = slice(part * D, (part + 1) * D)
        grad_act = mm_nt(cotangent, ref["w_down"][cut, :])
        grad_hidden = (gelu_slope(hidden_v[:, cut]) * grad_act).astype(LOW)
        ref["grad_hidden"][rows, cut] = grad_hidden
        grad = grad + mm_nt(grad_hidden, ref["w_up"][:, cut])
    ref["grad"][rows, :] = grad
    ref["grad_low"][rows, :] = grad.astype(LOW)
    mixed_v[...] = mm_nt(ref["grad_low"][rows, :], w_back).astype(LOW)
    for at, (mine, reads) in enumerate(readers):

        def write(pair, grad_q, grad_k, grad_v, mine=mine, at=at):
            ref["query_grad"][mine, pair * LANES : (pair + 1) * LANES] = grad_q
            link_grad[at, :, pair * LANES : (pair + 1) * LANES] = grad_k
            link_grad[at, :, D + pair * LANES : D + (pair + 1) * LANES] = grad_v

        attend_back(
            *reads,
            lambda pair, at=at: probs_v[at, pair],
            columns(mixed_v, slice(at * ROWS, (at + 1) * ROWS), 0),
            write,
        )


def middle_stage(micros, place, state, back, links):
    count = len(micros)
    names = ("query", "across", "wide", "cotangent", "w_cross", "w_up", "w_down")
    reads = {name: state[name] for name in names}
    reads.update({f"link{i}": link for i, link in enumerate(links)})
    keeps = {name: state[name] for name in ("narrow", "act", "result")}
    makes = {"link_grad": ((count, ROWS, 2 * D), LOW)}
    if back is None:
        makes.update(BACK)
    else:
        keeps.update(back)

    def kernel(place_ref, ref, *scratch):
        @pl.when(place_ref[0] != 0)
        def _():
            arrived = [ref[f"link{i}"] for i in range(count)]
            middle_step(micros, ref, ref["link_grad"], arrived, *scratch)

    return call(
        kernel,
        "middle_stage",
        place,
        reads,
        keeps,
        makes,
        scratch=(
            pltpu.VMEM((count * ROWS, FF), F32),
            pltpu.VMEM((count, PAIRS, ROWS, 2 * ROWS), F32),
            pltpu.VMEM((count * ROWS, D), LOW),
        ),
        cost=(2 * count * ROWS * D * 10000, 8_000_000),
    )


def put_block(core, keep, send, at, left_ref, left_at, right):
    own = pl.ds(pl.multiple_of(left_at + core * HALF, HALF), HALF)
    other = pl.ds(pl.multiple_of(left_at + (1 - core) * HALF, HALF), HALF)
    send[at] = mm_tn(left_ref[:, other], right).astype(LOW)
    keep[at] = mm_tn(left_ref[:, own], right)


def back_step(micro, first, ref):
    rows = slice(micro * ROWS, (micro + 1) * ROWS)

    @pl.when(first)
    def _():
        cotangent = ref["cotangent"][rows, :].astype(F32)
        grad = cotangent + mm_nt(ref["link_grad"][...], ref["w_cross"][...])
        grad_low = grad.astype(LOW)
        ref["grad_low"][rows, :] = grad_low
        for part in range(4):
            cut = slice(part * D, (part + 1) * D)
            grad_act = mm_nt(grad_low, ref["w_down"][cut, :])
            grad_hidden = (gelu_slope(ref["wide"][rows, cut]) * grad_act).astype(LOW)
            ref["grad_hidden"][rows, cut] = grad_hidden
            grad = grad + mm_nt(grad_hidden, ref["w_up"][:, cut])
        ref["grad"][rows, :] = grad

    @pl.when(jnp.logical_not(first))
    def _():
        through = mm_nt(ref["query_grad"][rows, :], ref["w_cross"][:, :D])
        ref["grad"][rows, :] = ref["grad"][rows, :] + through


def back_stage(micro, place, state, back, link_grad):
    names = ("cotangent", "w_cross", "w_up", "w_down", "wide")
    reads = {name: state[name] for name in names}
    reads["query_grad"] = back["query_grad"]
    reads["link_grad"] = link_grad
    keeps = {name: back[name] for name in ("grad_hidden", "grad_low", "grad")}

    def kernel(place_ref, ref):
        back_step(micro, place_ref[0] == 0, ref)

    return call(
        kernel,
        "back_stage",
        place,
        reads,
        keeps,
        {},
        cost=(2 * ROWS * D * 5000, 5_000_000),
    )


def early_kernel(place_ref, ref, right_v):
    core = place_ref[1]
    keep, send = ref["keep"], ref["send"]

    @pl.when(place_ref[0] == 0)
    def _():
        for micro in range(MB):
            right_v[micro * ROWS : (micro + 1) * ROWS, :] = ref[f"link_grad{micro}"][...]
        for part in range(2):
            cut = slice(part * D, (part + 1) * D)
            put_block(core, keep, send, CROSS_AT + part, ref["result"], 0, right_v[:, cut])
        right_v[:, :D] = ref["grad_low"][...]

    @pl.when(place_ref[0] != 0)
    def _():
        put_block(core, keep, send, CROSS_AT, ref["mid_low"], 0, ref["query_grad"][...])
        put_block(core, keep, send, CROSS_AT + 1, ref["cross_mix"], 0, ref["grad_low"][...])
        right_v[:, :D] = ref["cotangent"][...]

    for part in range(4):
        cut = slice(part * D, (part + 1) * D)
        put_block(core, keep, send, UP_AT + part, ref["narrow"], 0, ref["grad_hidden"][:, cut])
        put_block(core, keep, send, DOWN_AT + part, ref["act"], part * D, right_v[:, :D])


def early_stage(place, state, back, link_grads):
    reads = {name: state[name] for name in ("cotangent", "narrow", "act", "result", "mid_low")}
    names = ("cross_mix", "grad_hidden", "grad_low", "query_grad")
    reads.update({name: back[name] for name in names})
    reads.update({f"link_grad{i}": value for i, value in enumerate(link_grads)})
    makes = {"keep": ((EARLY, HALF, D), F32), "send": ((EARLY, HALF, D), LOW)}
    return call(
        early_kernel,
        "early_stage",
        place,
        reads,
        {},
        makes,
        scratch=(pltpu.VMEM((MB * ROWS, 2 * D), LOW),),
        cost=(2 * 256 * D * 5000, 20_000_000),
    )


def late_kernel(place_ref, ref, g_v, mixed_v, grad_proj):
    core = place_ref[1]
    keep, send = ref["keep"], ref["send"]
    g_v[...] = ref["grad"][...].astype(LOW)
    mixed_v[...] = mm_nt(g_v[...], ref["w_out"][...]).astype(LOW)
    for micro in range(MB):
        rows = slice(micro * ROWS, (micro + 1) * ROWS)

        def write(pair, grad_q, grad_k, grad_v, rows=rows):
            for part, value in enumerate((grad_q, grad_k, grad_v)):
                at = part * D + pair * LANES
                grad_proj[rows, at : at + LANES] = value

        attend_back(
            columns(ref["proj"], rows, 0),
            columns(ref["proj"], rows, D),
            columns(ref["proj"], rows, 2 * D),
            lambda pair, micro=micro: ref["probs"][micro, pair],
            columns(mixed_v, rows, 0),
            write,
        )
    put_block(core, keep, send, 0, ref["mix"], 0, g_v[...])
    for part in range(3):
        cut = slice(part * D, (part + 1) * D)
        put_block(core, keep, send, 1 + part, ref["tokens"], 0, grad_proj[:, cut])
    grad_in = ref["grad"][...] + mm_nt(grad_proj[...], ref["w_qkv"][...])
    ref["input_grad"][0] = grad_in.astype(LOW)
    ref["outputs"][0] = ref["result"][...]


def late_stage(place, state, grad):
    names = ("tokens", "mix", "proj", "probs", "result", "w_qkv", "w_out")
    reads = {name: state[name] for name in names}
    reads["grad"] = grad
    makes = {
        "keep": ((LATE, HALF, D), F32),
        "send": ((LATE, HALF, D), LOW),
        "outputs": ((1, MB * ROWS, D), LOW),
        "input_grad": ((1, MB * ROWS, D), LOW),
    }
    return call(
        late_kernel,
        "late_stage",
        place,
        reads,
        {},
        makes,
        scratch=(
            pltpu.VMEM((MB * ROWS, D), LOW),
            pltpu.VMEM((MB * ROWS, D), LOW),
            pltpu.VMEM((MB * ROWS, 3 * D), LOW),
        ),
        cost=(2 * 256 * D * 5000, 12_000_000),
    )


def chip_sum_kernel(keep_a, got_a, keep_b, got_b, total):
    total[:EARLY] = (keep_a[...] + got_a[...].astype(F32)).astype(LOW)
    total[EARLY:] = (keep_b[...] + got_b[...].astype(F32)).astype(LOW)


def chip_sum(keep_a, got_a, keep_b, got_b):
    return pl.pallas_call(
        chip_sum_kernel,
        out_shape=jax.ShapeDtypeStruct((BLOCKS, HALF, D), LOW),
        in_specs=[in_vmem()] * 4,
        out_specs=in_vmem(),
        compiler_params=pltpu.CompilerParams(vmem_limit_bytes=16 * 1024 * 1024),
        name="chip_sum",
    )(*held([keep_a, got_a, keep_b, got_b]))


GRADS = (((1, D, 3 * D), F32), ((1, D, D), F32), ((1, D, 2 * D), F32), ((1, D, FF), F32), ((1, FF, D), F32))


def unpack_half(half, packed, grads, slots, sems):
    g_qkv, g_out, g_cross, g_up, g_down = grads
    rows = pl.ds(pl.multiple_of(half * HALF, HALF), HALF)
    places = (
        [g_cross.at[0, rows, pl.ds(p * D, D)] for p in range(2)]
        + [g_up.at[0, rows, pl.ds(p * D, D)] for p in range(4)]
        + [
            g_down.at[0, pl.ds(pl.multiple_of(p * D + half * HALF, HALF), HALF), :]
            for p in range(4)
        ]
        + [g_out.at[0, rows, :]]
        + [g_qkv.at[0, rows, pl.ds(p * D, D)] for p in range(3)]
    )
    copies = []
    for block, place in enumerate(places):
        slots[block] = packed[block * HALF : (block + 1) * HALF, :].astype(F32)
        copies.append(fetch(slots.at[block], place, sems.at[block]))
    for copy in copies:
        copy.wait()


def unpack(place, own, other):
    out_shape = [jax.ShapeDtypeStruct(shape, kind) for shape, kind in GRADS]
    scratch = [pltpu.VMEM((BLOCKS, HALF, D), F32), pltpu.SemaphoreType.DMA((BLOCKS,))]

    def own_kernel(place_ref, packed, *refs):
        unpack_half(place_ref[1], packed, refs[:5], *refs[5:])

    def other_kernel(place_ref, packed, *refs):
        unpack_half(1 - place_ref[1], packed, refs[5:10], *refs[10:])

    grads = pl.pallas_call(
        own_kernel,
        out_shape=out_shape,
        in_specs=[in_smem(), in_vmem()],
        out_specs=[in_hbm()] * 5,
        scratch_shapes=scratch,
        name="unpack_own",
    )(place, own)
    return pl.pallas_call(
        other_kernel,
        out_shape=out_shape,
        in_specs=[in_smem(), in_vmem()] + [in_hbm()] * 5,
        out_specs=[in_hbm()] * 5,
        scratch_shapes=scratch,
        input_output_aliases={2 + i: i for i in range(5)},
        name="unpack_other",
    )(place, other, *grads)


def ring_groups(count):
    chips = count // 2
    across = 2 if chips % 2 == 0 else 1
    along = chips // across
    order = [z * across for z in range(along)]
    if across == 2:
        order += [z * across + 1 for z in reversed(range(along))]
    return [[2 * chip + core for chip in order] for core in range(2)]


def swap_cores(value, count):
    return lax.ppermute(value, "dp", [(i, i ^ 1) for i in range(count)])


def on_device(inputs, lengths, w_qkv, w_attn_out, w_cross, w_up, w_down, cotangent):
    count = lax.axis_size("dp")
    place = jnp.stack([lax.axis_index("section"), lax.axis_index("dp") % 2]).astype(jnp.int32)
    weights = dict(zip(WEIGHTS, (w_qkv, w_attn_out, w_cross, w_up, w_down)))

    def to_decoder(link):
        return lax.ppermute(link, "section", [(0, 1)])

    def to_encoder(link_grad):
        return lax.ppermute(link_grad, "section", [(1, 0)])

    state = first_stage(place, lengths, inputs, cotangent, weights)
    link0 = to_decoder(state.pop("link"))
    state.update(second_stage(place, lengths, state))
    link1 = to_decoder(state.pop("link"))
    if SPLIT:
        back = middle_stage((0,), place, state, None, [link0])
        grad0 = to_encoder(back.pop("link_grad"))
        state.update({name: back.pop(name) for name in ("narrow", "act", "result")})
        back = middle_stage((1,), place, state, back, [link1])
        grad1 = to_encoder(back.pop("link_grad"))
        state.update({name: back.pop(name) for name in ("narrow", "act", "result")})
        link_grads = [grad0[0], grad1[0]]
    else:
        back = middle_stage((0, 1), place, state, None, [link0, link1])
        grads = to_encoder(back.pop("link_grad"))
        state.update({name: back.pop(name) for name in ("narrow", "act", "result")})
        link_grads = [grads[0], grads[1]]
    for micro in range(MB):
        back.update(back_stage(micro, place, state, back, link_grads[micro]))
    early = early_stage(place, state, back, link_grads)
    got_a = swap_cores(early["send"], count)
    late = late_stage(place, state, back["grad"])
    got_b = swap_cores(late["send"], count)
    total = chip_sum(early["keep"], got_a, late["keep"], got_b).reshape(BLOCKS * HALF, D)
    groups = ring_groups(count)
    piece = lax.psum_scatter(
        total, "dp", scatter_dimension=0, tiled=True, axis_index_groups=groups
    )
    own = lax.all_gather(piece, "dp", axis=0, tiled=True, axis_index_groups=groups)
    grads = unpack(place, own, swap_cores(own, count))
    return (late["outputs"], late["input_grad"], *grads)


def solution(mesh):
    return jax.shard_map(
        on_device,
        mesh=mesh,
        in_specs=(
            P("section", "dp", None),
            P("dp", None, None),
            P("section", None, None),
            P("section", None, None),
            P("section", None, None),
            P("section", None, None),
            P("section", None, None),
            P("section", "dp", None),
        ),
        out_specs=(
            P("section", "dp", None),
            P("section", "dp", None),
            P("section", None, None),
            P("section", None, None),
            P("section", None, None),
            P("section", None, None),
            P("section", None, None),
        ),
        check_vma=False,
    )
```

```python
from types import SimpleNamespace

import jax
import jax.numpy as jnp
from jax import lax
from jax.experimental import pallas as pl
from jax.experimental.pallas import tpu as pltpu
from jax.sharding import PartitionSpec as P

D = 512
HEADS = 8
HEAD_DIM = 64
FF = 2048
ROWS = 128
SLOTS = 16
MB = 2
BOTH = MB * ROWS
PAIRS = HEADS // 2
LANES = 2 * HEAD_DIM
HALF = D // 2
SCALE = HEAD_DIM ** (-0.5)
GELU_IN = 0.7978845608028654
GELU_CUBE = 0.044715
LOW = jnp.bfloat16
F32 = jnp.float32
MIB = 1024 * 1024
DP = "dp"
SECTION = "section"
PLACE = 4


def mm(left, right):
    return jnp.dot(left, right, preferred_element_type=F32)


def mm_nt(left, right):
    return lax.dot_general(left, right, (((1,), (1,)), ((), ())), preferred_element_type=F32)


def mm_tn(left, right):
    return lax.dot_general(left, right, (((0,), (0,)), ((), ())), preferred_element_type=F32)


def gelu(hidden):
    inner = GELU_IN * (hidden + GELU_CUBE * (hidden * hidden * hidden))
    return hidden * (0.5 * (1.0 + jnp.tanh(inner)))


def gelu_slope(hidden):
    square = hidden * hidden
    inner = GELU_IN * (hidden + GELU_CUBE * (square * hidden))
    bent = jnp.tanh(inner)
    inner_slope = GELU_IN * (1.0 + (3.0 * GELU_CUBE) * square)
    return 0.5 * (1.0 + bent) + 0.5 * hidden * (1.0 - bent * bent) * inner_slope


def segments(lengths_ref, micro, which, dim):
    position = lax.broadcasted_iota(jnp.int32, (ROWS, ROWS), dim)
    end = jnp.int32(0)
    seg = jnp.zeros((ROWS, ROWS), jnp.int32)
    for slot in range(SLOTS):
        end = end + lengths_ref[micro, which, slot]
        seg = seg + (position >= end).astype(jnp.int32)
    return seg


def low_lanes():
    return lax.broadcasted_iota(jnp.int32, (ROWS, LANES), 1) < HEAD_DIM


def two_heads(pair, lanes):
    nothing = jnp.zeros_like(pair)
    return jnp.concatenate(
        [jnp.where(lanes, pair, nothing), jnp.where(lanes, nothing, pair)], axis=0
    )


def softmax(scores):
    highest = jnp.max(scores, axis=0, keepdims=True)
    raised = jnp.exp(scores - highest)
    return raised * (1.0 / jnp.sum(raised, axis=0, keepdims=True))


def two_halves(value):
    return value[:ROWS, :], value[ROWS:, :]


def attend(read_q, read_k, read_v, mask, write_probs, write_mix):
    lanes = low_lanes()
    for pair in range(PAIRS):
        query = (read_q(pair).astype(F32) * SCALE).astype(LOW)
        scores = mm_nt(two_heads(read_k(pair), lanes), query)
        heads = [softmax(jnp.where(mask, part, -1e30)) for part in two_halves(scores)]
        probs = jnp.concatenate(heads, axis=0)
        write_probs(pair, probs)
        write_mix(pair, mm_tn(probs.astype(LOW), two_heads(read_v(pair), lanes)).astype(LOW))


def attend_back(read_q, read_k, read_v, read_probs, read_grad, write):
    lanes = low_lanes()
    for pair in range(PAIRS):
        query = (read_q(pair).astype(F32) * SCALE).astype(LOW)
        probs = read_probs(pair)
        grad = read_grad(pair)
        grad_probs = mm_nt(two_heads(read_v(pair), lanes), grad)
        slopes = []
        for head, change in zip(two_halves(probs), two_halves(grad_probs)):
            total = jnp.sum(head * change, axis=0, keepdims=True)
            slopes.append((head * (change - total)).astype(LOW))
        slopes = jnp.concatenate(slopes, axis=0)
        grad_q = mm_tn(slopes, two_heads(read_k(pair), lanes)) * SCALE
        grad_k = jnp.where(lanes, *two_halves(mm(slopes, query)))
        grad_v = jnp.where(lanes, *two_halves(mm(probs.astype(LOW), grad)))
        write(pair, grad_q.astype(LOW), grad_k.astype(LOW), grad_v.astype(LOW))


def columns(ref, rows, start):
    def read(pair):
        return ref[rows, start + pair * LANES : start + (pair + 1) * LANES]

    return read


def fetch(source, target, sem):
    copy = pltpu.make_async_copy(source, target, sem)
    copy.start()
    return copy


WEIGHTS = dict(
    w_qkv=((D, 3 * D), LOW),
    w_out=((D, D), LOW),
    w_cross=((D, 2 * D), LOW),
    w_up=((D, FF), LOW),
    w_down=((FF, D), LOW),
)
HELD = dict(tokens=((BOTH, D), LOW), cotangent=((BOTH, D), LOW))
STATE = dict(
    proj=((BOTH, 3 * D), LOW),
    mix=((BOTH, D), LOW),
    probs=((MB, PAIRS, 2 * ROWS, ROWS), F32),
    wide=((BOTH, FF), F32),
    mid=((BOTH, D), F32),
    act=((BOTH, FF), LOW),
    narrow=((BOTH, D), LOW),
    result=((BOTH, D), LOW),
    left_a=((BOTH, D), LOW),
    query=((BOTH, D), LOW),
    across=((BOTH, ROWS), F32),
)
BACK = dict(
    hidden=((BOTH, FF), F32),
    across_mid=((BOTH, D), F32),
    left_b=((BOTH, D), LOW),
    right=((BOTH, 2 * D), LOW),
    grad_hidden=((BOTH, FF), LOW),
    gate=((BOTH, D), LOW),
    grad=((BOTH, D), F32),
    grad_low=((BOTH, D), LOW),
)


def shaped(table):
    return [pltpu.VMEM(shape, kind) for shape, kind in table.values()]


def same_shape(arrays):
    return [pltpu.VMEM(value.shape, value.dtype) for value in arrays]


def held(arrays):
    return [pltpu.with_memory_space_constraint(value, pltpu.VMEM) for value in arrays]


def in_place(place):
    return pltpu.with_memory_space_constraint(place, pltpu.SMEM)


def left(arrays):
    return [pltpu.with_memory_space_constraint(value, pltpu.HBM) for value in arrays]


def in_vmem():
    return pl.BlockSpec(memory_space=pltpu.VMEM)


def in_smem():
    return pl.BlockSpec(memory_space=pltpu.SMEM)


def in_hbm():
    return pl.BlockSpec(memory_space=pltpu.HBM)


TOKEN = ((8, LANES), F32)


def mflop(count):
    return count * 1_000_000, 0


def call(
    kernel, name, place, token, reads, keeps, makes, stores=None, scratch=(), cost=(0, 0), patches=None
):
    stores, patches = stores or {}, patches or {}
    out_shape = same_shape(keeps.values()) + shaped(makes) + shaped(dict(token=TOKEN))
    out_shape += [pltpu.HBM(shape, kind) for shape, kind in stores.values()]
    out_shape += [pltpu.HBM(value.shape, value.dtype) for value in patches.values()]
    reads_n, keeps_n, makes_n = len(reads), len(keeps), len(makes)
    stores_n, patches_n = len(stores), len(patches)
    aliases = {2 + reads_n + i: i for i in range(keeps_n)}
    for i in range(patches_n):
        aliases[2 + reads_n + keeps_n + i] = keeps_n + makes_n + 1 + stores_n + i

    def body(place_ref, token_in, *refs):
        del token_in
        refs = list(refs)
        named = dict(zip(reads, refs[:reads_n]))
        refs = refs[reads_n + keeps_n + patches_n :]
        named.update(zip(keeps, refs[:keeps_n]))
        named.update(zip(makes, refs[keeps_n : keeps_n + makes_n]))
        refs = refs[keeps_n + makes_n :]
        refs[0][...] = jnp.zeros(*TOKEN)
        named.update(zip(stores, refs[1 : 1 + stores_n]))
        refs = refs[1 + stores_n :]
        named.update(zip(patches, refs[:patches_n]))
        kernel(place_ref, SimpleNamespace(**named), *refs[patches_n:])

    results = pl.pallas_call(
        body,
        out_shape=out_shape,
        in_specs=[in_smem()] + [in_vmem()] * (1 + reads_n + keeps_n) + [in_hbm()] * patches_n,
        out_specs=[in_vmem()] * (keeps_n + makes_n + 1) + [in_hbm()] * (stores_n + patches_n),
        scratch_shapes=list(scratch),
        input_output_aliases=aliases,
        compiler_params=pltpu.CompilerParams(vmem_limit_bytes=16 * MIB),
        cost_estimate=pl.CostEstimate(flops=cost[0], bytes_accessed=cost[1], transcendentals=0),
        name=name,
    )(
        in_place(place),
        *held([token]),
        *held(reads.values()),
        *held(keeps.values()),
        *left(patches.values()),
    )
    names = list(keeps) + list(makes)
    token = results[len(names)]
    made = dict(zip(names, results))
    made.update(zip(list(stores) + list(patches), results[len(names) + 1 :]))
    return token, made


def forward_step(micro, first, lengths_ref, ref, link, gets):
    rows = slice(micro * ROWS, (micro + 1) * ROWS)
    gets.lengths.wait()
    seg_q_tgt = segments(lengths_ref, micro, 1, 1)
    seg_k_src = segments(lengths_ref, micro, 0, 0)
    ref.across[rows, :] = (seg_k_src == seg_q_tgt).astype(F32)
    earlier = lax.broadcasted_iota(jnp.int32, (ROWS, ROWS), 0) <= lax.broadcasted_iota(
        jnp.int32, (ROWS, ROWS), 1
    )
    source_mask = (seg_k_src == segments(lengths_ref, micro, 0, 1)).astype(jnp.int32)
    target_mask = ((segments(lengths_ref, micro, 1, 0) == seg_q_tgt) & earlier).astype(jnp.int32)
    mask = jnp.where(first, source_mask, target_mask) != 0
    gets.tokens.wait()
    tokens = ref.tokens[rows, :]
    for part in range(3):
        cut = slice(part * D, (part + 1) * D)
        gets.w_qkv[part].wait()
        ref.proj[rows, cut] = mm(tokens, ref.w_qkv[:, cut]).astype(LOW)

    def write_probs(pair, value):
        ref.probs[micro, pair] = value

    def write_mix(pair, value):
        ref.mix[rows, pair * LANES : (pair + 1) * LANES] = value

    attend(
        columns(ref.proj, rows, 0),
        columns(ref.proj, rows, D),
        columns(ref.proj, rows, 2 * D),
        mask,
        write_probs,
        write_mix,
    )
    gets.w_out.wait()
    mid = tokens.astype(F32) + mm(ref.mix[rows, :], ref.w_out[...])

    @pl.when(first)
    def _():
        ref.narrow[rows, :] = mid.astype(LOW)
        gets.w_up.wait()
        gets.w_down.wait()
        total = mid
        for part in range(4):
            cut = slice(part * D, (part + 1) * D)
            hidden = mm(ref.narrow[rows, :], ref.w_up[:, cut])
            ref.wide[rows, cut] = hidden
            ref.act[rows, cut] = gelu(hidden).astype(LOW)
            total = total + mm(ref.act[rows, cut], ref.w_down[cut, :])
        ref.result[rows, :] = total.astype(LOW)
        gets.w_cross.wait()
        for part in range(2):
            cut = slice(part * D, (part + 1) * D)
            link[:, cut] = mm(ref.result[rows, :], ref.w_cross[:, cut]).astype(LOW)
        ref.left_a[rows, :] = ref.result[rows, :]

    @pl.when(jnp.logical_not(first))
    def _():
        ref.left_a[rows, :] = mid.astype(LOW)
        ref.mid[rows, :] = mid


def decoder_ahead(ref, gets):
    gets.w_cross.wait()
    ref.query[...] = mm(ref.left_a[...], ref.w_cross[:, :D]).astype(LOW)
    gets.cotangent.wait()
    gets.w_down.wait()
    for part in range(4):
        cut = slice(part * D, (part + 1) * D)
        ref.wide[:, cut] = mm_nt(ref.cotangent[...], ref.w_down[cut, :])
    gets.w_up.wait()


class Fetch:
    def __init__(self, source, target, sem):
        self.copy = pltpu.make_async_copy(source, target, sem)

    def start(self):
        self.copy.start()

    def wait(self):
        self.copy.wait()


class Arrived:
    def wait(self):
        pass


def first_stage(lengths, tokens, w_qkv, w_out, w_cross, w_up, w_down):
    given = (lengths, tokens, w_qkv, w_out, w_up, w_down, w_cross)
    makes = {**WEIGHTS, **HELD, **STATE, **dict(link=((ROWS, 2 * D), LOW), token=TOKEN)}

    def body(lengths_in, tokens_in, qkv_in, out_in, up_in, down_in, cross_in, *refs):
        place_ref, lengths_ref, sems = refs[len(makes) :]
        ref = SimpleNamespace(**dict(zip(makes, refs)))
        index = lax.axis_index(DP).astype(jnp.int32)
        section = lax.axis_index(SECTION).astype(jnp.int32)
        place_ref[0] = section
        for bit in range(PLACE - 1):
            place_ref[1 + bit] = (index >> bit) % 2
        first = section == 0
        gets = SimpleNamespace(
            lengths=Fetch(lengths_in, lengths_ref, sems.at[0]),
            tokens=Fetch(tokens_in.at[0], ref.tokens, sems.at[1]),
            w_qkv=[
                Fetch(
                    qkv_in.at[0, :, pl.ds(part * D, D)],
                    ref.w_qkv.at[:, pl.ds(part * D, D)],
                    sems.at[2 + part],
                )
                for part in range(3)
            ],
            w_out=Fetch(out_in.at[0], ref.w_out, sems.at[5]),
            w_up=Fetch(up_in.at[0], ref.w_up, sems.at[6]),
            w_down=Fetch(down_in.at[0], ref.w_down, sems.at[7]),
            w_cross=Fetch(cross_in.at[0], ref.w_cross, sems.at[8]),
        )
        for get in [gets.lengths, gets.tokens, *gets.w_qkv, gets.w_out]:
            get.start()

        @pl.when(first)
        def _():
            gets.w_up.start()
            gets.w_down.start()
            gets.w_cross.start()

        ref.token[...] = jnp.zeros(*TOKEN)
        forward_step(0, first, lengths_ref, ref, ref.link, gets)

    results = pl.pallas_call(
        body,
        out_shape=shaped(makes) + [pltpu.SMEM((PLACE,), jnp.int32)],
        in_specs=[in_hbm()] * len(given),
        out_specs=[in_vmem()] * len(makes) + [in_smem()],
        scratch_shapes=[pltpu.SMEM((MB, 2, SLOTS), jnp.int32), pltpu.SemaphoreType.DMA((9,))],
        compiler_params=pltpu.CompilerParams(vmem_limit_bytes=16 * MIB),
        cost_estimate=pl.CostEstimate(
            flops=2 * ROWS * D * 7168, bytes_accessed=10_000_000, transcendentals=0
        ),
        name="first_stage",
    )(*left(given))
    made = SimpleNamespace(**dict(zip(makes, results)))
    link, token = made.link, made.token
    del made.link, made.token
    return results[-1], token, link, made


def second_stage(place, state, lengths, cotangent, w_cross, w_up, w_down):
    given = (lengths, cotangent, w_cross, w_up, w_down)
    kept = {**WEIGHTS, **HELD, **STATE}
    keeps = [getattr(state, name) for name in kept]

    def body(place_ref, lengths_in, cotangent_in, cross_in, up_in, down_in, *refs):
        refs = refs[len(keeps) :]
        ref = SimpleNamespace(**dict(zip(kept, refs)))
        link, lengths_ref, sems = refs[len(keeps) :]
        first = place_ref[0] == 0
        here = Arrived()
        get_lengths = Fetch(lengths_in, lengths_ref, sems.at[0])
        get_cotangent = Fetch(cotangent_in.at[0], ref.cotangent, sems.at[1])
        late = SimpleNamespace(
            cotangent=get_cotangent,
            w_cross=Fetch(cross_in.at[0], ref.w_cross, sems.at[2]),
            w_down=Fetch(down_in.at[0], ref.w_down, sems.at[3]),
            w_up=Fetch(up_in.at[0], ref.w_up, sems.at[4]),
        )
        get_lengths.start()
        get_cotangent.start()

        @pl.when(jnp.logical_not(first))
        def _():
            late.w_cross.start()
            late.w_down.start()
            late.w_up.start()

        gets = SimpleNamespace(
            lengths=get_lengths,
            tokens=here,
            w_qkv=[here] * 3,
            w_out=here,
            w_up=here,
            w_down=here,
            w_cross=here,
        )
        forward_step(1, first, lengths_ref, ref, link, gets)

        @pl.when(first)
        def _():
            get_cotangent.wait()

        @pl.when(jnp.logical_not(first))
        def _():
            decoder_ahead(ref, late)

    results = pl.pallas_call(
        body,
        out_shape=same_shape(keeps) + [pltpu.VMEM((ROWS, 2 * D), LOW)],
        in_specs=[in_smem()] + [in_hbm()] * len(given) + [in_vmem()] * len(keeps),
        out_specs=[in_vmem()] * (len(keeps) + 1),
        scratch_shapes=[pltpu.SMEM((MB, 2, SLOTS), jnp.int32), pltpu.SemaphoreType.DMA((5,))],
        input_output_aliases={1 + len(given) + i: i for i in range(len(keeps))},
        compiler_params=pltpu.CompilerParams(vmem_limit_bytes=16 * MIB),
        cost_estimate=pl.CostEstimate(
            flops=2 * ROWS * D * 7168, bytes_accessed=10_000_000, transcendentals=0
        ),
        name="second_stage",
    )(in_place(place), *left(given), *held(keeps))
    vars(state).update(zip(kept, results))
    return results[-1]


def middle_step(micro, ref, probs_v, mixed_v):
    rows = slice(micro * ROWS, (micro + 1) * ROWS)
    whole = slice(0, ROWS)
    reads = (
        columns(ref.query, rows, 0),
        columns(ref.link, whole, 0),
        columns(ref.link, whole, D),
    )

    def write_probs(pair, value):
        probs_v[pair] = value

    def write_mix(pair, value):
        ref.left_b[rows, pair * LANES : (pair + 1) * LANES] = value

    attend(*reads, ref.across[rows, :] != 0.0, write_probs, write_mix)
    after = ref.mid[rows, :] + mm(ref.left_b[rows, :], ref.w_cross[:, D:])
    ref.across_mid[rows, :] = after
    ref.narrow[rows, :] = after.astype(LOW)
    grad = ref.cotangent[rows, :].astype(F32)
    for part in range(4):
        cut = slice(part * D, (part + 1) * D)
        hidden = mm(ref.narrow[rows, :], ref.w_up[:, cut])
        ref.hidden[rows, cut] = hidden
        grad_hidden = (gelu_slope(hidden) * ref.wide[rows, cut]).astype(LOW)
        ref.grad_hidden[rows, cut] = grad_hidden
        grad = grad + mm_nt(grad_hidden, ref.w_up[:, cut])
    ref.grad[rows, :] = grad
    ref.right[rows, D:] = grad.astype(LOW)
    mixed_v[...] = mm_nt(ref.right[rows, D:], ref.w_cross[:, D:]).astype(LOW)

    def write(pair, grad_q, grad_k, grad_v):
        cut = slice(pair * LANES, (pair + 1) * LANES)
        ref.right[rows, cut] = grad_q
        ref.link_grad[:, cut] = grad_k
        ref.link_grad[:, D + pair * LANES : D + (pair + 1) * LANES] = grad_v

    attend_back(*reads, lambda pair: probs_v[pair], columns(mixed_v, whole, 0), write)


def middle_stage(micro, place, token, state, link):
    reads = dict(
        query=state.query,
        across=state.across,
        mid=state.mid,
        cotangent=state.cotangent,
        w_cross=state.w_cross,
        w_up=state.w_up,
        link=link,
    )
    keeps = dict(narrow=state.narrow, wide=state.wide)
    makes = dict(link_grad=((ROWS, 2 * D), LOW))
    if micro == 0:
        makes.update(BACK)
    else:
        keeps.update((name, getattr(state, name)) for name in BACK)

    def kernel(place_ref, ref, *scratch):
        @pl.when(place_ref[0] != 0)
        def _():
            middle_step(micro, ref, *scratch)

        @pl.when(place_ref[0] == 0)
        def _():
            rows = slice(micro * ROWS, (micro + 1) * ROWS)
            for part in range(4):
                cut = slice(part * D, (part + 1) * D)
                ref.wide[rows, cut] = gelu_slope(ref.wide[rows, cut])

    token, made = call(
        kernel,
        "middle_stage",
        place,
        token,
        reads,
        keeps,
        makes,
        scratch=(pltpu.VMEM((PAIRS, 2 * ROWS, ROWS), F32), pltpu.VMEM((ROWS, D), LOW)),
        cost=(2 * ROWS * D * 10000, 8_000_000),
    )
    vars(state).update(made)
    return token


def gate_step(micro, first, ref):
    rows = slice(micro * ROWS, (micro + 1) * ROWS)

    @pl.when(first)
    def _():
        cotangent = ref.cotangent[rows, :].astype(F32)
        grad = cotangent + mm_nt(ref.link_grad[...], ref.w_cross[...])
        ref.grad[rows, :] = grad
        ref.gate[rows, :] = grad.astype(LOW)
        ref.right[rows, :] = ref.link_grad[...]
        ref.left_b[rows, :] = ref.left_a[rows, :]

    @pl.when(jnp.logical_not(first))
    def _():
        ref.gate[rows, :] = ref.cotangent[rows, :]
        for part in range(4):
            cut = slice(part * D, (part + 1) * D)
            ref.act[rows, cut] = gelu(ref.hidden[rows, cut]).astype(LOW)


def back_step(micro, first, ref):
    rows = slice(micro * ROWS, (micro + 1) * ROWS)

    @pl.when(first)
    def _():
        grad = ref.grad[rows, :]
        for part in range(4):
            cut = slice(part * D, (part + 1) * D)
            grad_act = mm_nt(ref.gate[rows, :], ref.w_down[cut, :])
            grad_hidden = (ref.wide[rows, cut] * grad_act).astype(LOW)
            ref.grad_hidden[rows, cut] = grad_hidden
            grad = grad + mm_nt(grad_hidden, ref.w_up[:, cut])
        ref.grad[rows, :] = grad
        ref.grad_low[rows, :] = grad.astype(LOW)

    @pl.when(jnp.logical_not(first))
    def _():
        grad = ref.grad[rows, :] + mm_nt(ref.right[rows, :D], ref.w_cross[:, :D])
        ref.grad[rows, :] = grad
        ref.grad_low[rows, :] = grad.astype(LOW)


def back_stage(micro, place, token, state, link_grad, parts, send=(), cost=5000):
    reads = dict(
        cotangent=state.cotangent,
        w_cross=state.w_cross,
        w_up=state.w_up,
        w_down=state.w_down,
        wide=state.wide,
        left_a=state.left_a,
        link_grad=link_grad,
        narrow=state.narrow,
        mix=state.mix,
    )
    keeps = {name: getattr(state, name) for name in BACK}
    keeps.update(act=state.act)
    makes = {}
    for at, chunk in enumerate(send):
        makes["send%d" % at] = ((chunk.rows, D), LOW)

    def kernel(place_ref, ref):
        for part in parts:
            part(micro, place_ref[0] == 0, ref)
        for at, chunk in enumerate(send):
            put_send(place_ref, ref, chunk, getattr(ref, "send%d" % at))

    token, made = call(kernel, "back_stage", place, token, reads, keeps, makes, cost=mflop(cost))
    sends = [made.pop(name) for name in makes]
    vars(state).update(made)
    return token, sends


def late_kernel(place_ref, ref, mixed_v):
    mixed_v[...] = mm_nt(ref.grad_low[...], ref.w_out[...]).astype(LOW)
    for micro in range(MB):
        rows = slice(micro * ROWS, (micro + 1) * ROWS)

        def write(pair, grad_q, grad_k, grad_v, rows=rows):
            for part, value in enumerate((grad_q, grad_k, grad_v)):
                at = part * D + pair * LANES
                ref.grad_proj[rows, at : at + LANES] = value

        attend_back(
            columns(ref.proj, rows, 0),
            columns(ref.proj, rows, D),
            columns(ref.proj, rows, 2 * D),
            lambda pair, micro=micro: ref.probs[micro, pair],
            columns(mixed_v, rows, 0),
            write,
        )
    put_send(place_ref, ref, QKV, ref.send)


def late_stage(place, token, state, cost):
    reads = dict(
        grad_low=state.grad_low,
        w_out=state.w_out,
        proj=state.proj,
        probs=state.probs,
        tokens=state.tokens,
        mix=state.mix,
    )
    makes = dict(grad_proj=((BOTH, 3 * D), LOW), send=((QKV.rows, D), LOW))
    scratch = (pltpu.VMEM((BOTH, D), LOW),)
    token, made = call(
        late_kernel, "late_stage", place, token, reads, {}, makes, None, scratch, mflop(cost)
    )
    state.grad_proj = made["grad_proj"]
    return token, made["send"]


def final_kernel(place_ref, ref, result_v, grad_v, sems):
    @pl.when(place_ref[0] == 0)
    def _():
        result_v[...] = ref.result[...]

    @pl.when(place_ref[0] != 0)
    def _():
        total = ref.across_mid[...]
        for part in range(4):
            cut = slice(part * D, (part + 1) * D)
            total = total + mm(ref.act[:, cut], ref.w_down[cut, :])
        result_v[...] = total.astype(LOW)

    first = fetch(result_v, ref.outputs.at[0], sems.at[0])
    grad_v[...] = (ref.grad[...] + mm_nt(ref.grad_proj[...], ref.w_qkv[...])).astype(LOW)
    second = fetch(grad_v, ref.input_grad.at[0], sems.at[1])
    first.wait()
    second.wait()


def final_stage(place, token, state, cost):
    reads = dict(
        grad=state.grad,
        grad_proj=state.grad_proj,
        w_qkv=state.w_qkv,
        result=state.result,
        across_mid=state.across_mid,
        act=state.act,
        w_down=state.w_down,
    )
    half = ((1, BOTH, D), LOW)
    stores = dict(outputs=half, input_grad=half)
    scratch = [pltpu.VMEM((BOTH, D), LOW)] * 2 + [pltpu.SemaphoreType.DMA((2,))]
    return call(
        final_kernel, "final_stage", place, token, reads, {}, {}, stores, scratch, mflop(cost)
    )


PIECE = HALF // 2
PIECES = 7

Y_FIRST = (1, 2, 3)
Z_FIRST = (2, 1, 3)


def cut_of(part):
    return slice(part * D, (part + 1) * D)


class Gradient:
    def __init__(self, sides, store, down=False):
        self.sides = sides
        self.store = store
        self.down = down

    def rows(self, part, half, first, count):
        start = (part * D if self.down else 0) + first * PIECE
        return pl.ds(pl.multiple_of(start + half * HALF, PIECE), count * PIECE)

    def product(self, ref, part, half, first, count):
        left_ref, right_ref, column = self.sides(ref, part)
        return mm_tn(left_ref[:, self.rows(part, half, first, count)], right_ref[:, cut_of(column)])

    def target(self, array, part, half, first, count):
        column = 0 if self.down else part * D
        return array.at[0, self.rows(part, half, first, count), pl.ds(column, D)]


G_DOWN = Gradient(lambda ref, part: (ref.act, ref.gate, 0), dict(g_down=((1, FF, D), F32)), down=True)
G_UP = Gradient(lambda ref, part: (ref.narrow, ref.grad_hidden, part), dict(g_up=((1, D, FF), F32)))
G_CROSS = Gradient(
    lambda ref, part: ((ref.left_a, ref.left_b)[part], ref.right, part),
    dict(g_cross=((1, D, 2 * D), F32)),
)
G_OUT = Gradient(lambda ref, part: (ref.mix, ref.grad_low, 0), dict(g_out=((1, D, D), F32)))
G_QKV = Gradient(
    lambda ref, part: (ref.tokens, ref.grad_proj, part), dict(g_qkv=((1, D, 3 * D), F32))
)


class Chunk:
    def __init__(self, levels, operands, runs):
        self.levels = levels
        self.operands = operands
        self.runs = runs
        self.rows = PIECES * PIECE
        self.stores = {}
        for run in runs:
            self.stores.update(run[0].store)

    def each(self):
        at = 0
        for gradient, part, first, count in self.runs:
            yield slice(at, at + count * PIECE), gradient, (part, first, count)
            at += count * PIECE


def product_of(gradient, ref, run, half):
    part, first, count = run
    return gradient.product(ref, part, half, first, count)


CROSS = Chunk(
    (Y_FIRST, Z_FIRST),
    lambda state: dict(
        left_a=state.left_a,
        left_b=state.left_b,
        right=state.right,
        mix=state.mix,
        grad_low=state.grad_low,
        act=state.act,
        gate=state.gate,
        narrow=state.narrow,
        grad_hidden=state.grad_hidden,
    ),
    [(G_CROSS, 0, 0, 2), (G_CROSS, 1, 0, 2), (G_OUT, 0, 0, 1), (G_DOWN, 3, 1, 1), (G_UP, 3, 1, 1)],
)
DOWN = Chunk(
    (Y_FIRST, Z_FIRST),
    lambda state: dict(act=state.act, gate=state.gate),
    [(G_DOWN, 0, 0, 2), (G_DOWN, 1, 0, 2), (G_DOWN, 2, 0, 2), (G_DOWN, 3, 0, 1)],
)
UP = Chunk(
    (Z_FIRST, Y_FIRST),
    lambda state: dict(narrow=state.narrow, grad_hidden=state.grad_hidden),
    [(G_UP, 0, 0, 2), (G_UP, 1, 0, 2), (G_UP, 2, 0, 2), (G_UP, 3, 0, 1)],
)
QKV = Chunk(
    (Z_FIRST, Y_FIRST),
    lambda state: dict(
        tokens=state.tokens, grad_proj=state.grad_proj, mix=state.mix, grad_low=state.grad_low
    ),
    [(G_QKV, 0, 0, 2), (G_QKV, 1, 0, 2), (G_QKV, 2, 0, 2), (G_OUT, 0, 1, 1)],
)


def put_send(place_ref, ref, chunk, send):
    for here, gradient, run in chunk.each():
        send[here, :] = product_of(gradient, ref, run, 1 - place_ref[1]).astype(LOW)


class Summing:
    def __init__(self, chunk, state, place, count):
        self.chunk = chunk
        self.state = state
        self.place = place
        self.count = count
        self.depth = count.bit_length() - 2
        self.step = 0

    def swap(self, value, level):
        def partner(i):
            bit = self.chunk.levels[i % 2][level - 1] if 0 < level < 4 else level
            return i ^ (1 << bit)

        return lax.ppermute(value, "dp", [(i, partner(i)) for i in range(self.count)])

    def call(self, kernel, token, reads, makes, stores=None, scratch=(), patches=None):
        name = "sum_%d" % self.step
        rest = (stores, scratch, mflop(self.cost), patches)
        return call(kernel, name, self.place, token, reads, {}, makes, *rest)

    def halves(self, place_ref, level, rows):
        first, second = (place_ref[1 + levels[level - 1]] for levels in self.chunk.levels)
        bit = jnp.where(place_ref[1] == 0, first, second)
        half = rows // 2
        own = pl.ds(pl.multiple_of(bit * half, half), half)
        return own, pl.ds(pl.multiple_of((1 - bit) * half, half), half)

    def launch(self, send):
        self.got = self.swap(send, 0)

    def start(self, token, cost):
        def kernel(place_ref, ref):
            put_send(place_ref, ref, self.chunk, ref.send)

        makes = dict(send=((self.chunk.rows, D), LOW))
        reads = self.chunk.operands(self.state)
        token, made = call(kernel, "product", self.place, token, reads, {}, makes, cost=mflop(cost))
        self.launch(made["send"])
        return token

    def advance(self, token, grads, cost):
        self.cost = cost
        rows = self.chunk.rows
        if self.step == 0:
            token = self.split_first(token, rows)
        elif self.step == 1:
            token = self.split(token, rows // 2)
        elif self.step == 2:
            token = self.round_off(token, rows // 4)
        elif self.step == 3:
            for level in range(4, self.depth + 1):
                token = self.pair_sum(token, rows // 4, level)
            token = self.pair_sum(token, rows // 4, 2)
        elif self.step == 4:
            token = self.merge(token, rows // 4, 1)
        elif self.step == 5:
            token = self.merge(token, rows // 2, 0)
        else:
            token = self.unpack(token, grads, False, cost)
        self.step += 1
        return token

    def split_first(self, token, rows):
        chunk = self.chunk

        def kernel(place_ref, ref, total):
            for here, gradient, run in chunk.each():
                own = product_of(gradient, ref, run, place_ref[1])
                total[here, :] = own + ref.got[here, :].astype(F32)
            own, other = self.halves(place_ref, 1, rows)
            ref.send[...] = total[other, :].astype(LOW)
            ref.keep[...] = total[own, :]

        reads = dict(got=self.got, **chunk.operands(self.state))
        makes = dict(send=((rows // 2, D), LOW), keep=((rows // 2, D), F32))
        scratch = (pltpu.VMEM((rows, D), F32),)
        token, made = self.call(kernel, token, reads, makes, scratch=scratch)
        self.keep = made["keep"]
        self.got = self.swap(made["send"], 1)
        return token

    def split(self, token, rows):
        def kernel(place_ref, ref):
            own, other = self.halves(place_ref, 2, rows)
            ref.send[...] = (ref.keep[other, :] + ref.got[other, :].astype(F32)).astype(LOW)
            ref.kept[...] = ref.keep[own, :] + ref.got[own, :].astype(F32)

        reads = dict(keep=self.keep, got=self.got)
        makes = dict(send=((rows // 2, D), LOW), kept=((rows // 2, D), F32))
        token, made = self.call(kernel, token, reads, makes)
        self.keep = made["kept"]
        self.got = self.swap(made["send"], 2)
        return token

    def round_off(self, token, rows):
        def kernel(place_ref, ref):
            ref.piece[...] = (ref.keep[...] + ref.got[...].astype(F32)).astype(LOW)

        makes = dict(piece=((rows, D), LOW))
        token, made = self.call(kernel, token, dict(keep=self.keep, got=self.got), makes)
        self.piece = made["piece"]
        self.got = self.swap(self.piece, 3)
        return token

    def pair_sum(self, token, rows, level):
        def kernel(place_ref, ref):
            both = ref.held[...].astype(F32) + ref.got[...].astype(F32)
            ref.piece[...] = both.astype(LOW)

        makes = dict(piece=((rows, D), LOW))
        token, made = self.call(kernel, token, dict(held=self.piece, got=self.got), makes)
        self.piece = made["piece"]
        self.got = self.swap(self.piece, level)
        return token

    def merge(self, token, rows, level):
        def kernel(place_ref, ref):
            own, other = self.halves(place_ref, level + 1, 2 * rows)
            ref.piece[own, :] = ref.held[...]
            ref.piece[other, :] = ref.got[...]

        makes = dict(piece=((2 * rows, D), LOW))
        token, made = self.call(kernel, token, dict(held=self.piece, got=self.got), makes)
        self.piece = made["piece"]
        self.got = self.swap(self.piece, level)
        return token

    def unpack(self, token, grads, own, cost):
        chunk = self.chunk
        patches = {name: grads[name] for name in chunk.stores if name in grads}
        stores = {name: kind for name, kind in chunk.stores.items() if name not in grads}

        def kernel(place_ref, ref, wide, sems):
            half = place_ref[1] if own else 1 - place_ref[1]
            copies = []
            for index, (here, gradient, (part, first, count)) in enumerate(chunk.each()):
                wide[here, :] = ref.source[here, :].astype(F32)
                array = getattr(ref, list(gradient.store)[0])
                target = gradient.target(array, part, half, first, count)
                rows = pl.ds(here.start, here.stop - here.start)
                copies.append(fetch(wide.at[rows], target, sems.at[index]))
            for copy in copies:
                copy.wait()

        scratch = (pltpu.VMEM((chunk.rows, D), F32), pltpu.SemaphoreType.DMA((len(chunk.runs),)))
        reads = dict(source=self.piece if own else self.got)
        name = "unpack_%d" % own
        token, made = call(
            kernel, name, self.place, token, reads, {}, {}, stores, scratch, mflop(cost), patches
        )
        grads.update(made)
        return token


CHUNKS = (DOWN, CROSS, UP, QKV)
GATE, BACK_ATTN, BACK_FFN, FINAL, MORE, OWN = 10, 11, 12, 13, 14, 20
ORDER = (GATE, BACK_FFN, 0, MORE, 1, BACK_ATTN) + (0, 2, 1, 3) * 2 + (0, FINAL, 2, 1, 3) + (0, 2, 1, 3)
ORDER += (0, 2, OWN, 1, 3, OWN + 1, 0, 2, 1, OWN + 2, 3, 2, OWN + 3, 3)
COSTS = (1000, 1000, 8000, 4000, 8000, 8000, 8000, 4000, 1000, 1000, 1000, 1000, 1000, 1000, 1000, 1000, 1000, 1000, 1000, 1000, 1000, 1000, 1000, 1000, 8000, 8000, 1000, 1000, 8000, 1000, 1000, 1000, 1000, 50, 3000, 1000, 1000)


def on_device(inputs, lengths, w_qkv, w_attn_out, w_cross, w_up, w_down, cotangent):
    count = lax.axis_size("dp")
    place, token, link, state = first_stage(
        lengths, inputs, w_qkv, w_attn_out, w_cross, w_up, w_down
    )
    links = [lax.ppermute(link, "section", [(0, 1)])]
    link = second_stage(place, state, lengths, cotangent, w_cross, w_up, w_down)
    links.append(lax.ppermute(link, "section", [(0, 1)]))
    grads = []
    for micro in range(MB):
        token = middle_stage(micro, place, token, state, links[micro])
        grads.append(lax.ppermute(state.link_grad, "section", [(1, 0)]))
    token, _ = back_stage(0, place, token, state, grads[0], (gate_step, back_step))
    chunks = [Summing(chunk, state, place, count) for chunk in CHUNKS]
    made = {}
    for task, cost in zip(ORDER, COSTS):
        if task == GATE:
            token, sends = back_stage(1, place, token, state, grads[1], (gate_step,), [DOWN], cost)
            chunks[0].launch(*sends)
        elif task == BACK_FFN:
            token, sends = back_stage(1, place, token, state, grads[1], (back_step,), [CROSS], cost)
            chunks[1].launch(*sends)
        elif task == MORE:
            token = chunks[2].start(token, cost)
        elif task == BACK_ATTN:
            token, send = late_stage(place, token, state, cost)
            chunks[3].launch(send)
        elif task == FINAL:
            token, ends = final_stage(place, token, state, cost)
            made.update(ends)
        elif task >= OWN:
            token = chunks[task - OWN].unpack(token, made, True, cost)
        else:
            token = chunks[task].advance(token, made, cost)
    done = SimpleNamespace(**made)
    return (
        done.outputs,
        done.input_grad,
        done.g_qkv,
        done.g_out,
        done.g_cross,
        done.g_up,
        done.g_down,
    )


def solution(mesh):
    return jax.shard_map(
        on_device,
        mesh=mesh,
        in_specs=(
            P("section", "dp", None),
            P("dp", None, None),
            P("section", None, None),
            P("section", None, None),
            P("section", None, None),
            P("section", None, None),
            P("section", None, None),
            P("section", "dp", None),
        ),
        out_specs=(
            P("section", "dp", None),
            P("section", "dp", None),
            P("section", None, None),
            P("section", None, None),
            P("section", None, None),
            P("section", None, None),
            P("section", None, None),
        ),
        check_vma=False,
    )
```

```python
from types import SimpleNamespace

import jax
import jax.numpy as jnp
from jax import lax
from jax.experimental import pallas as pl
from jax.experimental.pallas import tpu as pltpu
from jax.sharding import PartitionSpec as P

D = 512
HEADS = 8
HEAD_DIM = 64
FF = 2048
ROWS = 128
SLOTS = 16
MB = 2
BOTH = MB * ROWS
PAIRS = HEADS // 2
LANES = 2 * HEAD_DIM
HALF = D // 2
SCALE = HEAD_DIM ** (-0.5)
GELU_IN = 0.7978845608028654
GELU_CUBE = 0.044715
LOW = jnp.bfloat16
F32 = jnp.float32
MIB = 1024 * 1024
DP = "dp"
SECTION = "section"
PLACE = 4


def in_two(value):
    rounded = value.astype(LOW)
    return rounded, (value - rounded.astype(F32)).astype(LOW)


def mm(left, right):
    return jnp.dot(left, right, preferred_element_type=F32)


def mm_nt(left, right):
    return lax.dot_general(left, right, (((1,), (1,)), ((), ())), preferred_element_type=F32)


def mm_tn(left, right):
    return lax.dot_general(left, right, (((0,), (0,)), ((), ())), preferred_element_type=F32)


def gelu(hidden):
    inner = GELU_IN * (hidden + GELU_CUBE * (hidden * hidden * hidden))
    return hidden * (0.5 * (1.0 + jnp.tanh(inner)))


def gelu_slope(hidden):
    square = hidden * hidden
    inner = GELU_IN * (hidden + GELU_CUBE * (square * hidden))
    bent = jnp.tanh(inner)
    inner_slope = GELU_IN * (1.0 + (3.0 * GELU_CUBE) * square)
    return 0.5 * (1.0 + bent) + 0.5 * hidden * (1.0 - bent * bent) * inner_slope


def segments(lengths_ref, micro, which, dim):
    position = lax.broadcasted_iota(jnp.int32, (ROWS, ROWS), dim)
    end = jnp.int32(0)
    seg = jnp.zeros((ROWS, ROWS), jnp.int32)
    for slot in range(SLOTS):
        end = end + lengths_ref[micro, which, slot]
        seg = seg + (position >= end).astype(jnp.int32)
    return seg


def low_lanes():
    return lax.broadcasted_iota(jnp.int32, (ROWS, LANES), 1) < HEAD_DIM


def two_heads(pair, lanes):
    nothing = jnp.zeros_like(pair)
    return jnp.concatenate(
        [jnp.where(lanes, pair, nothing), jnp.where(lanes, nothing, pair)], axis=0
    )


def softmax(scores):
    highest = jnp.max(scores, axis=0, keepdims=True)
    raised = jnp.exp(scores - highest)
    return raised * (1.0 / jnp.sum(raised, axis=0, keepdims=True))


def two_halves(value):
    return value[:ROWS, :], value[ROWS:, :]


def attend(read_q, read_k, read_v, mask, write_probs, write_mix):
    lanes = low_lanes()
    for pair in range(PAIRS):
        query = (read_q(pair).astype(F32) * SCALE).astype(LOW)
        scores = mm_nt(two_heads(read_k(pair), lanes), query)
        heads = [softmax(jnp.where(mask, part, -1e30)) for part in two_halves(scores)]
        probs = jnp.concatenate(heads, axis=0)
        write_probs(pair, probs)
        write_mix(pair, mm_tn(probs.astype(LOW), two_heads(read_v(pair), lanes)).astype(LOW))


def attend_back_values(read_probs, read_grad, write):
    lanes = low_lanes()
    for pair in range(PAIRS):
        grad_v = mm(read_probs(pair).astype(LOW), read_grad(pair))
        write(pair, jnp.where(lanes, *two_halves(grad_v)))


def attend_back_keys(read_q, read_k, read_v, read_probs, read_grad, write):
    lanes = low_lanes()
    for pair in range(PAIRS):
        query = (read_q(pair).astype(F32) * SCALE).astype(LOW)
        probs = read_probs(pair)
        grad_probs = mm_nt(two_heads(read_v(pair), lanes), read_grad(pair))
        slopes = []
        for head, change in zip(two_halves(probs), two_halves(grad_probs)):
            total = jnp.sum(head * change, axis=0, keepdims=True)
            slopes.append((head * (change - total)).astype(LOW))
        slopes = jnp.concatenate(slopes, axis=0)
        grad_q = mm_tn(slopes, two_heads(read_k(pair), lanes)) * SCALE
        grad_k = jnp.where(lanes, *two_halves(mm(slopes, query)))
        write(pair, grad_q, grad_k)


def columns(ref, rows, start):
    def read(pair):
        return ref[rows, start + pair * LANES : start + (pair + 1) * LANES]

    return read


def fetch(source, target, sem):
    copy = pltpu.make_async_copy(source, target, sem)
    copy.start()
    return copy


WEIGHTS = dict(
    w_qkv=((D, 3 * D), LOW),
    w_out=((D, D), LOW),
    w_cross=((D, 2 * D), LOW),
    w_up=((D, FF), LOW),
    w_down=((FF, D), LOW),
)
HELD = dict(tokens=((BOTH, D), LOW), cotangent=((BOTH, D), LOW))
STATE = dict(
    proj=((BOTH, 3 * D), LOW),
    mix=((BOTH, D), LOW),
    probs=((MB, PAIRS, 2 * ROWS, ROWS), F32),
    wide=((BOTH, FF), F32),
    mid=((BOTH, D), F32),
    act=((BOTH, FF), LOW),
    narrow=((BOTH, D), LOW),
    result=((BOTH, D), LOW),
    left_a=((BOTH, D), LOW),
    query=((BOTH, D), LOW),
    across=((BOTH, ROWS), F32),
)
BACK = dict(
    hidden=((BOTH, FF), F32),
    across_mid=((BOTH, D), F32),
    left_b=((BOTH, D), LOW),
    right=((BOTH, 2 * D), LOW),
    grad_hidden=((BOTH, FF), LOW),
    gate=((BOTH, D), LOW),
    grad=((BOTH, D), F32),
    grad_low=((BOTH, D), LOW),
)


def shaped(table):
    return [pltpu.VMEM(shape, kind) for shape, kind in table.values()]


def same_shape(arrays):
    return [pltpu.VMEM(value.shape, value.dtype) for value in arrays]


def held(arrays):
    return [pltpu.with_memory_space_constraint(value, pltpu.VMEM) for value in arrays]


def in_place(place):
    return pltpu.with_memory_space_constraint(place, pltpu.SMEM)


def left(arrays):
    return [pltpu.with_memory_space_constraint(value, pltpu.HBM) for value in arrays]


def in_vmem():
    return pl.BlockSpec(memory_space=pltpu.VMEM)


def in_smem():
    return pl.BlockSpec(memory_space=pltpu.SMEM)


def in_hbm():
    return pl.BlockSpec(memory_space=pltpu.HBM)


TOKEN = ((8, LANES), F32)


def mflop(count):
    return count * 1_000_000, 0


def call(
    kernel, name, place, token, reads, keeps, makes, stores=None, scratch=(), cost=(0, 0), patches=None
):
    stores, patches = stores or {}, patches or {}
    out_shape = same_shape(keeps.values()) + shaped(makes) + shaped(dict(token=TOKEN))
    out_shape += [pltpu.HBM(shape, kind) for shape, kind in stores.values()]
    out_shape += [pltpu.HBM(value.shape, value.dtype) for value in patches.values()]
    reads_n, keeps_n, makes_n = len(reads), len(keeps), len(makes)
    stores_n, patches_n = len(stores), len(patches)
    aliases = {2 + reads_n + i: i for i in range(keeps_n)}
    for i in range(patches_n):
        aliases[2 + reads_n + keeps_n + i] = keeps_n + makes_n + 1 + stores_n + i

    def body(place_ref, token_in, *refs):
        del token_in
        refs = list(refs)
        named = dict(zip(reads, refs[:reads_n]))
        refs = refs[reads_n + keeps_n + patches_n :]
        named.update(zip(keeps, refs[:keeps_n]))
        named.update(zip(makes, refs[keeps_n : keeps_n + makes_n]))
        refs = refs[keeps_n + makes_n :]
        refs[0][...] = jnp.zeros(*TOKEN)
        named.update(zip(stores, refs[1 : 1 + stores_n]))
        refs = refs[1 + stores_n :]
        named.update(zip(patches, refs[:patches_n]))
        kernel(place_ref, SimpleNamespace(**named), *refs[patches_n:])

    results = pl.pallas_call(
        body,
        out_shape=out_shape,
        in_specs=[in_smem()] + [in_vmem()] * (1 + reads_n + keeps_n) + [in_hbm()] * patches_n,
        out_specs=[in_vmem()] * (keeps_n + makes_n + 1) + [in_hbm()] * (stores_n + patches_n),
        scratch_shapes=list(scratch),
        input_output_aliases=aliases,
        compiler_params=pltpu.CompilerParams(vmem_limit_bytes=16 * MIB),
        cost_estimate=pl.CostEstimate(flops=cost[0], bytes_accessed=cost[1], transcendentals=0),
        name=name,
    )(
        in_place(place),
        *held([token]),
        *held(reads.values()),
        *held(keeps.values()),
        *left(patches.values()),
    )
    names = list(keeps) + list(makes)
    token = results[len(names)]
    made = dict(zip(names, results))
    made.update(zip(list(stores) + list(patches), results[len(names) + 1 :]))
    return token, made


def forward_step(micro, encoder, lengths_ref, ref, link, gets):
    rows = slice(micro * ROWS, (micro + 1) * ROWS)
    gets.tokens.wait()
    tokens = ref.tokens[rows, :]
    gets.w_qkv[0].wait()
    gets.lengths.wait()
    if encoder:
        mask = segments(lengths_ref, micro, 0, 0) == segments(lengths_ref, micro, 0, 1)
    else:
        seg_tgt = segments(lengths_ref, micro, 1, 1)
        source = segments(lengths_ref, micro, 0, 0)
        ref.across[rows, :] = (source == seg_tgt).astype(F32)
        earlier = lax.broadcasted_iota(jnp.int32, (ROWS, ROWS), 0) <= lax.broadcasted_iota(
            jnp.int32, (ROWS, ROWS), 1
        )
        mask = (segments(lengths_ref, micro, 1, 0) == seg_tgt) & earlier
    for part in range(3):
        cut = slice(part * D, (part + 1) * D)
        if part:
            gets.w_qkv[part].wait()
        ref.proj[rows, cut] = mm(tokens, ref.w_qkv[:, cut]).astype(LOW)

    def write_probs(pair, value):
        ref.probs[micro, pair] = value

    def write_mix(pair, value):
        ref.mix[rows, pair * LANES : (pair + 1) * LANES] = value

    attend(
        columns(ref.proj, rows, 0),
        columns(ref.proj, rows, D),
        columns(ref.proj, rows, 2 * D),
        mask,
        write_probs,
        write_mix,
    )
    gets.w_out.wait()
    mid = tokens.astype(F32) + mm(ref.mix[rows, :], ref.w_out[...])

    if not encoder:
        ref.left_a[rows, :] = mid.astype(LOW)
        ref.mid[rows, :] = mid
        return
    ref.narrow[rows, :] = mid.astype(LOW)
    gets.w_up.wait()
    gets.w_down.wait()
    for part in range(4):
        cut = slice(part * D, (part + 1) * D)
        hidden = mm(ref.narrow[rows, :], ref.w_up[:, cut])
        ref.wide[rows, cut] = hidden
        ref.act[rows, cut] = gelu(hidden).astype(LOW)
    total = mid + mm(ref.act[rows, :], ref.w_down[...])
    ref.result[rows, :] = total.astype(LOW)
    gets.w_cross.wait()
    link[...] = mm(ref.result[rows, :], ref.w_cross[...]).astype(LOW)
    ref.left_a[rows, :] = ref.result[rows, :]


def decoder_ahead(ref, gets):
    gets.w_cross.wait()
    ref.query[...] = mm(ref.left_a[...], ref.w_cross[:, :D]).astype(LOW)
    gets.cotangent.wait()
    gets.w_down.wait()
    for part in range(4):
        cut = slice(part * D, (part + 1) * D)
        ref.wide[:, cut] = mm_nt(ref.cotangent[...], ref.w_down[cut, :])
    gets.w_up.wait()


class Fetch:
    def __init__(self, source, target, sem):
        self.copy = pltpu.make_async_copy(source, target, sem)

    def start(self):
        self.copy.start()

    def wait(self):
        self.copy.wait()


class Arrived:
    def wait(self):
        pass


def fetches(ref, sems, lengths_ref, sources):
    lengths_in, tokens_in, qkv_in, out_in, up_in, down_in, cross_in, cotangent_in = sources
    parts = [pl.ds(part * D, D) for part in range(3)]
    return SimpleNamespace(
        lengths=Fetch(lengths_in, lengths_ref, sems.at[0]),
        tokens=Fetch(tokens_in.at[0], ref.tokens, sems.at[1]),
        w_qkv=[
            Fetch(qkv_in.at[0, :, part], ref.w_qkv.at[:, part], sems.at[2 + at])
            for at, part in enumerate(parts)
        ],
        w_out=Fetch(out_in.at[0], ref.w_out, sems.at[5]),
        w_up=Fetch(up_in.at[0], ref.w_up, sems.at[6]),
        w_down=Fetch(down_in.at[0], ref.w_down, sems.at[7]),
        w_cross=Fetch(cross_in.at[0], ref.w_cross, sems.at[8]),
        cotangent=Fetch(cotangent_in.at[0], ref.cotangent, sems.at[9]),
    )


def start_all(gets):
    order = [gets.lengths, gets.tokens, *gets.w_qkv, gets.w_out, gets.w_up, gets.w_down, gets.w_cross]
    for get in order:
        get.start()


FETCHED = 8
FETCH_SCRATCH = [pltpu.SMEM((MB, 2, SLOTS), jnp.int32), pltpu.SemaphoreType.DMA((FETCHED + 2,))]


def first_stage(given):
    makes = {**WEIGHTS, **HELD, **STATE, **dict(link=((ROWS, 2 * D), LOW), token=TOKEN)}

    def body(*refs):
        place_ref, lengths_ref, sems = refs[FETCHED + len(makes) :]
        ref = SimpleNamespace(**dict(zip(makes, refs[FETCHED:])))
        index = lax.axis_index(DP).astype(jnp.int32)
        section = lax.axis_index(SECTION).astype(jnp.int32)
        place_ref[0] = section
        for bit in range(PLACE - 1):
            place_ref[1 + bit] = (index >> bit) % 2
        ref.token[...] = jnp.zeros(*TOKEN)

        @pl.when(section == 0)
        def _():
            gets = fetches(ref, sems, lengths_ref, refs[:FETCHED])
            start_all(gets)
            forward_step(0, True, lengths_ref, ref, ref.link, gets)

    results = pl.pallas_call(
        body,
        out_shape=shaped(makes) + [pltpu.SMEM((PLACE,), jnp.int32)],
        in_specs=[in_hbm()] * FETCHED,
        out_specs=[in_vmem()] * len(makes) + [in_smem()],
        scratch_shapes=FETCH_SCRATCH,
        compiler_params=pltpu.CompilerParams(vmem_limit_bytes=16 * MIB),
        cost_estimate=pl.CostEstimate(
            flops=2 * ROWS * D * 7168, bytes_accessed=10_000_000, transcendentals=0
        ),
        name="first_stage",
    )(*left(given))
    made = SimpleNamespace(**dict(zip(makes, results)))
    link, token = made.link, made.token
    del made.link, made.token
    return results[-1], token, link, made


def second_stage(place, state, given):
    kept = {**WEIGHTS, **HELD, **STATE}
    keeps = [getattr(state, name) for name in kept]

    def body(place_ref, *refs):
        sources = refs[:FETCHED]
        refs = refs[FETCHED + len(keeps) :]
        ref = SimpleNamespace(**dict(zip(kept, refs)))
        link, lengths_ref, sems = refs[len(keeps) :]
        gets = fetches(ref, sems, lengths_ref, sources)
        here = Arrived()

        @pl.when(place_ref[0] == 0)
        def _():
            gets.lengths.start()
            gets.cotangent.start()
            arrived = SimpleNamespace(
                lengths=gets.lengths,
                tokens=here,
                w_qkv=[here] * 3,
                w_out=here,
                w_up=here,
                w_down=here,
                w_cross=here,
            )
            forward_step(1, True, lengths_ref, ref, link, arrived)
            gets.cotangent.wait()

        @pl.when(place_ref[0] != 0)
        def _():
            start_all(gets)
            gets.cotangent.start()
            forward_step(0, False, lengths_ref, ref, link, gets)
            arrived = SimpleNamespace(lengths=here, tokens=here, w_qkv=[here] * 3, w_out=here)
            forward_step(1, False, lengths_ref, ref, link, arrived)
            decoder_ahead(ref, gets)

    results = pl.pallas_call(
        body,
        out_shape=same_shape(keeps) + [pltpu.VMEM((ROWS, 2 * D), LOW)],
        in_specs=[in_smem()] + [in_hbm()] * FETCHED + [in_vmem()] * len(keeps),
        out_specs=[in_vmem()] * (len(keeps) + 1),
        scratch_shapes=FETCH_SCRATCH,
        input_output_aliases={1 + FETCHED + i: i for i in range(len(keeps))},
        compiler_params=pltpu.CompilerParams(vmem_limit_bytes=16 * MIB),
        cost_estimate=pl.CostEstimate(
            flops=2 * ROWS * D * 7168, bytes_accessed=10_000_000, transcendentals=0
        ),
        name="second_stage",
    )(in_place(place), *left(given), *held(keeps))
    vars(state).update(zip(kept, results))
    return results[-1]


def middle_step(micro, ref):
    rows = slice(micro * ROWS, (micro + 1) * ROWS)
    whole = slice(0, ROWS)

    def write_probs(pair, value):
        ref.link_probs[pair] = value

    def write_mix(pair, value):
        ref.left_b[rows, pair * LANES : (pair + 1) * LANES] = value

    attend(
        columns(ref.query, rows, 0),
        columns(ref.link, whole, 0),
        columns(ref.link, whole, D),
        ref.across[rows, :] != 0.0,
        write_probs,
        write_mix,
    )
    after = ref.mid[rows, :] + mm(ref.left_b[rows, :], ref.w_cross[:, D:])
    ref.across_mid[rows, :] = after
    ref.narrow[rows, :] = after.astype(LOW)
    grad = ref.cotangent[rows, :].astype(F32)
    for part in range(4):
        cut = slice(part * D, (part + 1) * D)
        hidden = mm(ref.narrow[rows, :], ref.w_up[:, cut])
        ref.hidden[rows, cut] = hidden
        grad_hidden = (gelu_slope(hidden) * ref.wide[rows, cut]).astype(LOW)
        ref.grad_hidden[rows, cut] = grad_hidden
        grad = grad + mm_nt(grad_hidden, ref.w_up[:, cut])
    ref.grad[rows, :] = grad
    ref.right[rows, D:] = grad.astype(LOW)
    ref.mixed[...] = mm_nt(ref.right[rows, D:], ref.w_cross[:, D:]).astype(LOW)

    def write(pair, grad_v):
        ref.values_grad[:, pair * LANES : (pair + 1) * LANES] = grad_v.astype(LOW)

    attend_back_values(lambda pair: ref.link_probs[pair], columns(ref.mixed, whole, 0), write)


def middle_keys(micro, ref):
    rows = slice(micro * ROWS, (micro + 1) * ROWS)
    whole = slice(0, ROWS)

    def write(pair, grad_q, grad_k):
        cut = slice(pair * LANES, (pair + 1) * LANES)
        ref.right[rows, cut] = grad_q.astype(LOW)
        ref.keys_grad[:, cut] = grad_k.astype(LOW)

    attend_back_keys(
        columns(ref.query, rows, 0),
        columns(ref.link, whole, 0),
        columns(ref.link, whole, D),
        lambda pair: ref.link_probs[pair],
        columns(ref.mixed, whole, 0),
        write,
    )


def two_sides(link_grad):
    return link_grad.at[pl.ds(0, ROWS)], link_grad.at[pl.ds(ROWS, ROWS)]


LINK_STATE = dict(link_probs=((PAIRS, 2 * ROWS, ROWS), F32), mixed=((ROWS, D), LOW))
SIDE = ((ROWS, D), LOW)


def middle_stage(micro, place, token, state, link):
    reads = dict(
        query=state.query,
        across=state.across,
        mid=state.mid,
        cotangent=state.cotangent,
        w_cross=state.w_cross,
        w_up=state.w_up,
        link=link,
    )
    keeps = dict(narrow=state.narrow, wide=state.wide)
    makes, scratch = {}, ()
    if micro == 0:
        makes.update(link_grad=((2 * ROWS, D), LOW), **BACK)
        scratch = shaped(LINK_STATE)
    else:
        makes.update(values_grad=SIDE, **LINK_STATE)
        keeps.update((name, getattr(state, name)) for name in BACK)

    def kernel(place_ref, ref, *own):
        vars(ref).update(zip(LINK_STATE, own))

        @pl.when(place_ref[0] != 0)
        def _():
            if micro == 0:
                ref.keys_grad, ref.values_grad = two_sides(ref.link_grad)
            middle_step(micro, ref)
            if micro == 0:
                middle_keys(micro, ref)

        @pl.when(place_ref[0] == 0)
        def _():
            rows = slice(micro * ROWS, (micro + 1) * ROWS)
            for part in range(4):
                cut = slice(part * D, (part + 1) * D)
                ref.wide[rows, cut] = gelu_slope(ref.wide[rows, cut])

    cost = (2 * ROWS * D * 10000, 8_000_000)
    token, made = call(
        kernel, "middle_stage", place, token, reads, keeps, makes, scratch=scratch, cost=cost
    )
    vars(state).update(made)
    return token


def middle_keys_stage(micro, place, token, state, link):
    reads = dict(query=state.query, link=link, link_probs=state.link_probs, mixed=state.mixed)

    def kernel(place_ref, ref):
        @pl.when(place_ref[0] != 0)
        def _():
            middle_keys(micro, ref)

    cost = mflop(200)
    keeps, makes = dict(right=state.right), dict(keys_grad=SIDE)
    token, made = call(kernel, "middle_keys", place, token, reads, keeps, makes, cost=cost)
    vars(state).update(made)
    return token


def values_step(micro, first, ref):
    rows = slice(micro * ROWS, (micro + 1) * ROWS)

    @pl.when(first)
    def _():
        cotangent = ref.cotangent[rows, :].astype(F32)
        ref.grad[rows, :] = cotangent + mm_nt(ref.values_grad[...], ref.w_cross[:, D:])
        ref.right[rows, D:] = ref.values_grad[...]


def gate_step(micro, first, ref):
    rows = slice(micro * ROWS, (micro + 1) * ROWS)

    @pl.when(first)
    def _():
        grad = ref.grad[rows, :] + mm_nt(ref.keys_grad[...], ref.w_cross[:, :D])
        ref.grad[rows, :] = grad
        ref.gate[rows, :] = grad.astype(LOW)
        ref.right[rows, :D] = ref.keys_grad[...]
        ref.left_b[rows, :] = ref.left_a[rows, :]

    @pl.when(jnp.logical_not(first))
    def _():
        ref.gate[rows, :] = ref.cotangent[rows, :]
        for part in range(4):
            cut = slice(part * D, (part + 1) * D)
            ref.act[rows, cut] = gelu(ref.hidden[rows, cut]).astype(LOW)


def back_step(micro, first, ref):
    rows = slice(micro * ROWS, (micro + 1) * ROWS)

    @pl.when(first)
    def _():
        grad = ref.grad[rows, :]
        for part in range(4):
            cut = slice(part * D, (part + 1) * D)
            grad_act = mm_nt(ref.gate[rows, :], ref.w_down[cut, :])
            grad_hidden = (ref.wide[rows, cut] * grad_act).astype(LOW)
            ref.grad_hidden[rows, cut] = grad_hidden
            grad = grad + mm_nt(grad_hidden, ref.w_up[:, cut])
        ref.grad[rows, :] = grad
        ref.grad_low[rows, :] = grad.astype(LOW)

    @pl.when(jnp.logical_not(first))
    def _():
        grad = ref.grad[rows, :] + mm_nt(ref.right[rows, :D], ref.w_cross[:, :D])
        ref.grad[rows, :] = grad
        ref.grad_low[rows, :] = grad.astype(LOW)


def back_stage(micro, place, token, state, link_grad, parts, send=(), cost=5000):
    reads = dict(
        cotangent=state.cotangent,
        w_cross=state.w_cross,
        w_up=state.w_up,
        w_down=state.w_down,
        wide=state.wide,
        left_a=state.left_a,
        **link_grad,
        narrow=state.narrow,
        mix=state.mix,
    )
    keeps = {name: getattr(state, name) for name in BACK}
    keeps.update(act=state.act)
    makes = {}
    for at, chunk in enumerate(send):
        makes["send%d" % at] = ((chunk.rows, D), LOW)

    def kernel(place_ref, ref):
        if micro == 0:
            ref.keys_grad, ref.values_grad = two_sides(ref.link_grad)
        for part in parts:
            part(micro, place_ref[0] == 0, ref)
        for at, chunk in enumerate(send):
            put_send(place_ref, ref, chunk, getattr(ref, "send%d" % at))

    token, made = call(kernel, "back_stage", place, token, reads, keeps, makes, cost=mflop(cost))
    sends = [made.pop(name) for name in makes]
    vars(state).update(made)
    return token, sends


def late_kernel(place_ref, ref, mixed_v):
    mixed_v[...] = mm_nt(ref.grad_low[...], ref.w_out[...]).astype(LOW)
    for micro in range(MB):
        rows = slice(micro * ROWS, (micro + 1) * ROWS)

        def write(pair, *grads, rows=rows, first=0):
            for part, value in enumerate(grads):
                at = (first + part) * D + pair * LANES
                rounded, rest = in_two(value)
                ref.grad_proj[rows, at : at + LANES] = rounded
                ref.grad_rest[rows, at : at + LANES] = rest

        def read_probs(pair, micro=micro):
            return ref.probs[micro, pair]

        attend_back_keys(
            columns(ref.proj, rows, 0),
            columns(ref.proj, rows, D),
            columns(ref.proj, rows, 2 * D),
            read_probs,
            columns(mixed_v, rows, 0),
            write,
        )
        attend_back_values(
            read_probs,
            columns(mixed_v, rows, 0),
            lambda pair, value, write=write: write(pair, value, first=2),
        )
    for here, gradient, run in QKV.each():
        value = product_of(gradient, ref, run, 1 - place_ref[1])
        ref.send[here, :], ref.more[here, :] = in_two(value)


def late_stage(place, token, state, cost):
    reads = dict(
        grad_low=state.grad_low,
        w_out=state.w_out,
        proj=state.proj,
        probs=state.probs,
        tokens=state.tokens,
        mix=state.mix,
    )
    wide, side = ((BOTH, 3 * D), LOW), ((QKV.rows, D), LOW)
    makes = dict(grad_proj=wide, grad_rest=wide, send=side, more=side)
    scratch = (pltpu.VMEM((BOTH, D), LOW),)
    token, made = call(
        late_kernel, "late_stage", place, token, reads, {}, makes, None, scratch, mflop(cost)
    )
    sends = made.pop("send"), made.pop("more")
    vars(state).update(made)
    return token, sends


def final_kernel(place_ref, ref, result_v, grad_v, sems):
    @pl.when(place_ref[0] == 0)
    def _():
        result_v[...] = ref.result[...]

    @pl.when(place_ref[0] != 0)
    def _():
        total = ref.across_mid[...]
        for part in range(4):
            cut = slice(part * D, (part + 1) * D)
            total = total + mm(ref.act[:, cut], ref.w_down[cut, :])
        result_v[...] = total.astype(LOW)

    first = fetch(result_v, ref.outputs.at[0], sems.at[0])
    grad_v[...] = (ref.grad[...] + mm_nt(ref.grad_proj[...], ref.w_qkv[...])).astype(LOW)
    second = fetch(grad_v, ref.input_grad.at[0], sems.at[1])
    first.wait()
    second.wait()


def final_stage(place, token, state, cost):
    reads = dict(
        grad=state.grad,
        grad_proj=state.grad_proj,
        w_qkv=state.w_qkv,
        result=state.result,
        across_mid=state.across_mid,
        act=state.act,
        w_down=state.w_down,
    )
    half = ((1, BOTH, D), LOW)
    stores = dict(outputs=half, input_grad=half)
    scratch = [pltpu.VMEM((BOTH, D), LOW)] * 2 + [pltpu.SemaphoreType.DMA((2,))]
    return call(
        final_kernel, "final_stage", place, token, reads, {}, {}, stores, scratch, mflop(cost)
    )


PIECE = HALF // 2
PIECES = 7

Y_FIRST = (1, 2, 3)
Z_FIRST = (2, 1, 3)


def cut_of(part):
    return slice(part * D, (part + 1) * D)


class Gradient:
    def __init__(self, sides, store, down=False):
        self.sides = sides
        self.store = store
        self.down = down

    def rows(self, part, half, first, count):
        start = (part * D if self.down else 0) + first * PIECE
        return pl.ds(pl.multiple_of(start + half * HALF, PIECE), count * PIECE)

    def product(self, ref, part, half, first, count):
        left_ref, right_ref, column, *rest = self.sides(ref, part)
        value = left_ref[:, self.rows(part, half, first, count)]
        total = mm_tn(value, right_ref[:, cut_of(column)])
        for rest_ref in rest:
            total = total + mm_tn(value, rest_ref[:, cut_of(column)])
        return total

    def target(self, array, part, half, first, count):
        column = 0 if self.down else part * D
        return array.at[0, self.rows(part, half, first, count), pl.ds(column, D)]


G_DOWN = Gradient(lambda ref, part: (ref.act, ref.gate, 0), dict(g_down=((1, FF, D), F32)), down=True)
G_UP = Gradient(lambda ref, part: (ref.narrow, ref.grad_hidden, part), dict(g_up=((1, D, FF), F32)))
G_CROSS = Gradient(
    lambda ref, part: ((ref.left_a, ref.left_b)[part], ref.right, part),
    dict(g_cross=((1, D, 2 * D), F32)),
)
G_OUT = Gradient(lambda ref, part: (ref.mix, ref.grad_low, 0), dict(g_out=((1, D, D), F32)))
G_QKV = Gradient(
    lambda ref, part: (ref.tokens, ref.grad_proj, part, ref.grad_rest),
    dict(g_qkv=((1, D, 3 * D), F32)),
)


class Chunk:
    def __init__(self, levels, operands, runs, fine=False):
        self.levels = levels
        self.fine = fine
        self.operands = operands
        self.runs = runs
        self.rows = PIECES * PIECE
        self.stores = {}
        for run in runs:
            self.stores.update(run[0].store)

    def each(self):
        at = 0
        for gradient, part, first, count in self.runs:
            yield slice(at, at + count * PIECE), gradient, (part, first, count)
            at += count * PIECE


def product_of(gradient, ref, run, half):
    part, first, count = run
    return gradient.product(ref, part, half, first, count)


CROSS = Chunk(
    (Y_FIRST, Z_FIRST),
    lambda state: dict(
        left_a=state.left_a,
        left_b=state.left_b,
        right=state.right,
        mix=state.mix,
        grad_low=state.grad_low,
        act=state.act,
        gate=state.gate,
        narrow=state.narrow,
        grad_hidden=state.grad_hidden,
    ),
    [(G_CROSS, 0, 0, 2), (G_CROSS, 1, 0, 2), (G_OUT, 0, 0, 1), (G_DOWN, 3, 1, 1), (G_UP, 3, 1, 1)],
)
DOWN = Chunk(
    (Y_FIRST, Z_FIRST),
    lambda state: dict(act=state.act, gate=state.gate),
    [(G_DOWN, 0, 0, 2), (G_DOWN, 1, 0, 2), (G_DOWN, 2, 0, 2), (G_DOWN, 3, 0, 1)],
)
UP = Chunk(
    (Y_FIRST, Z_FIRST),
    lambda state: dict(narrow=state.narrow, grad_hidden=state.grad_hidden),
    [(G_UP, 0, 0, 2), (G_UP, 1, 0, 2), (G_UP, 2, 0, 2), (G_UP, 3, 0, 1)],
)
QKV = Chunk(
    (Z_FIRST, Y_FIRST),
    lambda state: dict(
        tokens=state.tokens,
        grad_proj=state.grad_proj,
        grad_rest=state.grad_rest,
        mix=state.mix,
        grad_low=state.grad_low,
    ),
    [(G_QKV, 0, 0, 2), (G_QKV, 1, 0, 2), (G_QKV, 2, 0, 2), (G_OUT, 0, 1, 1)],
    fine=True,
)


def put_send(place_ref, ref, chunk, send):
    for here, gradient, run in chunk.each():
        send[here, :] = product_of(gradient, ref, run, 1 - place_ref[1]).astype(LOW)


class Summing:
    def __init__(self, chunk, state, place, count):
        self.chunk = chunk
        self.state = state
        self.place = place
        self.count = count
        self.depth = count.bit_length() - 2
        self.step = 0

    def swap(self, value, level):
        def partner(i):
            bit = self.chunk.levels[i % 2][level - 1] if 0 < level < 4 else level
            return i ^ (1 << bit)

        return lax.ppermute(value, "dp", [(i, partner(i)) for i in range(self.count)])

    def call(self, kernel, token, reads, makes, stores=None, scratch=(), patches=None):
        name = "sum_%d" % self.step
        rest = (stores, scratch, mflop(self.cost), patches)
        return call(kernel, name, self.place, token, reads, {}, makes, *rest)

    def halves(self, place_ref, level, rows):
        first, second = (place_ref[1 + levels[level - 1]] for levels in self.chunk.levels)
        bit = jnp.where(place_ref[1] == 0, first, second)
        half = rows // 2
        own = pl.ds(pl.multiple_of(bit * half, half), half)
        return own, pl.ds(pl.multiple_of((1 - bit) * half, half), half)

    def launch(self, send, *more):
        self.got = self.swap(send, 0)
        self.more = dict(more=self.swap(*more, 0)) if more else {}

    def start(self, token, cost):
        def kernel(place_ref, ref):
            put_send(place_ref, ref, self.chunk, ref.send)

        makes = dict(send=((self.chunk.rows, D), LOW))
        reads = self.chunk.operands(self.state)
        token, made = call(kernel, "product", self.place, token, reads, {}, makes, cost=mflop(cost))
        self.launch(made["send"])
        return token

    def advance(self, token, grads, cost):
        self.cost = cost
        rows = self.chunk.rows
        if self.step == 0:
            token = self.split_first(token, rows)
        elif self.step == 1:
            token = self.split(token, rows // 2)
        elif self.step == 2:
            token = self.round_off(token, rows // 4)
        elif self.step == 3:
            for level in range(4, self.depth + 1):
                token = self.pair_sum(token, rows // 4, level, False)
            token = self.pair_sum(token, rows // 4, 2, True)
        elif self.step == 4:
            token = self.merge(token, rows // 4, 1)
        elif self.step == 5:
            token = self.merge(token, rows // 2, 0)
        else:
            token = self.unpack(token, grads, False, cost)
        self.step += 1
        return token

    def split_first(self, token, rows):
        chunk = self.chunk

        def kernel(place_ref, ref, total):
            for here, gradient, run in chunk.each():
                own = product_of(gradient, ref, run, place_ref[1])
                total[here, :] = own + ref.got[here, :].astype(F32)
                if chunk.fine:
                    total[here, :] = total[here, :] + ref.more[here, :].astype(F32)
            own, other = self.halves(place_ref, 1, rows)
            ref.send[...] = total[other, :].astype(LOW)
            ref.keep[...] = total[own, :]

        reads = dict(got=self.got, **self.more, **chunk.operands(self.state))
        makes = dict(send=((rows // 2, D), LOW), keep=((rows // 2, D), F32))
        scratch = (pltpu.VMEM((rows, D), F32),)
        token, made = self.call(kernel, token, reads, makes, scratch=scratch)
        self.keep = made["keep"]
        self.got = self.swap(made["send"], 1)
        return token

    def split(self, token, rows):
        def kernel(place_ref, ref):
            own, other = self.halves(place_ref, 2, rows)
            ref.send[...] = (ref.keep[other, :] + ref.got[other, :].astype(F32)).astype(LOW)
            ref.kept[...] = ref.keep[own, :] + ref.got[own, :].astype(F32)

        reads = dict(keep=self.keep, got=self.got)
        makes = dict(send=((rows // 2, D), LOW), kept=((rows // 2, D), F32))
        token, made = self.call(kernel, token, reads, makes)
        self.keep = made["kept"]
        self.got = self.swap(made["send"], 2)
        return token

    def round_off(self, token, rows):
        fine = False

        def kernel(place_ref, ref):
            total = ref.keep[...] + ref.got[...].astype(F32)
            if fine:
                ref.piece[...], ref.rest[...] = in_two(total)
            else:
                ref.piece[...] = total.astype(LOW)

        side = ((rows, D), LOW)
        makes = dict(piece=side, rest=side) if fine else dict(piece=side)
        token, made = self.call(kernel, token, dict(keep=self.keep, got=self.got), makes)
        self.spread(made, 3)
        return token

    def spread(self, made, level):
        self.piece = made["piece"]
        self.got = self.swap(self.piece, level)
        self.more = {}
        if "rest" in made:
            self.more = dict(rest=made["rest"], more=self.swap(made["rest"], level))

    def pair_sum(self, token, rows, level, last):
        fine = False

        def kernel(place_ref, ref):
            own, other = ref.held[...].astype(F32), ref.got[...].astype(F32)
            if fine:
                own, other = own + ref.rest[...].astype(F32), other + ref.more[...].astype(F32)
            if fine and not last:
                ref.piece[...], ref.rest_out[...] = in_two(own + other)
            else:
                ref.piece[...] = (own + other).astype(LOW)

        side = ((rows, D), LOW)
        makes = dict(piece=side, rest_out=side) if fine and not last else dict(piece=side)
        reads = dict(held=self.piece, got=self.got, **self.more)
        token, made = self.call(kernel, token, reads, makes)
        if "rest_out" in made:
            made["rest"] = made.pop("rest_out")
        self.spread(made, level)
        return token

    def merge(self, token, rows, level):
        def kernel(place_ref, ref):
            own, other = self.halves(place_ref, level + 1, 2 * rows)
            ref.piece[own, :] = ref.held[...]
            ref.piece[other, :] = ref.got[...]

        makes = dict(piece=((2 * rows, D), LOW))
        token, made = self.call(kernel, token, dict(held=self.piece, got=self.got), makes)
        self.piece = made["piece"]
        self.got = self.swap(self.piece, level)
        return token

    def unpack(self, token, grads, own, cost):
        chunk = self.chunk
        patches = {name: grads[name] for name in chunk.stores if name in grads}
        stores = {name: kind for name, kind in chunk.stores.items() if name not in grads}

        def kernel(place_ref, ref, wide, sems):
            half = place_ref[1] if own else 1 - place_ref[1]
            copies = []
            for index, (here, gradient, (part, first, count)) in enumerate(chunk.each()):
                wide[here, :] = ref.source[here, :].astype(F32)
                array = getattr(ref, list(gradient.store)[0])
                target = gradient.target(array, part, half, first, count)
                rows = pl.ds(here.start, here.stop - here.start)
                copies.append(fetch(wide.at[rows], target, sems.at[index]))
            for copy in copies:
                copy.wait()

        scratch = (pltpu.VMEM((chunk.rows, D), F32), pltpu.SemaphoreType.DMA((len(chunk.runs),)))
        reads = dict(source=self.piece if own else self.got)
        name = "unpack_%d" % own
        token, made = call(
            kernel, name, self.place, token, reads, {}, {}, stores, scratch, mflop(cost), patches
        )
        grads.update(made)
        return token


CHUNKS = (DOWN, CROSS, UP, QKV)
GATE, BACK_ATTN, BACK_FFN, FINAL, MORE, OWN = 10, 11, 12, 13, 14, 20
ORDER = (10, 12, 0, 14, 1, 11, 0, 2, 1, 3, 0, 2, 1, 3, 0, 13, 2, 1, 3, 0, 2, 1, 3, 0, 2, 20, 1, 21, 3, 0, 2, 1, 22, 3, 2, 23, 3)
COSTS = (1000, 1000, 8000, 4000, 8000, 8000, 8000, 4000, 1000, 1000, 1000, 1000, 1000, 1000, 1000, 1000, 1000, 1000, 1000, 1000, 1000, 1000, 1000, 1000, 8000, 8000, 1000, 8000, 1000, 1000, 1000, 1000, 1000, 50, 3000, 1000, 1000)


def on_device(inputs, lengths, w_qkv, w_attn_out, w_cross, w_up, w_down, cotangent):
    count = lax.axis_size("dp")
    given = (lengths, inputs, w_qkv, w_attn_out, w_up, w_down, w_cross, cotangent)
    place, token, link, state = first_stage(given)
    links = [lax.ppermute(link, "section", [(0, 1)])]
    link = second_stage(place, state, given)
    links.append(lax.ppermute(link, "section", [(0, 1)]))

    def to_encoder(side):
        return lax.ppermute(side, "section", [(1, 0)])

    token = middle_stage(0, place, token, state, links[0])
    grads = [dict(link_grad=to_encoder(state.link_grad))]
    token = middle_stage(1, place, token, state, links[1])
    values = to_encoder(state.values_grad)
    token = middle_keys_stage(1, place, token, state, links[1])
    grads.append(dict(keys_grad=to_encoder(state.keys_grad)))
    token, _ = back_stage(0, place, token, state, grads[0], (values_step, gate_step, back_step), cost=900)
    token, _ = back_stage(1, place, token, state, dict(values_grad=values), (values_step,), cost=300)
    chunks = [Summing(chunk, state, place, count) for chunk in CHUNKS]
    made = {}
    for task, cost in zip(ORDER, COSTS):
        if task == GATE:
            token, sends = back_stage(1, place, token, state, grads[1], (gate_step,), [DOWN], cost)
            chunks[0].launch(*sends)
        elif task == BACK_FFN:
            token, sends = back_stage(1, place, token, state, grads[1], (back_step,), [CROSS], cost)
            chunks[1].launch(*sends)
        elif task == MORE:
            token = chunks[2].start(token, cost)
        elif task == BACK_ATTN:
            token, sends = late_stage(place, token, state, cost)
            chunks[3].launch(*sends)
        elif task == FINAL:
            token, ends = final_stage(place, token, state, cost)
            made.update(ends)
        elif task >= OWN:
            token = chunks[task - OWN].unpack(token, made, True, cost)
        else:
            token = chunks[task].advance(token, made, cost)
    done = SimpleNamespace(**made)
    return (
        done.outputs,
        done.input_grad,
        done.g_qkv,
        done.g_out,
        done.g_cross,
        done.g_up,
        done.g_down,
    )


def solution(mesh):
    return jax.shard_map(
        on_device,
        mesh=mesh,
        in_specs=(
            P("section", "dp", None),
            P("dp", None, None),
            P("section", None, None),
            P("section", None, None),
            P("section", None, None),
            P("section", None, None),
            P("section", None, None),
            P("section", "dp", None),
        ),
        out_specs=(
            P("section", "dp", None),
            P("section", "dp", None),
            P("section", None, None),
            P("section", None, None),
            P("section", None, None),
            P("section", None, None),
            P("section", None, None),
        ),
        check_vma=False,
    )
```

```python
from types import SimpleNamespace

import jax
import jax.numpy as jnp
from jax import lax
from jax.experimental import pallas as pl
from jax.experimental.pallas import tpu as pltpu
from jax.sharding import PartitionSpec as P

D = 512
HEADS = 8
HEAD_DIM = 64
FF = 2048
ROWS = 128
SLOTS = 16
MB = 2
BOTH = MB * ROWS
PAIRS = HEADS // 2
LANES = 2 * HEAD_DIM
HALF = D // 2
SCALE = HEAD_DIM ** (-0.5)
GELU_IN = 0.7978845608028654
GELU_CUBE = 0.044715
LOW = jnp.bfloat16
F32 = jnp.float32
MIB = 1024 * 1024
DP = "dp"
SECTION = "section"
PLACE = 4


def in_two(value):
    rounded = value.astype(LOW)
    return rounded, (value - rounded.astype(F32)).astype(LOW)


def mm(left, right):
    return jnp.dot(left, right, preferred_element_type=F32)


def mm_nt(left, right):
    return lax.dot_general(left, right, (((1,), (1,)), ((), ())), preferred_element_type=F32)


def mm_tn(left, right):
    return lax.dot_general(left, right, (((0,), (0,)), ((), ())), preferred_element_type=F32)


def gelu(hidden):
    inner = GELU_IN * (hidden + GELU_CUBE * (hidden * hidden * hidden))
    return hidden * (0.5 * (1.0 + jnp.tanh(inner)))


def gelu_slope(hidden):
    square = hidden * hidden
    inner = GELU_IN * (hidden + GELU_CUBE * (square * hidden))
    bent = jnp.tanh(inner)
    inner_slope = GELU_IN * (1.0 + (3.0 * GELU_CUBE) * square)
    return 0.5 * (1.0 + bent) + 0.5 * hidden * (1.0 - bent * bent) * inner_slope


def segments(lengths_ref, micro, which, dim):
    position = lax.broadcasted_iota(jnp.int32, (ROWS, ROWS), dim)
    end = jnp.int32(0)
    seg = jnp.zeros((ROWS, ROWS), jnp.int32)
    for slot in range(SLOTS):
        end = end + lengths_ref[micro, which, slot]
        seg = seg + (position >= end).astype(jnp.int32)
    return seg


def low_lanes():
    return lax.broadcasted_iota(jnp.int32, (ROWS, LANES), 1) < HEAD_DIM


def two_heads(pair, lanes):
    nothing = jnp.zeros_like(pair)
    return jnp.concatenate(
        [jnp.where(lanes, pair, nothing), jnp.where(lanes, nothing, pair)], axis=0
    )


def softmax(scores):
    highest = jnp.max(scores, axis=0, keepdims=True)
    raised = jnp.exp(scores - highest)
    return raised * (1.0 / jnp.sum(raised, axis=0, keepdims=True))


def two_halves(value):
    return value[:ROWS, :], value[ROWS:, :]


def attend(read_q, read_k, read_v, mask, write_probs, write_mix):
    lanes = low_lanes()
    for pair in range(PAIRS):
        query = (read_q(pair).astype(F32) * SCALE).astype(LOW)
        scores = mm_nt(two_heads(read_k(pair), lanes), query)
        heads = [softmax(jnp.where(mask, part, -1e30)) for part in two_halves(scores)]
        probs = jnp.concatenate(heads, axis=0)
        write_probs(pair, probs)
        write_mix(pair, mm_tn(probs.astype(LOW), two_heads(read_v(pair), lanes)).astype(LOW))


def attend_back_values(read_probs, read_grad, write):
    lanes = low_lanes()
    for pair in range(PAIRS):
        grad_v = mm(read_probs(pair).astype(LOW), read_grad(pair))
        write(pair, jnp.where(lanes, *two_halves(grad_v)))


def attend_back_keys(read_q, read_k, read_v, read_probs, read_grad, write):
    lanes = low_lanes()
    for pair in range(PAIRS):
        query = (read_q(pair).astype(F32) * SCALE).astype(LOW)
        probs = read_probs(pair)
        grad_probs = mm_nt(two_heads(read_v(pair), lanes), read_grad(pair))
        slopes = []
        for head, change in zip(two_halves(probs), two_halves(grad_probs)):
            total = jnp.sum(head * change, axis=0, keepdims=True)
            slopes.append((head * (change - total)).astype(LOW))
        slopes = jnp.concatenate(slopes, axis=0)
        grad_q = mm_tn(slopes, two_heads(read_k(pair), lanes)) * SCALE
        grad_k = jnp.where(lanes, *two_halves(mm(slopes, query)))
        write(pair, grad_q, grad_k)


def columns(ref, rows, start):
    def read(pair):
        return ref[rows, start + pair * LANES : start + (pair + 1) * LANES]

    return read


def fetch(source, target, sem):
    copy = pltpu.make_async_copy(source, target, sem)
    copy.start()
    return copy


WEIGHTS = dict(
    w_qkv=((D, 3 * D), LOW),
    w_out=((D, D), LOW),
    w_cross=((D, 2 * D), LOW),
    w_up=((D, FF), LOW),
    w_down=((FF, D), LOW),
)
HELD = dict(tokens=((BOTH, D), LOW), cotangent=((BOTH, D), LOW))
STATE = dict(
    proj=((BOTH, 3 * D), LOW),
    mix=((BOTH, D), LOW),
    probs=((MB, PAIRS, 2 * ROWS, ROWS), F32),
    wide=((BOTH, FF), F32),
    mid=((BOTH, D), F32),
    act=((BOTH, FF), LOW),
    narrow=((BOTH, D), LOW),
    result=((BOTH, D), LOW),
    left_a=((BOTH, D), LOW),
    query=((BOTH, D), LOW),
    across=((BOTH, ROWS), F32),
)
BACK = dict(
    hidden=((BOTH, FF), F32),
    across_mid=((BOTH, D), F32),
    left_b=((BOTH, D), LOW),
    right=((BOTH, 2 * D), LOW),
    grad_hidden=((BOTH, FF), LOW),
    gate=((BOTH, D), LOW),
    grad=((BOTH, D), F32),
    grad_low=((BOTH, D), LOW),
)


def shaped(table):
    return [pltpu.VMEM(shape, kind) for shape, kind in table.values()]


def same_shape(arrays):
    return [pltpu.VMEM(value.shape, value.dtype) for value in arrays]


def held(arrays):
    return [pltpu.with_memory_space_constraint(value, pltpu.VMEM) for value in arrays]


def in_place(place):
    return pltpu.with_memory_space_constraint(place, pltpu.SMEM)


def left(arrays):
    return [pltpu.with_memory_space_constraint(value, pltpu.HBM) for value in arrays]


def in_vmem():
    return pl.BlockSpec(memory_space=pltpu.VMEM)


def in_smem():
    return pl.BlockSpec(memory_space=pltpu.SMEM)


def in_hbm():
    return pl.BlockSpec(memory_space=pltpu.HBM)


TOKEN = ((8, LANES), F32)


def mflop(count):
    return count * 1_000_000, 0


def call(
    kernel, name, place, token, reads, keeps, makes, stores=None, scratch=(), cost=(0, 0), patches=None
):
    stores, patches = stores or {}, patches or {}
    out_shape = same_shape(keeps.values()) + shaped(makes) + shaped(dict(token=TOKEN))
    out_shape += [pltpu.HBM(shape, kind) for shape, kind in stores.values()]
    out_shape += [pltpu.HBM(value.shape, value.dtype) for value in patches.values()]
    reads_n, keeps_n, makes_n = len(reads), len(keeps), len(makes)
    stores_n, patches_n = len(stores), len(patches)
    aliases = {2 + reads_n + i: i for i in range(keeps_n)}
    for i in range(patches_n):
        aliases[2 + reads_n + keeps_n + i] = keeps_n + makes_n + 1 + stores_n + i

    def body(place_ref, token_in, *refs):
        del token_in
        refs = list(refs)
        named = dict(zip(reads, refs[:reads_n]))
        refs = refs[reads_n + keeps_n + patches_n :]
        named.update(zip(keeps, refs[:keeps_n]))
        named.update(zip(makes, refs[keeps_n : keeps_n + makes_n]))
        refs = refs[keeps_n + makes_n :]
        refs[0][...] = jnp.zeros(*TOKEN)
        named.update(zip(stores, refs[1 : 1 + stores_n]))
        refs = refs[1 + stores_n :]
        named.update(zip(patches, refs[:patches_n]))
        kernel(place_ref, SimpleNamespace(**named), *refs[patches_n:])

    results = pl.pallas_call(
        body,
        out_shape=out_shape,
        in_specs=[in_smem()] + [in_vmem()] * (1 + reads_n + keeps_n) + [in_hbm()] * patches_n,
        out_specs=[in_vmem()] * (keeps_n + makes_n + 1) + [in_hbm()] * (stores_n + patches_n),
        scratch_shapes=list(scratch),
        input_output_aliases=aliases,
        compiler_params=pltpu.CompilerParams(vmem_limit_bytes=16 * MIB),
        cost_estimate=pl.CostEstimate(flops=cost[0], bytes_accessed=cost[1], transcendentals=0),
        name=name,
    )(
        in_place(place),
        *held([token]),
        *held(reads.values()),
        *held(keeps.values()),
        *left(patches.values()),
    )
    names = list(keeps) + list(makes)
    token = results[len(names)]
    made = dict(zip(names, results))
    made.update(zip(list(stores) + list(patches), results[len(names) + 1 :]))
    return token, made


def forward_step(micro, encoder, lengths_ref, ref, link, gets):
    rows = slice(micro * ROWS, (micro + 1) * ROWS)
    gets.tokens.wait()
    tokens = ref.tokens[rows, :]
    gets.w_qkv[0].wait()
    gets.lengths.wait()
    if encoder:
        mask = segments(lengths_ref, micro, 0, 0) == segments(lengths_ref, micro, 0, 1)
    else:
        seg_tgt = segments(lengths_ref, micro, 1, 1)
        source = segments(lengths_ref, micro, 0, 0)
        ref.across[rows, :] = (source == seg_tgt).astype(F32)
        earlier = lax.broadcasted_iota(jnp.int32, (ROWS, ROWS), 0) <= lax.broadcasted_iota(
            jnp.int32, (ROWS, ROWS), 1
        )
        mask = (segments(lengths_ref, micro, 1, 0) == seg_tgt) & earlier
    for part in range(3):
        cut = slice(part * D, (part + 1) * D)
        if part:
            gets.w_qkv[part].wait()
        ref.proj[rows, cut] = mm(tokens, ref.w_qkv[:, cut]).astype(LOW)

    def write_probs(pair, value):
        ref.probs[micro, pair] = value

    def write_mix(pair, value):
        ref.mix[rows, pair * LANES : (pair + 1) * LANES] = value

    attend(
        columns(ref.proj, rows, 0),
        columns(ref.proj, rows, D),
        columns(ref.proj, rows, 2 * D),
        mask,
        write_probs,
        write_mix,
    )
    gets.w_out.wait()
    mid = tokens.astype(F32) + mm(ref.mix[rows, :], ref.w_out[...])

    if not encoder:
        ref.left_a[rows, :] = mid.astype(LOW)
        ref.mid[rows, :] = mid
        return
    ref.narrow[rows, :] = mid.astype(LOW)
    gets.w_up.wait()
    gets.w_down.wait()
    for part in range(4):
        cut = slice(part * D, (part + 1) * D)
        hidden = mm(ref.narrow[rows, :], ref.w_up[:, cut])
        ref.wide[rows, cut] = hidden
        ref.act[rows, cut] = gelu(hidden).astype(LOW)
    total = mid + mm(ref.act[rows, :], ref.w_down[...])
    ref.result[rows, :] = total.astype(LOW)
    gets.w_cross.wait()
    link[...] = mm(ref.result[rows, :], ref.w_cross[...]).astype(LOW)
    ref.left_a[rows, :] = ref.result[rows, :]


def decoder_ahead(ref, gets):
    gets.w_cross.wait()
    ref.query[...] = mm(ref.left_a[...], ref.w_cross[:, :D]).astype(LOW)
    gets.cotangent.wait()
    gets.w_down.wait()
    for part in range(4):
        cut = slice(part * D, (part + 1) * D)
        ref.wide[:, cut] = mm_nt(ref.cotangent[...], ref.w_down[cut, :])
    gets.w_up.wait()


class Fetch:
    def __init__(self, source, target, sem):
        self.copy = pltpu.make_async_copy(source, target, sem)

    def start(self):
        self.copy.start()

    def wait(self):
        self.copy.wait()


class Arrived:
    def wait(self):
        pass


def fetches(ref, sems, lengths_ref, sources):
    lengths_in, tokens_in, qkv_in, out_in, up_in, down_in, cross_in, cotangent_in = sources
    parts = [pl.ds(part * D, D) for part in range(3)]
    return SimpleNamespace(
        lengths=Fetch(lengths_in, lengths_ref, sems.at[0]),
        tokens=Fetch(tokens_in.at[0], ref.tokens, sems.at[1]),
        w_qkv=[
            Fetch(qkv_in.at[0, :, part], ref.w_qkv.at[:, part], sems.at[2 + at])
            for at, part in enumerate(parts)
        ],
        w_out=Fetch(out_in.at[0], ref.w_out, sems.at[5]),
        w_up=Fetch(up_in.at[0], ref.w_up, sems.at[6]),
        w_down=Fetch(down_in.at[0], ref.w_down, sems.at[7]),
        w_cross=Fetch(cross_in.at[0], ref.w_cross, sems.at[8]),
        cotangent=Fetch(cotangent_in.at[0], ref.cotangent, sems.at[9]),
    )


def start_all(gets):
    order = [gets.lengths, gets.tokens, *gets.w_qkv, gets.w_out, gets.w_up, gets.w_down, gets.w_cross]
    for get in order:
        get.start()


FETCHED = 8
FETCH_SCRATCH = [pltpu.SMEM((MB, 2, SLOTS), jnp.int32), pltpu.SemaphoreType.DMA((FETCHED + 2,))]


def first_stage(given):
    makes = {**WEIGHTS, **HELD, **STATE, **dict(link=((ROWS, 2 * D), LOW), token=TOKEN)}

    def body(*refs):
        place_ref, lengths_ref, sems = refs[FETCHED + len(makes) :]
        ref = SimpleNamespace(**dict(zip(makes, refs[FETCHED:])))
        index = lax.axis_index(DP).astype(jnp.int32)
        section = lax.axis_index(SECTION).astype(jnp.int32)
        place_ref[0] = section
        for bit in range(PLACE - 1):
            place_ref[1 + bit] = (index >> bit) % 2
        ref.token[...] = jnp.zeros(*TOKEN)

        @pl.when(section == 0)
        def _():
            gets = fetches(ref, sems, lengths_ref, refs[:FETCHED])
            start_all(gets)
            forward_step(0, True, lengths_ref, ref, ref.link, gets)

    results = pl.pallas_call(
        body,
        out_shape=shaped(makes) + [pltpu.SMEM((PLACE,), jnp.int32)],
        in_specs=[in_hbm()] * FETCHED,
        out_specs=[in_vmem()] * len(makes) + [in_smem()],
        scratch_shapes=FETCH_SCRATCH,
        compiler_params=pltpu.CompilerParams(vmem_limit_bytes=16 * MIB),
        cost_estimate=pl.CostEstimate(
            flops=2 * ROWS * D * 7168, bytes_accessed=10_000_000, transcendentals=0
        ),
        name="first_stage",
    )(*left(given))
    made = SimpleNamespace(**dict(zip(makes, results)))
    link, token = made.link, made.token
    del made.link, made.token
    return results[-1], token, link, made


def second_stage(place, state, given):
    kept = {**WEIGHTS, **HELD, **STATE}
    keeps = [getattr(state, name) for name in kept]

    def body(place_ref, *refs):
        sources = refs[:FETCHED]
        refs = refs[FETCHED + len(keeps) :]
        ref = SimpleNamespace(**dict(zip(kept, refs)))
        link, lengths_ref, sems = refs[len(keeps) :]
        gets = fetches(ref, sems, lengths_ref, sources)
        here = Arrived()

        @pl.when(place_ref[0] == 0)
        def _():
            gets.lengths.start()
            gets.cotangent.start()
            arrived = SimpleNamespace(
                lengths=gets.lengths,
                tokens=here,
                w_qkv=[here] * 3,
                w_out=here,
                w_up=here,
                w_down=here,
                w_cross=here,
            )
            forward_step(1, True, lengths_ref, ref, link, arrived)
            gets.cotangent.wait()

        @pl.when(place_ref[0] != 0)
        def _():
            start_all(gets)
            gets.cotangent.start()
            forward_step(0, False, lengths_ref, ref, link, gets)
            arrived = SimpleNamespace(lengths=here, tokens=here, w_qkv=[here] * 3, w_out=here)
            forward_step(1, False, lengths_ref, ref, link, arrived)
            decoder_ahead(ref, gets)

    results = pl.pallas_call(
        body,
        out_shape=same_shape(keeps) + [pltpu.VMEM((ROWS, 2 * D), LOW)],
        in_specs=[in_smem()] + [in_hbm()] * FETCHED + [in_vmem()] * len(keeps),
        out_specs=[in_vmem()] * (len(keeps) + 1),
        scratch_shapes=FETCH_SCRATCH,
        input_output_aliases={1 + FETCHED + i: i for i in range(len(keeps))},
        compiler_params=pltpu.CompilerParams(vmem_limit_bytes=16 * MIB),
        cost_estimate=pl.CostEstimate(
            flops=2 * ROWS * D * 7168, bytes_accessed=10_000_000, transcendentals=0
        ),
        name="second_stage",
    )(in_place(place), *left(given), *held(keeps))
    vars(state).update(zip(kept, results))
    return results[-1]


def middle_step(micro, ref):
    rows = slice(micro * ROWS, (micro + 1) * ROWS)
    whole = slice(0, ROWS)

    def write_probs(pair, value):
        ref.link_probs[pair] = value

    def write_mix(pair, value):
        ref.left_b[rows, pair * LANES : (pair + 1) * LANES] = value

    attend(
        columns(ref.query, rows, 0),
        columns(ref.link, whole, 0),
        columns(ref.link, whole, D),
        ref.across[rows, :] != 0.0,
        write_probs,
        write_mix,
    )
    after = ref.mid[rows, :] + mm(ref.left_b[rows, :], ref.w_cross[:, D:])
    ref.across_mid[rows, :] = after
    ref.narrow[rows, :] = after.astype(LOW)
    grad = ref.cotangent[rows, :].astype(F32)
    for part in range(4):
        cut = slice(part * D, (part + 1) * D)
        hidden = mm(ref.narrow[rows, :], ref.w_up[:, cut])
        ref.hidden[rows, cut] = hidden
        grad_hidden = (gelu_slope(hidden) * ref.wide[rows, cut]).astype(LOW)
        ref.grad_hidden[rows, cut] = grad_hidden
        grad = grad + mm_nt(grad_hidden, ref.w_up[:, cut])
    ref.grad[rows, :] = grad
    ref.right[rows, D:] = grad.astype(LOW)
    ref.mixed[...] = mm_nt(ref.right[rows, D:], ref.w_cross[:, D:]).astype(LOW)

    def write(pair, grad_v):
        ref.values_grad[:, pair * LANES : (pair + 1) * LANES] = grad_v.astype(LOW)

    attend_back_values(lambda pair: ref.link_probs[pair], columns(ref.mixed, whole, 0), write)


def middle_keys(micro, ref):
    rows = slice(micro * ROWS, (micro + 1) * ROWS)
    whole = slice(0, ROWS)

    def write(pair, grad_q, grad_k):
        cut = slice(pair * LANES, (pair + 1) * LANES)
        ref.right[rows, cut] = grad_q.astype(LOW)
        ref.keys_grad[:, cut] = grad_k.astype(LOW)

    attend_back_keys(
        columns(ref.query, rows, 0),
        columns(ref.link, whole, 0),
        columns(ref.link, whole, D),
        lambda pair: ref.link_probs[pair],
        columns(ref.mixed, whole, 0),
        write,
    )


def two_sides(link_grad):
    return link_grad.at[pl.ds(0, ROWS)], link_grad.at[pl.ds(ROWS, ROWS)]


LINK_STATE = dict(link_probs=((PAIRS, 2 * ROWS, ROWS), F32), mixed=((ROWS, D), LOW))
SIDE = ((ROWS, D), LOW)


def middle_stage(micro, place, token, state, link):
    reads = dict(
        query=state.query,
        across=state.across,
        mid=state.mid,
        cotangent=state.cotangent,
        w_cross=state.w_cross,
        w_up=state.w_up,
        link=link,
    )
    keeps = dict(narrow=state.narrow, wide=state.wide)
    makes, scratch = {}, ()
    if micro == 0:
        makes.update(link_grad=((2 * ROWS, D), LOW), **BACK)
        scratch = shaped(LINK_STATE)
    else:
        makes.update(values_grad=SIDE, **LINK_STATE)
        keeps.update((name, getattr(state, name)) for name in BACK)

    def kernel(place_ref, ref, *own):
        vars(ref).update(zip(LINK_STATE, own))

        @pl.when(place_ref[0] != 0)
        def _():
            if micro == 0:
                ref.keys_grad, ref.values_grad = two_sides(ref.link_grad)
            middle_step(micro, ref)
            if micro == 0:
                middle_keys(micro, ref)

        @pl.when(place_ref[0] == 0)
        def _():
            rows = slice(micro * ROWS, (micro + 1) * ROWS)
            for part in range(4):
                cut = slice(part * D, (part + 1) * D)
                ref.wide[rows, cut] = gelu_slope(ref.wide[rows, cut])

    cost = (2 * ROWS * D * 10000, 8_000_000)
    token, made = call(
        kernel, "middle_stage", place, token, reads, keeps, makes, scratch=scratch, cost=cost
    )
    vars(state).update(made)
    return token


def middle_keys_stage(micro, place, token, state, link):
    reads = dict(query=state.query, link=link, link_probs=state.link_probs, mixed=state.mixed)

    def kernel(place_ref, ref):
        @pl.when(place_ref[0] != 0)
        def _():
            middle_keys(micro, ref)

    cost = mflop(200)
    keeps, makes = dict(right=state.right), dict(keys_grad=SIDE)
    token, made = call(kernel, "middle_keys", place, token, reads, keeps, makes, cost=cost)
    vars(state).update(made)
    return token


def values_step(micro, first, ref):
    rows = slice(micro * ROWS, (micro + 1) * ROWS)

    @pl.when(first)
    def _():
        cotangent = ref.cotangent[rows, :].astype(F32)
        ref.grad[rows, :] = cotangent + mm_nt(ref.values_grad[...], ref.w_cross[:, D:])
        ref.right[rows, D:] = ref.values_grad[...]


def gate_step(micro, first, ref):
    rows = slice(micro * ROWS, (micro + 1) * ROWS)

    @pl.when(first)
    def _():
        grad = ref.grad[rows, :] + mm_nt(ref.keys_grad[...], ref.w_cross[:, :D])
        ref.grad[rows, :] = grad
        ref.gate[rows, :] = grad.astype(LOW)
        ref.right[rows, :D] = ref.keys_grad[...]
        ref.left_b[rows, :] = ref.left_a[rows, :]

    @pl.when(jnp.logical_not(first))
    def _():
        ref.gate[rows, :] = ref.cotangent[rows, :]
        for part in range(4):
            cut = slice(part * D, (part + 1) * D)
            ref.act[rows, cut] = gelu(ref.hidden[rows, cut]).astype(LOW)


def back_step(micro, first, ref):
    rows = slice(micro * ROWS, (micro + 1) * ROWS)

    @pl.when(first)
    def _():
        grad = ref.grad[rows, :]
        for part in range(4):
            cut = slice(part * D, (part + 1) * D)
            grad_act = mm_nt(ref.gate[rows, :], ref.w_down[cut, :])
            grad_hidden = (ref.wide[rows, cut] * grad_act).astype(LOW)
            ref.grad_hidden[rows, cut] = grad_hidden
            grad = grad + mm_nt(grad_hidden, ref.w_up[:, cut])
        ref.grad[rows, :] = grad
        ref.grad_low[rows, :] = grad.astype(LOW)

    @pl.when(jnp.logical_not(first))
    def _():
        grad = ref.grad[rows, :] + mm_nt(ref.right[rows, :D], ref.w_cross[:, :D])
        ref.grad[rows, :] = grad
        ref.grad_low[rows, :] = grad.astype(LOW)


def back_stage(micro, place, token, state, link_grad, parts, send=(), cost=5000):
    reads = dict(
        cotangent=state.cotangent,
        w_cross=state.w_cross,
        w_up=state.w_up,
        w_down=state.w_down,
        wide=state.wide,
        left_a=state.left_a,
        **link_grad,
        narrow=state.narrow,
        mix=state.mix,
    )
    keeps = {name: getattr(state, name) for name in BACK}
    keeps.update(act=state.act)
    makes = {}
    for at, chunk in enumerate(send):
        makes["send%d" % at] = ((chunk.rows, D), LOW)

    def kernel(place_ref, ref):
        if micro == 0:
            ref.keys_grad, ref.values_grad = two_sides(ref.link_grad)
        for part in parts:
            part(micro, place_ref[0] == 0, ref)
        for at, chunk in enumerate(send):
            put_send(place_ref, ref, chunk, getattr(ref, "send%d" % at))

    token, made = call(kernel, "back_stage", place, token, reads, keeps, makes, cost=mflop(cost))
    sends = [made.pop(name) for name in makes]
    vars(state).update(made)
    return token, sends


def late_kernel(place_ref, ref, mixed_v):
    mixed_v[...] = mm_nt(ref.grad_low[...], ref.w_out[...]).astype(LOW)
    for micro in range(MB):
        rows = slice(micro * ROWS, (micro + 1) * ROWS)

        def write(pair, *grads, rows=rows, first=0):
            for part, value in enumerate(grads):
                at = (first + part) * D + pair * LANES
                rounded, rest = in_two(value)
                ref.grad_proj[rows, at : at + LANES] = rounded
                ref.grad_rest[rows, at : at + LANES] = rest

        def read_probs(pair, micro=micro):
            return ref.probs[micro, pair]

        attend_back_keys(
            columns(ref.proj, rows, 0),
            columns(ref.proj, rows, D),
            columns(ref.proj, rows, 2 * D),
            read_probs,
            columns(mixed_v, rows, 0),
            write,
        )
        attend_back_values(
            read_probs,
            columns(mixed_v, rows, 0),
            lambda pair, value, write=write: write(pair, value, first=2),
        )
    for here, gradient, run in QKV.each():
        value = product_of(gradient, ref, run, 1 - place_ref[1])
        ref.send[here, :], ref.more[here, :] = in_two(value)


def late_stage(place, token, state, cost):
    reads = dict(
        grad_low=state.grad_low,
        w_out=state.w_out,
        proj=state.proj,
        probs=state.probs,
        tokens=state.tokens,
        mix=state.mix,
    )
    wide, side = ((BOTH, 3 * D), LOW), ((QKV.rows, D), LOW)
    makes = dict(grad_proj=wide, grad_rest=wide, send=side, more=side)
    scratch = (pltpu.VMEM((BOTH, D), LOW),)
    token, made = call(
        late_kernel, "late_stage", place, token, reads, {}, makes, None, scratch, mflop(cost)
    )
    sends = made.pop("send"), made.pop("more")
    vars(state).update(made)
    return token, sends


def final_kernel(place_ref, ref, result_v, grad_v, sems):
    @pl.when(place_ref[0] == 0)
    def _():
        result_v[...] = ref.result[...]

    @pl.when(place_ref[0] != 0)
    def _():
        total = ref.across_mid[...]
        for part in range(4):
            cut = slice(part * D, (part + 1) * D)
            total = total + mm(ref.act[:, cut], ref.w_down[cut, :])
        result_v[...] = total.astype(LOW)

    first = fetch(result_v, ref.outputs.at[0], sems.at[0])
    grad_v[...] = (ref.grad[...] + mm_nt(ref.grad_proj[...], ref.w_qkv[...])).astype(LOW)
    second = fetch(grad_v, ref.input_grad.at[0], sems.at[1])
    first.wait()
    second.wait()


def final_stage(place, token, state, cost):
    reads = dict(
        grad=state.grad,
        grad_proj=state.grad_proj,
        w_qkv=state.w_qkv,
        result=state.result,
        across_mid=state.across_mid,
        act=state.act,
        w_down=state.w_down,
    )
    half = ((1, BOTH, D), LOW)
    stores = dict(outputs=half, input_grad=half)
    scratch = [pltpu.VMEM((BOTH, D), LOW)] * 2 + [pltpu.SemaphoreType.DMA((2,))]
    return call(
        final_kernel, "final_stage", place, token, reads, {}, {}, stores, scratch, mflop(cost)
    )


PIECE = HALF // 2
PIECES = 7

Y_FIRST = (1, 2, 3)
Z_FIRST = (2, 1, 3)


def cut_of(part):
    return slice(part * D, (part + 1) * D)


class Gradient:
    def __init__(self, sides, store, down=False):
        self.sides = sides
        self.store = store
        self.down = down

    def rows(self, part, half, first, count):
        start = (part * D if self.down else 0) + first * PIECE
        return pl.ds(pl.multiple_of(start + half * HALF, PIECE), count * PIECE)

    def product(self, ref, part, half, first, count):
        left_ref, right_ref, column, *rest = self.sides(ref, part)
        value = left_ref[:, self.rows(part, half, first, count)]
        total = mm_tn(value, right_ref[:, cut_of(column)])
        for rest_ref in rest:
            total = total + mm_tn(value, rest_ref[:, cut_of(column)])
        return total

    def target(self, array, part, half, first, count):
        column = 0 if self.down else part * D
        return array.at[0, self.rows(part, half, first, count), pl.ds(column, D)]


G_DOWN = Gradient(lambda ref, part: (ref.act, ref.gate, 0), dict(g_down=((1, FF, D), F32)), down=True)
G_UP = Gradient(lambda ref, part: (ref.narrow, ref.grad_hidden, part), dict(g_up=((1, D, FF), F32)))
G_CROSS = Gradient(
    lambda ref, part: ((ref.left_a, ref.left_b)[part], ref.right, part),
    dict(g_cross=((1, D, 2 * D), F32)),
)
G_OUT = Gradient(lambda ref, part: (ref.mix, ref.grad_low, 0), dict(g_out=((1, D, D), F32)))
G_QKV = Gradient(
    lambda ref, part: (ref.tokens, ref.grad_proj, part, ref.grad_rest),
    dict(g_qkv=((1, D, 3 * D), F32)),
)


class Chunk:
    def __init__(self, levels, operands, runs, fine=False):
        self.levels = levels
        self.fine = fine
        self.operands = operands
        self.runs = runs
        self.rows = PIECES * PIECE
        self.stores = {}
        for run in runs:
            self.stores.update(run[0].store)

    def each(self):
        at = 0
        for gradient, part, first, count in self.runs:
            yield slice(at, at + count * PIECE), gradient, (part, first, count)
            at += count * PIECE


def product_of(gradient, ref, run, half):
    part, first, count = run
    return gradient.product(ref, part, half, first, count)


CROSS = Chunk(
    (Y_FIRST, Z_FIRST),
    lambda state: dict(
        left_a=state.left_a,
        left_b=state.left_b,
        right=state.right,
        mix=state.mix,
        grad_low=state.grad_low,
        act=state.act,
        gate=state.gate,
        narrow=state.narrow,
        grad_hidden=state.grad_hidden,
    ),
    [(G_CROSS, 0, 0, 2), (G_CROSS, 1, 0, 2), (G_OUT, 0, 0, 1), (G_DOWN, 3, 1, 1), (G_UP, 3, 1, 1)],
)
DOWN = Chunk(
    (Y_FIRST, Z_FIRST),
    lambda state: dict(act=state.act, gate=state.gate),
    [(G_DOWN, 0, 0, 2), (G_DOWN, 1, 0, 2), (G_DOWN, 2, 0, 2), (G_DOWN, 3, 0, 1)],
)
UP = Chunk(
    (Y_FIRST, Z_FIRST),
    lambda state: dict(narrow=state.narrow, grad_hidden=state.grad_hidden),
    [(G_UP, 0, 0, 2), (G_UP, 1, 0, 2), (G_UP, 2, 0, 2), (G_UP, 3, 0, 1)],
)
QKV = Chunk(
    (Z_FIRST, Y_FIRST),
    lambda state: dict(
        tokens=state.tokens,
        grad_proj=state.grad_proj,
        grad_rest=state.grad_rest,
        mix=state.mix,
        grad_low=state.grad_low,
    ),
    [(G_QKV, 0, 0, 2), (G_QKV, 1, 0, 2), (G_QKV, 2, 0, 2), (G_OUT, 0, 1, 1)],
    fine=True,
)


def put_send(place_ref, ref, chunk, send):
    for here, gradient, run in chunk.each():
        send[here, :] = product_of(gradient, ref, run, 1 - place_ref[1]).astype(LOW)


class Summing:
    def __init__(self, chunk, state, place, count):
        self.chunk = chunk
        self.state = state
        self.place = place
        self.count = count
        self.depth = count.bit_length() - 2
        self.step = 0

    def swap(self, value, level):
        def partner(i):
            bit = self.chunk.levels[i % 2][level - 1] if 0 < level < 4 else level
            return i ^ (1 << bit)

        return lax.ppermute(value, "dp", [(i, partner(i)) for i in range(self.count)])

    def call(self, kernel, token, reads, makes, stores=None, scratch=(), patches=None):
        name = "sum_%d" % self.step
        rest = (stores, scratch, mflop(self.cost), patches)
        return call(kernel, name, self.place, token, reads, {}, makes, *rest)

    def halves(self, place_ref, level, rows):
        first, second = (place_ref[1 + levels[level - 1]] for levels in self.chunk.levels)
        bit = jnp.where(place_ref[1] == 0, first, second)
        half = rows // 2
        own = pl.ds(pl.multiple_of(bit * half, half), half)
        return own, pl.ds(pl.multiple_of((1 - bit) * half, half), half)

    def launch(self, send, *more):
        self.got = self.swap(send, 0)
        self.more = dict(more=self.swap(*more, 0)) if more else {}

    def start(self, token, cost):
        def kernel(place_ref, ref):
            put_send(place_ref, ref, self.chunk, ref.send)

        makes = dict(send=((self.chunk.rows, D), LOW))
        reads = self.chunk.operands(self.state)
        token, made = call(kernel, "product", self.place, token, reads, {}, makes, cost=mflop(cost))
        self.launch(made["send"])
        return token

    def advance(self, token, grads, cost):
        self.cost = cost
        rows = self.chunk.rows
        if self.step == 0:
            token = self.split_first(token, rows)
        elif self.step == 1:
            token = self.split(token, rows // 2)
        elif self.step == 2:
            token = self.round_off(token, rows // 4)
        elif self.step == 3:
            for level in range(4, self.depth + 1):
                token = self.pair_sum(token, rows // 4, level, False)
            token = self.pair_sum(token, rows // 4, 2, True)
        elif self.step == 4:
            token = self.merge(token, rows // 4, 1)
        elif self.step == 5:
            token = self.merge(token, rows // 2, 0)
        else:
            token = self.unpack(token, grads, False, cost)
        self.step += 1
        return token

    def split_first(self, token, rows):
        chunk = self.chunk

        def kernel(place_ref, ref, total):
            for here, gradient, run in chunk.each():
                own = product_of(gradient, ref, run, place_ref[1])
                total[here, :] = own + ref.got[here, :].astype(F32)
                if chunk.fine:
                    total[here, :] = total[here, :] + ref.more[here, :].astype(F32)
            own, other = self.halves(place_ref, 1, rows)
            if chunk.fine:
                ref.send[...], ref.more_out[...] = in_two(total[other, :])
            else:
                ref.send[...] = total[other, :].astype(LOW)
            ref.keep[...] = total[own, :]

        reads = dict(got=self.got, **self.more, **chunk.operands(self.state))
        side = ((rows // 2, D), LOW)
        makes = dict(send=side, keep=((rows // 2, D), F32))
        if chunk.fine:
            makes.update(more_out=side)
        scratch = (pltpu.VMEM((rows, D), F32),)
        token, made = self.call(kernel, token, reads, makes, scratch=scratch)
        self.keep = made["keep"]
        self.send_on(made, 1)
        return token

    def send_on(self, made, level):
        self.got = self.swap(made["send"], level)
        self.more = {}
        if self.chunk.fine:
            self.more = dict(more=self.swap(made["more_out"], level))

    def split(self, token, rows):
        fine = self.chunk.fine

        def kernel(place_ref, ref):
            own, other = self.halves(place_ref, 2, rows)

            def total(part):
                value = ref.keep[part, :] + ref.got[part, :].astype(F32)
                return value + ref.more[part, :].astype(F32) if fine else value

            if fine:
                ref.send[...], ref.more_out[...] = in_two(total(other))
            else:
                ref.send[...] = total(other).astype(LOW)
            ref.kept[...] = total(own)

        side = ((rows // 2, D), LOW)
        makes = dict(send=side, kept=((rows // 2, D), F32))
        if fine:
            makes.update(more_out=side)
        reads = dict(keep=self.keep, got=self.got, **self.more)
        token, made = self.call(kernel, token, reads, makes)
        self.keep = made["kept"]
        self.send_on(made, 2)
        return token

    def round_off(self, token, rows):
        fine = self.chunk.fine

        def kernel(place_ref, ref):
            total = ref.keep[...] + ref.got[...].astype(F32)
            if fine:
                total = total + ref.more[...].astype(F32)
                ref.piece[...], ref.rest[...] = in_two(total)
            else:
                ref.piece[...] = total.astype(LOW)

        side = ((rows, D), LOW)
        makes = dict(piece=side, rest=side) if fine else dict(piece=side)
        reads = dict(keep=self.keep, got=self.got, **self.more)
        token, made = self.call(kernel, token, reads, makes)
        self.spread(made, 3)
        return token

    def spread(self, made, level):
        self.piece = made["piece"]
        self.got = self.swap(self.piece, level)
        self.more = {}
        if "rest" in made:
            self.more = dict(rest=made["rest"], more=self.swap(made["rest"], level))

    def pair_sum(self, token, rows, level, last):
        fine = self.chunk.fine

        def kernel(place_ref, ref):
            own, other = ref.held[...].astype(F32), ref.got[...].astype(F32)
            if fine:
                own, other = own + ref.rest[...].astype(F32), other + ref.more[...].astype(F32)
            if fine and not last:
                ref.piece[...], ref.rest_out[...] = in_two(own + other)
            else:
                ref.piece[...] = (own + other).astype(LOW)

        side = ((rows, D), LOW)
        makes = dict(piece=side, rest_out=side) if fine and not last else dict(piece=side)
        reads = dict(held=self.piece, got=self.got, **self.more)
        token, made = self.call(kernel, token, reads, makes)
        if "rest_out" in made:
            made["rest"] = made.pop("rest_out")
        self.spread(made, level)
        return token

    def merge(self, token, rows, level):
        def kernel(place_ref, ref):
            own, other = self.halves(place_ref, level + 1, 2 * rows)
            ref.piece[own, :] = ref.held[...]
            ref.piece[other, :] = ref.got[...]

        makes = dict(piece=((2 * rows, D), LOW))
        token, made = self.call(kernel, token, dict(held=self.piece, got=self.got), makes)
        self.piece = made["piece"]
        self.got = self.swap(self.piece, level)
        return token

    def unpack(self, token, grads, own, cost):
        chunk = self.chunk
        patches = {name: grads[name] for name in chunk.stores if name in grads}
        stores = {name: kind for name, kind in chunk.stores.items() if name not in grads}

        def kernel(place_ref, ref, wide, sems):
            half = place_ref[1] if own else 1 - place_ref[1]
            copies = []
            for index, (here, gradient, (part, first, count)) in enumerate(chunk.each()):
                wide[here, :] = ref.source[here, :].astype(F32)
                array = getattr(ref, list(gradient.store)[0])
                target = gradient.target(array, part, half, first, count)
                rows = pl.ds(here.start, here.stop - here.start)
                copies.append(fetch(wide.at[rows], target, sems.at[index]))
            for copy in copies:
                copy.wait()

        scratch = (pltpu.VMEM((chunk.rows, D), F32), pltpu.SemaphoreType.DMA((len(chunk.runs),)))
        reads = dict(source=self.piece if own else self.got)
        name = "unpack_%d" % own
        token, made = call(
            kernel, name, self.place, token, reads, {}, {}, stores, scratch, mflop(cost), patches
        )
        grads.update(made)
        return token


CHUNKS = (DOWN, CROSS, UP, QKV)
GATE, BACK_ATTN, BACK_FFN, FINAL, MORE, OWN = 10, 11, 12, 13, 14, 20
ORDER = (10, 12, 0, 14, 1, 11, 0, 2, 1, 3, 0, 2, 1, 3, 0, 13, 2, 1, 3, 0, 2, 1, 3, 0, 2, 20, 1, 21, 3, 0, 2, 1, 22, 3, 2, 23, 3)
COSTS = (1000, 1000, 8000, 4000, 8000, 8000, 8000, 4000, 1000, 1000, 1000, 1000, 1000, 1000, 1000, 1000, 1000, 1000, 1000, 1000, 1000, 1000, 1000, 1000, 8000, 8000, 1000, 8000, 1000, 1000, 1000, 1000, 1000, 50, 3000, 1000, 1000)


def on_device(inputs, lengths, w_qkv, w_attn_out, w_cross, w_up, w_down, cotangent):
    count = lax.axis_size("dp")
    given = (lengths, inputs, w_qkv, w_attn_out, w_up, w_down, w_cross, cotangent)
    place, token, link, state = first_stage(given)
    links = [lax.ppermute(link, "section", [(0, 1)])]
    link = second_stage(place, state, given)
    links.append(lax.ppermute(link, "section", [(0, 1)]))

    def to_encoder(side):
        return lax.ppermute(side, "section", [(1, 0)])

    token = middle_stage(0, place, token, state, links[0])
    grads = [dict(link_grad=to_encoder(state.link_grad))]
    token = middle_stage(1, place, token, state, links[1])
    values = to_encoder(state.values_grad)
    token = middle_keys_stage(1, place, token, state, links[1])
    grads.append(dict(keys_grad=to_encoder(state.keys_grad)))
    token, _ = back_stage(0, place, token, state, grads[0], (values_step, gate_step, back_step), cost=900)
    token, _ = back_stage(1, place, token, state, dict(values_grad=values), (values_step,), cost=300)
    chunks = [Summing(chunk, state, place, count) for chunk in CHUNKS]
    made = {}
    for task, cost in zip(ORDER, COSTS):
        if task == GATE:
            token, sends = back_stage(1, place, token, state, grads[1], (gate_step,), [DOWN], cost)
            chunks[0].launch(*sends)
        elif task == BACK_FFN:
            token, sends = back_stage(1, place, token, state, grads[1], (back_step,), [CROSS], cost)
            chunks[1].launch(*sends)
        elif task == MORE:
            token = chunks[2].start(token, cost)
        elif task == BACK_ATTN:
            token, sends = late_stage(place, token, state, cost)
            chunks[3].launch(*sends)
        elif task == FINAL:
            token, ends = final_stage(place, token, state, cost)
            made.update(ends)
        elif task >= OWN:
            token = chunks[task - OWN].unpack(token, made, True, cost)
        else:
            token = chunks[task].advance(token, made, cost)
    done = SimpleNamespace(**made)
    return (
        done.outputs,
        done.input_grad,
        done.g_qkv,
        done.g_out,
        done.g_cross,
        done.g_up,
        done.g_down,
    )


def solution(mesh):
    return jax.shard_map(
        on_device,
        mesh=mesh,
        in_specs=(
            P("section", "dp", None),
            P("dp", None, None),
            P("section", None, None),
            P("section", None, None),
            P("section", None, None),
            P("section", None, None),
            P("section", None, None),
            P("section", "dp", None),
        ),
        out_specs=(
            P("section", "dp", None),
            P("section", "dp", None),
            P("section", None, None),
            P("section", None, None),
            P("section", None, None),
            P("section", None, None),
            P("section", None, None),
        ),
        check_vma=False,
    )
```

```python
from types import SimpleNamespace

import jax
import jax.numpy as jnp
from jax import lax
from jax.experimental import pallas as pl
from jax.experimental.pallas import tpu as pltpu
from jax.sharding import PartitionSpec as P

D = 512
HEADS = 8
HEAD_DIM = 64
FF = 2048
ROWS = 128
SLOTS = 16
MB = 2
BOTH = MB * ROWS
PAIRS = HEADS // 2
LANES = 2 * HEAD_DIM
HALF = D // 2
SCALE = HEAD_DIM ** (-0.5)
GELU_IN = 0.7978845608028654
GELU_CUBE = 0.044715
LOW = jnp.bfloat16
F32 = jnp.float32
MIB = 1024 * 1024
DP = "dp"
SECTION = "section"
PLACE = 4


def in_two(value):
    rounded = value.astype(LOW)
    return rounded, (value - rounded.astype(F32)).astype(LOW)


def mm(left, right):
    return jnp.dot(left, right, preferred_element_type=F32)


def mm_nt(left, right):
    return lax.dot_general(left, right, (((1,), (1,)), ((), ())), preferred_element_type=F32)


def mm_tn(left, right):
    return lax.dot_general(left, right, (((0,), (0,)), ((), ())), preferred_element_type=F32)


def gelu(hidden):
    inner = GELU_IN * (hidden + GELU_CUBE * (hidden * hidden * hidden))
    return hidden * (0.5 * (1.0 + jnp.tanh(inner)))


def gelu_slope(hidden):
    square = hidden * hidden
    inner = GELU_IN * (hidden + GELU_CUBE * (square * hidden))
    bent = jnp.tanh(inner)
    inner_slope = GELU_IN * (1.0 + (3.0 * GELU_CUBE) * square)
    return 0.5 * (1.0 + bent) + 0.5 * hidden * (1.0 - bent * bent) * inner_slope


def segments(lengths_ref, micro, which, dim):
    position = lax.broadcasted_iota(jnp.int32, (ROWS, ROWS), dim)
    end = jnp.int32(0)
    seg = jnp.zeros((ROWS, ROWS), jnp.int32)
    for slot in range(SLOTS):
        end = end + lengths_ref[micro, which, slot]
        seg = seg + (position >= end).astype(jnp.int32)
    return seg


def low_lanes():
    return lax.broadcasted_iota(jnp.int32, (ROWS, LANES), 1) < HEAD_DIM


def two_heads(pair, lanes):
    nothing = jnp.zeros_like(pair)
    return jnp.concatenate(
        [jnp.where(lanes, pair, nothing), jnp.where(lanes, nothing, pair)], axis=0
    )


def softmax(scores):
    highest = jnp.max(scores, axis=0, keepdims=True)
    raised = jnp.exp(scores - highest)
    return raised * (1.0 / jnp.sum(raised, axis=0, keepdims=True))


def two_halves(value):
    return value[:ROWS, :], value[ROWS:, :]


def attend(read_q, read_k, read_v, mask, write_probs, write_mix):
    lanes = low_lanes()
    for pair in range(PAIRS):
        query = (read_q(pair).astype(F32) * SCALE).astype(LOW)
        scores = mm_nt(two_heads(read_k(pair), lanes), query)
        heads = [softmax(jnp.where(mask, part, -1e30)) for part in two_halves(scores)]
        probs = jnp.concatenate(heads, axis=0)
        write_probs(pair, probs)
        write_mix(pair, mm_tn(probs.astype(LOW), two_heads(read_v(pair), lanes)).astype(LOW))


def attend_back_values(read_probs, read_grad, write):
    lanes = low_lanes()
    for pair in range(PAIRS):
        grad_v = mm(read_probs(pair).astype(LOW), read_grad(pair))
        write(pair, jnp.where(lanes, *two_halves(grad_v)))


def attend_back_keys(read_q, read_k, read_v, read_probs, read_grad, write):
    lanes = low_lanes()
    for pair in range(PAIRS):
        query = (read_q(pair).astype(F32) * SCALE).astype(LOW)
        probs = read_probs(pair)
        grad_probs = mm_nt(two_heads(read_v(pair), lanes), read_grad(pair))
        slopes = []
        for head, change in zip(two_halves(probs), two_halves(grad_probs)):
            total = jnp.sum(head * change, axis=0, keepdims=True)
            slopes.append((head * (change - total)).astype(LOW))
        slopes = jnp.concatenate(slopes, axis=0)
        grad_q = mm_tn(slopes, two_heads(read_k(pair), lanes)) * SCALE
        grad_k = jnp.where(lanes, *two_halves(mm(slopes, query)))
        write(pair, grad_q, grad_k)


def columns(ref, rows, start):
    def read(pair):
        return ref[rows, start + pair * LANES : start + (pair + 1) * LANES]

    return read


def fetch(source, target, sem):
    copy = pltpu.make_async_copy(source, target, sem)
    copy.start()
    return copy


WEIGHTS = dict(
    w_qkv=((D, 3 * D), LOW),
    w_out=((D, D), LOW),
    w_cross=((D, 2 * D), LOW),
    w_up=((D, FF), LOW),
    w_down=((FF, D), LOW),
)
HELD = dict(tokens=((BOTH, D), LOW), cotangent=((BOTH, D), LOW))
STATE = dict(
    proj=((BOTH, 3 * D), LOW),
    mix=((BOTH, D), LOW),
    probs=((MB, PAIRS, 2 * ROWS, ROWS), F32),
    wide=((BOTH, FF), F32),
    mid=((BOTH, D), F32),
    act=((BOTH, FF), LOW),
    narrow=((BOTH, D), LOW),
    result=((BOTH, D), LOW),
    left_a=((BOTH, D), LOW),
    query=((BOTH, D), LOW),
    across=((BOTH, ROWS), F32),
)
BACK = dict(
    hidden=((BOTH, FF), F32),
    across_mid=((BOTH, D), F32),
    left_b=((BOTH, D), LOW),
    right=((BOTH, 2 * D), LOW),
    grad_hidden=((BOTH, FF), LOW),
    gate=((BOTH, D), LOW),
    grad=((BOTH, D), F32),
    grad_low=((BOTH, D), LOW),
)


def shaped(table):
    return [pltpu.VMEM(shape, kind) for shape, kind in table.values()]


def same_shape(arrays):
    return [pltpu.VMEM(value.shape, value.dtype) for value in arrays]


def held(arrays):
    return [pltpu.with_memory_space_constraint(value, pltpu.VMEM) for value in arrays]


def in_place(place):
    return pltpu.with_memory_space_constraint(place, pltpu.SMEM)


def left(arrays):
    return [pltpu.with_memory_space_constraint(value, pltpu.HBM) for value in arrays]


def in_vmem():
    return pl.BlockSpec(memory_space=pltpu.VMEM)


def in_smem():
    return pl.BlockSpec(memory_space=pltpu.SMEM)


def in_hbm():
    return pl.BlockSpec(memory_space=pltpu.HBM)


TOKEN = ((8, LANES), F32)


def mflop(count):
    return count * 1_000_000, 0


def call(
    kernel, name, place, token, reads, keeps, makes, stores=None, scratch=(), cost=(0, 0), patches=None
):
    stores, patches = stores or {}, patches or {}
    out_shape = same_shape(keeps.values()) + shaped(makes) + shaped(dict(token=TOKEN))
    out_shape += [pltpu.HBM(shape, kind) for shape, kind in stores.values()]
    out_shape += [pltpu.HBM(value.shape, value.dtype) for value in patches.values()]
    reads_n, keeps_n, makes_n = len(reads), len(keeps), len(makes)
    stores_n, patches_n = len(stores), len(patches)
    aliases = {2 + reads_n + i: i for i in range(keeps_n)}
    for i in range(patches_n):
        aliases[2 + reads_n + keeps_n + i] = keeps_n + makes_n + 1 + stores_n + i

    def body(place_ref, token_in, *refs):
        del token_in
        refs = list(refs)
        named = dict(zip(reads, refs[:reads_n]))
        refs = refs[reads_n + keeps_n + patches_n :]
        named.update(zip(keeps, refs[:keeps_n]))
        named.update(zip(makes, refs[keeps_n : keeps_n + makes_n]))
        refs = refs[keeps_n + makes_n :]
        refs[0][...] = jnp.zeros(*TOKEN)
        named.update(zip(stores, refs[1 : 1 + stores_n]))
        refs = refs[1 + stores_n :]
        named.update(zip(patches, refs[:patches_n]))
        kernel(place_ref, SimpleNamespace(**named), *refs[patches_n:])

    results = pl.pallas_call(
        body,
        out_shape=out_shape,
        in_specs=[in_smem()] + [in_vmem()] * (1 + reads_n + keeps_n) + [in_hbm()] * patches_n,
        out_specs=[in_vmem()] * (keeps_n + makes_n + 1) + [in_hbm()] * (stores_n + patches_n),
        scratch_shapes=list(scratch),
        input_output_aliases=aliases,
        compiler_params=pltpu.CompilerParams(vmem_limit_bytes=16 * MIB),
        cost_estimate=pl.CostEstimate(flops=cost[0], bytes_accessed=cost[1], transcendentals=0),
        name=name,
    )(
        in_place(place),
        *held([token]),
        *held(reads.values()),
        *held(keeps.values()),
        *left(patches.values()),
    )
    names = list(keeps) + list(makes)
    token = results[len(names)]
    made = dict(zip(names, results))
    made.update(zip(list(stores) + list(patches), results[len(names) + 1 :]))
    return token, made


def forward_step(micro, encoder, lengths_ref, ref, link, gets):
    rows = slice(micro * ROWS, (micro + 1) * ROWS)
    gets.tokens.wait()
    tokens = ref.tokens[rows, :]
    gets.w_qkv[0].wait()
    gets.lengths.wait()
    if encoder:
        mask = segments(lengths_ref, micro, 0, 0) == segments(lengths_ref, micro, 0, 1)
    else:
        seg_tgt = segments(lengths_ref, micro, 1, 1)
        source = segments(lengths_ref, micro, 0, 0)
        ref.across[rows, :] = (source == seg_tgt).astype(F32)
        earlier = lax.broadcasted_iota(jnp.int32, (ROWS, ROWS), 0) <= lax.broadcasted_iota(
            jnp.int32, (ROWS, ROWS), 1
        )
        mask = (segments(lengths_ref, micro, 1, 0) == seg_tgt) & earlier
    for part in range(3):
        cut = slice(part * D, (part + 1) * D)
        if part:
            gets.w_qkv[part].wait()
        ref.proj[rows, cut] = mm(tokens, ref.w_qkv[:, cut]).astype(LOW)

    def write_probs(pair, value):
        ref.probs[micro, pair] = value

    def write_mix(pair, value):
        ref.mix[rows, pair * LANES : (pair + 1) * LANES] = value

    attend(
        columns(ref.proj, rows, 0),
        columns(ref.proj, rows, D),
        columns(ref.proj, rows, 2 * D),
        mask,
        write_probs,
        write_mix,
    )
    gets.w_out.wait()
    mid = tokens.astype(F32) + mm(ref.mix[rows, :], ref.w_out[...])

    if not encoder:
        ref.left_a[rows, :] = mid.astype(LOW)
        ref.mid[rows, :] = mid
        return
    ref.narrow[rows, :] = mid.astype(LOW)
    gets.w_up.wait()
    gets.w_down.wait()
    for part in range(4):
        cut = slice(part * D, (part + 1) * D)
        hidden = mm(ref.narrow[rows, :], ref.w_up[:, cut])
        ref.wide[rows, cut] = hidden
        ref.act[rows, cut] = gelu(hidden).astype(LOW)
    total = mid + mm(ref.act[rows, :], ref.w_down[...])
    ref.result[rows, :] = total.astype(LOW)
    gets.w_cross.wait()
    link[...] = mm(ref.result[rows, :], ref.w_cross[...]).astype(LOW)
    ref.left_a[rows, :] = ref.result[rows, :]


def decoder_ahead(ref, gets):
    gets.w_cross.wait()
    ref.query[...] = mm(ref.left_a[...], ref.w_cross[:, :D]).astype(LOW)
    gets.cotangent.wait()
    gets.w_down.wait()
    for part in range(4):
        cut = slice(part * D, (part + 1) * D)
        ref.wide[:, cut] = mm_nt(ref.cotangent[...], ref.w_down[cut, :])
    gets.w_up.wait()


class Fetch:
    def __init__(self, source, target, sem):
        self.copy = pltpu.make_async_copy(source, target, sem)

    def start(self):
        self.copy.start()

    def wait(self):
        self.copy.wait()


class Arrived:
    def wait(self):
        pass


def fetches(ref, sems, lengths_ref, sources):
    lengths_in, tokens_in, qkv_in, out_in, up_in, down_in, cross_in, cotangent_in = sources
    parts = [pl.ds(part * D, D) for part in range(3)]
    return SimpleNamespace(
        lengths=Fetch(lengths_in, lengths_ref, sems.at[0]),
        tokens=Fetch(tokens_in.at[0], ref.tokens, sems.at[1]),
        w_qkv=[
            Fetch(qkv_in.at[0, :, part], ref.w_qkv.at[:, part], sems.at[2 + at])
            for at, part in enumerate(parts)
        ],
        w_out=Fetch(out_in.at[0], ref.w_out, sems.at[5]),
        w_up=Fetch(up_in.at[0], ref.w_up, sems.at[6]),
        w_down=Fetch(down_in.at[0], ref.w_down, sems.at[7]),
        w_cross=Fetch(cross_in.at[0], ref.w_cross, sems.at[8]),
        cotangent=Fetch(cotangent_in.at[0], ref.cotangent, sems.at[9]),
    )


def start_all(gets):
    order = [gets.lengths, gets.tokens, *gets.w_qkv, gets.w_out, gets.w_up, gets.w_down, gets.w_cross]
    for get in order:
        get.start()


FETCHED = 8
FETCH_SCRATCH = [pltpu.SMEM((MB, 2, SLOTS), jnp.int32), pltpu.SemaphoreType.DMA((FETCHED + 2,))]


def first_stage(given):
    makes = {**WEIGHTS, **HELD, **STATE, **dict(link=((ROWS, 2 * D), LOW), token=TOKEN)}

    def body(*refs):
        place_ref, lengths_ref, sems = refs[FETCHED + len(makes) :]
        ref = SimpleNamespace(**dict(zip(makes, refs[FETCHED:])))
        index = lax.axis_index(DP).astype(jnp.int32)
        section = lax.axis_index(SECTION).astype(jnp.int32)
        place_ref[0] = section
        for bit in range(PLACE - 1):
            place_ref[1 + bit] = (index >> bit) % 2
        ref.token[...] = jnp.zeros(*TOKEN)

        @pl.when(section == 0)
        def _():
            gets = fetches(ref, sems, lengths_ref, refs[:FETCHED])
            start_all(gets)
            forward_step(0, True, lengths_ref, ref, ref.link, gets)

    results = pl.pallas_call(
        body,
        out_shape=shaped(makes) + [pltpu.SMEM((PLACE,), jnp.int32)],
        in_specs=[in_hbm()] * FETCHED,
        out_specs=[in_vmem()] * len(makes) + [in_smem()],
        scratch_shapes=FETCH_SCRATCH,
        compiler_params=pltpu.CompilerParams(vmem_limit_bytes=16 * MIB),
        cost_estimate=pl.CostEstimate(
            flops=2 * ROWS * D * 7168, bytes_accessed=10_000_000, transcendentals=0
        ),
        name="first_stage",
    )(*left(given))
    made = SimpleNamespace(**dict(zip(makes, results)))
    link, token = made.link, made.token
    del made.link, made.token
    return results[-1], token, link, made


def second_stage(place, state, given):
    kept = {**WEIGHTS, **HELD, **STATE}
    keeps = [getattr(state, name) for name in kept]

    def body(place_ref, *refs):
        sources = refs[:FETCHED]
        refs = refs[FETCHED + len(keeps) :]
        ref = SimpleNamespace(**dict(zip(kept, refs)))
        link, lengths_ref, sems = refs[len(keeps) :]
        gets = fetches(ref, sems, lengths_ref, sources)
        here = Arrived()

        @pl.when(place_ref[0] == 0)
        def _():
            gets.lengths.start()
            gets.cotangent.start()
            arrived = SimpleNamespace(
                lengths=gets.lengths,
                tokens=here,
                w_qkv=[here] * 3,
                w_out=here,
                w_up=here,
                w_down=here,
                w_cross=here,
            )
            forward_step(1, True, lengths_ref, ref, link, arrived)
            gets.cotangent.wait()

        @pl.when(place_ref[0] != 0)
        def _():
            start_all(gets)
            gets.cotangent.start()
            forward_step(0, False, lengths_ref, ref, link, gets)
            arrived = SimpleNamespace(lengths=here, tokens=here, w_qkv=[here] * 3, w_out=here)
            forward_step(1, False, lengths_ref, ref, link, arrived)
            decoder_ahead(ref, gets)

    results = pl.pallas_call(
        body,
        out_shape=same_shape(keeps) + [pltpu.VMEM((ROWS, 2 * D), LOW)],
        in_specs=[in_smem()] + [in_hbm()] * FETCHED + [in_vmem()] * len(keeps),
        out_specs=[in_vmem()] * (len(keeps) + 1),
        scratch_shapes=FETCH_SCRATCH,
        input_output_aliases={1 + FETCHED + i: i for i in range(len(keeps))},
        compiler_params=pltpu.CompilerParams(vmem_limit_bytes=16 * MIB),
        cost_estimate=pl.CostEstimate(
            flops=2 * ROWS * D * 7168, bytes_accessed=10_000_000, transcendentals=0
        ),
        name="second_stage",
    )(in_place(place), *left(given), *held(keeps))
    vars(state).update(zip(kept, results))
    return results[-1]


def middle_step(micro, ref):
    rows = slice(micro * ROWS, (micro + 1) * ROWS)
    whole = slice(0, ROWS)

    def write_probs(pair, value):
        ref.link_probs[pair] = value

    def write_mix(pair, value):
        ref.left_b[rows, pair * LANES : (pair + 1) * LANES] = value

    attend(
        columns(ref.query, rows, 0),
        columns(ref.link, whole, 0),
        columns(ref.link, whole, D),
        ref.across[rows, :] != 0.0,
        write_probs,
        write_mix,
    )
    after = ref.mid[rows, :] + mm(ref.left_b[rows, :], ref.w_cross[:, D:])
    ref.across_mid[rows, :] = after
    ref.narrow[rows, :] = after.astype(LOW)
    grad = ref.cotangent[rows, :].astype(F32)
    for part in range(4):
        cut = slice(part * D, (part + 1) * D)
        hidden = mm(ref.narrow[rows, :], ref.w_up[:, cut])
        ref.hidden[rows, cut] = hidden
        grad_hidden = (gelu_slope(hidden) * ref.wide[rows, cut]).astype(LOW)
        ref.grad_hidden[rows, cut] = grad_hidden
        grad = grad + mm_nt(grad_hidden, ref.w_up[:, cut])
    ref.grad[rows, :] = grad
    ref.right[rows, D:] = grad.astype(LOW)
    ref.mixed[...] = mm_nt(ref.right[rows, D:], ref.w_cross[:, D:]).astype(LOW)

    def write(pair, grad_v):
        ref.values_grad[:, pair * LANES : (pair + 1) * LANES] = grad_v.astype(LOW)

    attend_back_values(lambda pair: ref.link_probs[pair], columns(ref.mixed, whole, 0), write)


def middle_keys(micro, ref):
    rows = slice(micro * ROWS, (micro + 1) * ROWS)
    whole = slice(0, ROWS)

    def write(pair, grad_q, grad_k):
        cut = slice(pair * LANES, (pair + 1) * LANES)
        ref.right[rows, cut] = grad_q.astype(LOW)
        ref.keys_grad[:, cut] = grad_k.astype(LOW)

    attend_back_keys(
        columns(ref.query, rows, 0),
        columns(ref.link, whole, 0),
        columns(ref.link, whole, D),
        lambda pair: ref.link_probs[pair],
        columns(ref.mixed, whole, 0),
        write,
    )


def two_sides(link_grad):
    return link_grad.at[pl.ds(0, ROWS)], link_grad.at[pl.ds(ROWS, ROWS)]


LINK_STATE = dict(link_probs=((PAIRS, 2 * ROWS, ROWS), F32), mixed=((ROWS, D), LOW))
SIDE = ((ROWS, D), LOW)


def middle_stage(micro, place, token, state, link):
    reads = dict(
        query=state.query,
        across=state.across,
        mid=state.mid,
        cotangent=state.cotangent,
        w_cross=state.w_cross,
        w_up=state.w_up,
        link=link,
    )
    keeps = dict(narrow=state.narrow, wide=state.wide)
    makes, scratch = {}, ()
    if micro == 0:
        makes.update(link_grad=((2 * ROWS, D), LOW), **BACK)
        scratch = shaped(LINK_STATE)
    else:
        makes.update(values_grad=SIDE, **LINK_STATE)
        keeps.update((name, getattr(state, name)) for name in BACK)

    def kernel(place_ref, ref, *own):
        vars(ref).update(zip(LINK_STATE, own))

        @pl.when(place_ref[0] != 0)
        def _():
            if micro == 0:
                ref.keys_grad, ref.values_grad = two_sides(ref.link_grad)
            middle_step(micro, ref)
            if micro == 0:
                middle_keys(micro, ref)

        @pl.when(place_ref[0] == 0)
        def _():
            rows = slice(micro * ROWS, (micro + 1) * ROWS)
            for part in range(4):
                cut = slice(part * D, (part + 1) * D)
                ref.wide[rows, cut] = gelu_slope(ref.wide[rows, cut])

    cost = (2 * ROWS * D * 10000, 8_000_000)
    token, made = call(
        kernel, "middle_stage", place, token, reads, keeps, makes, scratch=scratch, cost=cost
    )
    vars(state).update(made)
    return token


def middle_keys_stage(micro, place, token, state, link):
    reads = dict(query=state.query, link=link, link_probs=state.link_probs, mixed=state.mixed)

    def kernel(place_ref, ref):
        @pl.when(place_ref[0] != 0)
        def _():
            middle_keys(micro, ref)

    cost = mflop(200)
    keeps, makes = dict(right=state.right), dict(keys_grad=SIDE)
    token, made = call(kernel, "middle_keys", place, token, reads, keeps, makes, cost=cost)
    vars(state).update(made)
    return token


def values_step(micro, first, ref):
    rows = slice(micro * ROWS, (micro + 1) * ROWS)

    @pl.when(first)
    def _():
        cotangent = ref.cotangent[rows, :].astype(F32)
        ref.grad[rows, :] = cotangent + mm_nt(ref.values_grad[...], ref.w_cross[:, D:])
        ref.right[rows, D:] = ref.values_grad[...]


def gate_step(micro, first, ref):
    rows = slice(micro * ROWS, (micro + 1) * ROWS)

    @pl.when(first)
    def _():
        grad = ref.grad[rows, :] + mm_nt(ref.keys_grad[...], ref.w_cross[:, :D])
        ref.grad[rows, :] = grad
        ref.gate[rows, :] = grad.astype(LOW)
        ref.right[rows, :D] = ref.keys_grad[...]
        ref.left_b[rows, :] = ref.left_a[rows, :]

    @pl.when(jnp.logical_not(first))
    def _():
        ref.gate[rows, :] = ref.cotangent[rows, :]
        for part in range(4):
            cut = slice(part * D, (part + 1) * D)
            ref.act[rows, cut] = gelu(ref.hidden[rows, cut]).astype(LOW)


def back_step(micro, first, ref):
    rows = slice(micro * ROWS, (micro + 1) * ROWS)

    @pl.when(first)
    def _():
        grad = ref.grad[rows, :]
        for part in range(4):
            cut = slice(part * D, (part + 1) * D)
            grad_act = mm_nt(ref.gate[rows, :], ref.w_down[cut, :])
            grad_hidden = (ref.wide[rows, cut] * grad_act).astype(LOW)
            ref.grad_hidden[rows, cut] = grad_hidden
            grad = grad + mm_nt(grad_hidden, ref.w_up[:, cut])
        ref.grad[rows, :] = grad
        ref.grad_low[rows, :] = grad.astype(LOW)

    @pl.when(jnp.logical_not(first))
    def _():
        grad = ref.grad[rows, :] + mm_nt(ref.right[rows, :D], ref.w_cross[:, :D])
        ref.grad[rows, :] = grad
        ref.grad_low[rows, :] = grad.astype(LOW)


def back_stage(micro, place, token, state, link_grad, parts, send=(), cost=5000):
    reads = dict(
        cotangent=state.cotangent,
        w_cross=state.w_cross,
        w_up=state.w_up,
        w_down=state.w_down,
        wide=state.wide,
        left_a=state.left_a,
        **link_grad,
        narrow=state.narrow,
        mix=state.mix,
    )
    keeps = {name: getattr(state, name) for name in BACK}
    keeps.update(act=state.act)
    makes = {}
    for at, chunk in enumerate(send):
        makes["send%d" % at] = ((chunk.rows, D), LOW)

    def kernel(place_ref, ref):
        if micro == 0:
            ref.keys_grad, ref.values_grad = two_sides(ref.link_grad)
        for part in parts:
            part(micro, place_ref[0] == 0, ref)
        for at, chunk in enumerate(send):
            put_send(place_ref, ref, chunk, getattr(ref, "send%d" % at))

    token, made = call(kernel, "back_stage", place, token, reads, keeps, makes, cost=mflop(cost))
    sends = [made.pop(name) for name in makes]
    vars(state).update(made)
    return token, sends


def late_kernel(place_ref, ref, mixed_v):
    mixed_v[...] = mm_nt(ref.grad_low[...], ref.w_out[...]).astype(LOW)
    for micro in range(MB):
        rows = slice(micro * ROWS, (micro + 1) * ROWS)

        def write(pair, *grads, rows=rows, first=0):
            for part, value in enumerate(grads):
                at = (first + part) * D + pair * LANES
                rounded, rest = in_two(value)
                ref.grad_proj[rows, at : at + LANES] = rounded
                ref.grad_rest[rows, at : at + LANES] = rest

        def read_probs(pair, micro=micro):
            return ref.probs[micro, pair]

        attend_back_keys(
            columns(ref.proj, rows, 0),
            columns(ref.proj, rows, D),
            columns(ref.proj, rows, 2 * D),
            read_probs,
            columns(mixed_v, rows, 0),
            write,
        )
        attend_back_values(
            read_probs,
            columns(mixed_v, rows, 0),
            lambda pair, value, write=write: write(pair, value, first=2),
        )
    for here, gradient, run in QKV.each():
        value = product_of(gradient, ref, run, 1 - place_ref[1])
        ref.send[here, :], ref.more[here, :] = in_two(value)


def late_stage(place, token, state, cost):
    reads = dict(
        grad_low=state.grad_low,
        w_out=state.w_out,
        proj=state.proj,
        probs=state.probs,
        tokens=state.tokens,
        mix=state.mix,
    )
    wide, side = ((BOTH, 3 * D), LOW), ((QKV.rows, D), LOW)
    makes = dict(grad_proj=wide, grad_rest=wide, send=side, more=side)
    scratch = (pltpu.VMEM((BOTH, D), LOW),)
    token, made = call(
        late_kernel, "late_stage", place, token, reads, {}, makes, None, scratch, mflop(cost)
    )
    sends = made.pop("send"), made.pop("more")
    vars(state).update(made)
    return token, sends


def final_kernel(place_ref, ref, result_v, grad_v, sems):
    @pl.when(place_ref[0] == 0)
    def _():
        result_v[...] = ref.result[...]

    @pl.when(place_ref[0] != 0)
    def _():
        total = ref.across_mid[...]
        for part in range(4):
            cut = slice(part * D, (part + 1) * D)
            total = total + mm(ref.act[:, cut], ref.w_down[cut, :])
        result_v[...] = total.astype(LOW)

    first = fetch(result_v, ref.outputs.at[0], sems.at[0])
    grad_v[...] = (ref.grad[...] + mm_nt(ref.grad_proj[...], ref.w_qkv[...])).astype(LOW)
    second = fetch(grad_v, ref.input_grad.at[0], sems.at[1])
    first.wait()
    second.wait()


def final_stage(place, token, state, cost):
    reads = dict(
        grad=state.grad,
        grad_proj=state.grad_proj,
        w_qkv=state.w_qkv,
        result=state.result,
        across_mid=state.across_mid,
        act=state.act,
        w_down=state.w_down,
    )
    half = ((1, BOTH, D), LOW)
    stores = dict(outputs=half, input_grad=half)
    scratch = [pltpu.VMEM((BOTH, D), LOW)] * 2 + [pltpu.SemaphoreType.DMA((2,))]
    return call(
        final_kernel, "final_stage", place, token, reads, {}, {}, stores, scratch, mflop(cost)
    )


PIECE = HALF // 2
PIECES = 7

Y_FIRST = (1, 2, 3)
Z_FIRST = (2, 1, 3)


def cut_of(part):
    return slice(part * D, (part + 1) * D)


class Gradient:
    def __init__(self, sides, store, down=False):
        self.sides = sides
        self.store = store
        self.down = down

    def rows(self, part, half, first, count):
        start = (part * D if self.down else 0) + first * PIECE
        return pl.ds(pl.multiple_of(start + half * HALF, PIECE), count * PIECE)

    def product(self, ref, part, half, first, count):
        left_ref, right_ref, column, *rest = self.sides(ref, part)
        value = left_ref[:, self.rows(part, half, first, count)]
        total = mm_tn(value, right_ref[:, cut_of(column)])
        for rest_ref in rest:
            total = total + mm_tn(value, rest_ref[:, cut_of(column)])
        return total

    def target(self, array, part, half, first, count):
        column = 0 if self.down else part * D
        return array.at[0, self.rows(part, half, first, count), pl.ds(column, D)]


G_DOWN = Gradient(lambda ref, part: (ref.act, ref.gate, 0), dict(g_down=((1, FF, D), F32)), down=True)
G_UP = Gradient(lambda ref, part: (ref.narrow, ref.grad_hidden, part), dict(g_up=((1, D, FF), F32)))
G_CROSS = Gradient(
    lambda ref, part: ((ref.left_a, ref.left_b)[part], ref.right, part),
    dict(g_cross=((1, D, 2 * D), F32)),
)
G_OUT = Gradient(lambda ref, part: (ref.mix, ref.grad_low, 0), dict(g_out=((1, D, D), F32)))
G_QKV = Gradient(
    lambda ref, part: (ref.tokens, ref.grad_proj, part, ref.grad_rest),
    dict(g_qkv=((1, D, 3 * D), F32)),
)


class Chunk:
    def __init__(self, levels, operands, runs, fine=False):
        self.levels = levels
        self.fine = fine
        self.operands = operands
        self.runs = runs
        self.rows = PIECES * PIECE
        self.stores = {}
        for run in runs:
            self.stores.update(run[0].store)

    def each(self):
        at = 0
        for gradient, part, first, count in self.runs:
            yield slice(at, at + count * PIECE), gradient, (part, first, count)
            at += count * PIECE


def product_of(gradient, ref, run, half):
    part, first, count = run
    return gradient.product(ref, part, half, first, count)


CROSS = Chunk(
    (Y_FIRST, Z_FIRST),
    lambda state: dict(
        left_a=state.left_a,
        left_b=state.left_b,
        right=state.right,
        mix=state.mix,
        grad_low=state.grad_low,
        act=state.act,
        gate=state.gate,
        narrow=state.narrow,
        grad_hidden=state.grad_hidden,
    ),
    [(G_CROSS, 0, 0, 2), (G_CROSS, 1, 0, 2), (G_OUT, 0, 0, 1), (G_DOWN, 3, 1, 1), (G_UP, 3, 1, 1)],
)
DOWN = Chunk(
    (Y_FIRST, Z_FIRST),
    lambda state: dict(act=state.act, gate=state.gate),
    [(G_DOWN, 0, 0, 2), (G_DOWN, 1, 0, 2), (G_DOWN, 2, 0, 2), (G_DOWN, 3, 0, 1)],
)
UP = Chunk(
    (Y_FIRST, Z_FIRST),
    lambda state: dict(narrow=state.narrow, grad_hidden=state.grad_hidden),
    [(G_UP, 0, 0, 2), (G_UP, 1, 0, 2), (G_UP, 2, 0, 2), (G_UP, 3, 0, 1)],
)
QKV = Chunk(
    (Z_FIRST, Y_FIRST),
    lambda state: dict(
        tokens=state.tokens,
        grad_proj=state.grad_proj,
        grad_rest=state.grad_rest,
        mix=state.mix,
        grad_low=state.grad_low,
    ),
    [(G_QKV, 0, 0, 2), (G_QKV, 1, 0, 2), (G_QKV, 2, 0, 2), (G_OUT, 0, 1, 1)],
    fine=True,
)


def put_send(place_ref, ref, chunk, send):
    for here, gradient, run in chunk.each():
        send[here, :] = product_of(gradient, ref, run, 1 - place_ref[1]).astype(LOW)


class Summing:
    def __init__(self, chunk, state, place, count):
        self.chunk = chunk
        self.state = state
        self.place = place
        self.count = count
        self.depth = count.bit_length() - 2
        self.step = 0

    def swap(self, value, level):
        def partner(i):
            bit = self.chunk.levels[i % 2][level - 1] if 0 < level < 4 else level
            return i ^ (1 << bit)

        return lax.ppermute(value, "dp", [(i, partner(i)) for i in range(self.count)])

    def call(self, kernel, token, reads, makes, stores=None, scratch=(), patches=None):
        name = "sum_%d" % self.step
        rest = (stores, scratch, mflop(self.cost), patches)
        return call(kernel, name, self.place, token, reads, {}, makes, *rest)

    def halves(self, place_ref, level, rows):
        first, second = (place_ref[1 + levels[level - 1]] for levels in self.chunk.levels)
        bit = jnp.where(place_ref[1] == 0, first, second)
        half = rows // 2
        own = pl.ds(pl.multiple_of(bit * half, half), half)
        return own, pl.ds(pl.multiple_of((1 - bit) * half, half), half)

    def launch(self, send, *more):
        self.got = self.swap(send, 0)
        self.more = dict(more=self.swap(*more, 0)) if more else {}

    def start(self, token, cost):
        def kernel(place_ref, ref):
            put_send(place_ref, ref, self.chunk, ref.send)

        makes = dict(send=((self.chunk.rows, D), LOW))
        reads = self.chunk.operands(self.state)
        token, made = call(kernel, "product", self.place, token, reads, {}, makes, cost=mflop(cost))
        self.launch(made["send"])
        return token

    def advance(self, token, grads, cost):
        self.cost = cost
        rows = self.chunk.rows
        if self.step == 0:
            token = self.split_first(token, rows)
        elif self.step == 1:
            token = self.split(token, rows // 2)
        elif self.step == 2:
            token = self.round_off(token, rows // 4)
        elif self.step == 3:
            for level in range(4, self.depth + 1):
                token = self.pair_sum(token, rows // 4, level, False)
            token = self.pair_sum(token, rows // 4, 2, True)
        elif self.step == 4:
            token = self.merge(token, rows // 4, 1)
        elif self.step == 5:
            token = self.merge(token, rows // 2, 0)
        else:
            token = self.unpack(token, grads, False, cost)
        self.step += 1
        return token

    def split_first(self, token, rows):
        chunk = self.chunk

        def kernel(place_ref, ref, total):
            for here, gradient, run in chunk.each():
                own = product_of(gradient, ref, run, place_ref[1])
                total[here, :] = own + ref.got[here, :].astype(F32)
                if chunk.fine:
                    total[here, :] = total[here, :] + ref.more[here, :].astype(F32)
            own, other = self.halves(place_ref, 1, rows)
            ref.send[...] = total[other, :].astype(LOW)
            ref.keep[...] = total[own, :]

        reads = dict(got=self.got, **self.more, **chunk.operands(self.state))
        makes = dict(send=((rows // 2, D), LOW), keep=((rows // 2, D), F32))
        scratch = (pltpu.VMEM((rows, D), F32),)
        token, made = self.call(kernel, token, reads, makes, scratch=scratch)
        self.keep = made["keep"]
        self.got = self.swap(made["send"], 1)
        return token

    def split(self, token, rows):
        def kernel(place_ref, ref):
            own, other = self.halves(place_ref, 2, rows)
            ref.send[...] = (ref.keep[other, :] + ref.got[other, :].astype(F32)).astype(LOW)
            ref.kept[...] = ref.keep[own, :] + ref.got[own, :].astype(F32)

        reads = dict(keep=self.keep, got=self.got)
        makes = dict(send=((rows // 2, D), LOW), kept=((rows // 2, D), F32))
        token, made = self.call(kernel, token, reads, makes)
        self.keep = made["kept"]
        self.got = self.swap(made["send"], 2)
        return token

    def round_off(self, token, rows):
        fine = False

        def kernel(place_ref, ref):
            total = ref.keep[...] + ref.got[...].astype(F32)
            if fine:
                ref.piece[...], ref.rest[...] = in_two(total)
            else:
                ref.piece[...] = total.astype(LOW)

        side = ((rows, D), LOW)
        makes = dict(piece=side, rest=side) if fine else dict(piece=side)
        token, made = self.call(kernel, token, dict(keep=self.keep, got=self.got), makes)
        self.spread(made, 3)
        return token

    def spread(self, made, level):
        self.piece = made["piece"]
        self.got = self.swap(self.piece, level)
        self.more = {}
        if "rest" in made:
            self.more = dict(rest=made["rest"], more=self.swap(made["rest"], level))

    def pair_sum(self, token, rows, level, last):
        fine = False

        def kernel(place_ref, ref):
            own, other = ref.held[...].astype(F32), ref.got[...].astype(F32)
            if fine:
                own, other = own + ref.rest[...].astype(F32), other + ref.more[...].astype(F32)
            if fine and not last:
                ref.piece[...], ref.rest_out[...] = in_two(own + other)
            else:
                ref.piece[...] = (own + other).astype(LOW)

        side = ((rows, D), LOW)
        makes = dict(piece=side, rest_out=side) if fine and not last else dict(piece=side)
        reads = dict(held=self.piece, got=self.got, **self.more)
        token, made = self.call(kernel, token, reads, makes)
        if "rest_out" in made:
            made["rest"] = made.pop("rest_out")
        self.spread(made, level)
        return token

    def merge(self, token, rows, level):
        def kernel(place_ref, ref):
            own, other = self.halves(place_ref, level + 1, 2 * rows)
            ref.piece[own, :] = ref.held[...]
            ref.piece[other, :] = ref.got[...]

        makes = dict(piece=((2 * rows, D), LOW))
        token, made = self.call(kernel, token, dict(held=self.piece, got=self.got), makes)
        self.piece = made["piece"]
        self.got = self.swap(self.piece, level)
        return token

    def unpack(self, token, grads, own, cost):
        chunk = self.chunk
        patches = {name: grads[name] for name in chunk.stores if name in grads}
        stores = {name: kind for name, kind in chunk.stores.items() if name not in grads}

        def kernel(place_ref, ref, wide, sems):
            half = place_ref[1] if own else 1 - place_ref[1]
            copies = []
            for index, (here, gradient, (part, first, count)) in enumerate(chunk.each()):
                wide[here, :] = ref.source[here, :].astype(F32)
                array = getattr(ref, list(gradient.store)[0])
                target = gradient.target(array, part, half, first, count)
                rows = pl.ds(here.start, here.stop - here.start)
                copies.append(fetch(wide.at[rows], target, sems.at[index]))
            for copy in copies:
                copy.wait()

        scratch = (pltpu.VMEM((chunk.rows, D), F32), pltpu.SemaphoreType.DMA((len(chunk.runs),)))
        reads = dict(source=self.piece if own else self.got)
        name = "unpack_%d" % own
        token, made = call(
            kernel, name, self.place, token, reads, {}, {}, stores, scratch, mflop(cost), patches
        )
        grads.update(made)
        return token


CHUNKS = (DOWN, CROSS, UP, QKV)
GATE, BACK_ATTN, BACK_FFN, FINAL, MORE, OWN = 10, 11, 12, 13, 14, 20
ORDER = (10, 12, 0, 14, 1, 11, 2, 0, 3, 1, 0, 2, 1, 3, 0, 13, 2, 1, 3, 0, 2, 1, 3, 0, 2, 20, 1, 21, 3, 0, 2, 1, 22, 3, 2, 23, 3)
COSTS = (1000, 1000, 8000, 4000, 8000, 8000, 4000, 8000, 1000, 1000, 1000, 1000, 1000, 1000, 1000, 1000, 1000, 1000, 1000, 1000, 1000, 1000, 1000, 1000, 8000, 8000, 1000, 8000, 1000, 1000, 1000, 1000, 1000, 50, 3000, 1000, 1000)


def on_device(inputs, lengths, w_qkv, w_attn_out, w_cross, w_up, w_down, cotangent):
    count = lax.axis_size("dp")
    given = (lengths, inputs, w_qkv, w_attn_out, w_up, w_down, w_cross, cotangent)
    place, token, link, state = first_stage(given)
    links = [lax.ppermute(link, "section", [(0, 1)])]
    link = second_stage(place, state, given)
    links.append(lax.ppermute(link, "section", [(0, 1)]))

    def to_encoder(side):
        return lax.ppermute(side, "section", [(1, 0)])

    token = middle_stage(0, place, token, state, links[0])
    grads = [dict(link_grad=to_encoder(state.link_grad))]
    token = middle_stage(1, place, token, state, links[1])
    values = to_encoder(state.values_grad)
    token = middle_keys_stage(1, place, token, state, links[1])
    grads.append(dict(keys_grad=to_encoder(state.keys_grad)))
    token, _ = back_stage(0, place, token, state, grads[0], (values_step, gate_step, back_step), cost=900)
    token, _ = back_stage(1, place, token, state, dict(values_grad=values), (values_step,), cost=300)
    chunks = [Summing(chunk, state, place, count) for chunk in CHUNKS]
    made = {}
    for task, cost in zip(ORDER, COSTS):
        if task == GATE:
            token, sends = back_stage(1, place, token, state, grads[1], (gate_step,), [DOWN], cost)
            chunks[0].launch(*sends)
        elif task == BACK_FFN:
            token, sends = back_stage(1, place, token, state, grads[1], (back_step,), [CROSS], cost)
            chunks[1].launch(*sends)
        elif task == MORE:
            token = chunks[2].start(token, cost)
        elif task == BACK_ATTN:
            token, sends = late_stage(place, token, state, cost)
            chunks[3].launch(*sends)
        elif task == FINAL:
            token, ends = final_stage(place, token, state, cost)
            made.update(ends)
        elif task >= OWN:
            token = chunks[task - OWN].unpack(token, made, True, cost)
        else:
            token = chunks[task].advance(token, made, cost)
    done = SimpleNamespace(**made)
    return (
        done.outputs,
        done.input_grad,
        done.g_qkv,
        done.g_out,
        done.g_cross,
        done.g_up,
        done.g_down,
    )


def solution(mesh):
    return jax.shard_map(
        on_device,
        mesh=mesh,
        in_specs=(
            P("section", "dp", None),
            P("dp", None, None),
            P("section", None, None),
            P("section", None, None),
            P("section", None, None),
            P("section", None, None),
            P("section", None, None),
            P("section", "dp", None),
        ),
        out_specs=(
            P("section", "dp", None),
            P("section", "dp", None),
            P("section", None, None),
            P("section", None, None),
            P("section", None, None),
            P("section", None, None),
            P("section", None, None),
        ),
        check_vma=False,
    )
```

```python
from types import SimpleNamespace

import jax
import jax.numpy as jnp
from jax import lax
from jax.experimental import pallas as pl
from jax.experimental.pallas import tpu as pltpu
from jax.sharding import PartitionSpec as P

D = 512
HEADS = 8
HEAD_DIM = 64
FF = 2048
ROWS = 128
SLOTS = 16
MB = 2
BOTH = MB * ROWS
PAIRS = HEADS // 2
LANES = 2 * HEAD_DIM
HALF = D // 2
SCALE = HEAD_DIM ** (-0.5)
GELU_IN = 0.7978845608028654
GELU_CUBE = 0.044715
LOW = jnp.bfloat16
F32 = jnp.float32
MIB = 1024 * 1024
DP = "dp"
SECTION = "section"
PLACE = 4


def in_two(value):
    rounded = value.astype(LOW)
    return rounded, (value - rounded.astype(F32)).astype(LOW)


def mm(left, right):
    return jnp.dot(left, right, preferred_element_type=F32)


def mm_nt(left, right):
    return lax.dot_general(left, right, (((1,), (1,)), ((), ())), preferred_element_type=F32)


def mm_tn(left, right):
    return lax.dot_general(left, right, (((0,), (0,)), ((), ())), preferred_element_type=F32)


def gelu(hidden):
    inner = GELU_IN * (hidden + GELU_CUBE * (hidden * hidden * hidden))
    return hidden * (0.5 * (1.0 + jnp.tanh(inner)))


def gelu_slope(hidden):
    square = hidden * hidden
    inner = GELU_IN * (hidden + GELU_CUBE * (square * hidden))
    bent = jnp.tanh(inner)
    inner_slope = GELU_IN * (1.0 + (3.0 * GELU_CUBE) * square)
    return 0.5 * (1.0 + bent) + 0.5 * hidden * (1.0 - bent * bent) * inner_slope


def segments(lengths_ref, micro, which, dim):
    position = lax.broadcasted_iota(jnp.int32, (ROWS, ROWS), dim)
    end = jnp.int32(0)
    seg = jnp.zeros((ROWS, ROWS), jnp.int32)
    for slot in range(SLOTS):
        end = end + lengths_ref[micro, which, slot]
        seg = seg + (position >= end).astype(jnp.int32)
    return seg


def low_lanes():
    return lax.broadcasted_iota(jnp.int32, (ROWS, LANES), 1) < HEAD_DIM


def two_heads(pair, lanes):
    nothing = jnp.zeros_like(pair)
    return jnp.concatenate(
        [jnp.where(lanes, pair, nothing), jnp.where(lanes, nothing, pair)], axis=0
    )


def softmax(scores):
    highest = jnp.max(scores, axis=0, keepdims=True)
    raised = jnp.exp(scores - highest)
    return raised * (1.0 / jnp.sum(raised, axis=0, keepdims=True))


def two_halves(value):
    return value[:ROWS, :], value[ROWS:, :]


def attend(read_q, read_k, read_v, mask, write_probs, write_mix):
    lanes = low_lanes()
    for pair in range(PAIRS):
        query = (read_q(pair).astype(F32) * SCALE).astype(LOW)
        scores = mm_nt(two_heads(read_k(pair), lanes), query)
        heads = [softmax(jnp.where(mask, part, -1e30)) for part in two_halves(scores)]
        probs = jnp.concatenate(heads, axis=0)
        write_probs(pair, probs)
        write_mix(pair, mm_tn(probs.astype(LOW), two_heads(read_v(pair), lanes)).astype(LOW))


def attend_back_values(read_probs, read_grad, write):
    lanes = low_lanes()
    for pair in range(PAIRS):
        grad_v = mm(read_probs(pair).astype(LOW), read_grad(pair))
        write(pair, jnp.where(lanes, *two_halves(grad_v)))


def attend_back_keys(read_q, read_k, read_v, read_probs, read_grad, write):
    lanes = low_lanes()
    for pair in range(PAIRS):
        query = (read_q(pair).astype(F32) * SCALE).astype(LOW)
        probs = read_probs(pair)
        grad_probs = mm_nt(two_heads(read_v(pair), lanes), read_grad(pair))
        slopes = []
        for head, change in zip(two_halves(probs), two_halves(grad_probs)):
            total = jnp.sum(head * change, axis=0, keepdims=True)
            slopes.append((head * (change - total)).astype(LOW))
        slopes = jnp.concatenate(slopes, axis=0)
        grad_q = mm_tn(slopes, two_heads(read_k(pair), lanes)) * SCALE
        grad_k = jnp.where(lanes, *two_halves(mm(slopes, query)))
        write(pair, grad_q, grad_k)


def columns(ref, rows, start):
    def read(pair):
        return ref[rows, start + pair * LANES : start + (pair + 1) * LANES]

    return read


def fetch(source, target, sem):
    copy = pltpu.make_async_copy(source, target, sem)
    copy.start()
    return copy


WEIGHTS = dict(
    w_qkv=((D, 3 * D), LOW),
    w_out=((D, D), LOW),
    w_cross=((D, 2 * D), LOW),
    w_up=((D, FF), LOW),
    w_down=((FF, D), LOW),
)
HELD = dict(tokens=((BOTH, D), LOW), cotangent=((BOTH, D), LOW))
STATE = dict(
    proj=((BOTH, 3 * D), LOW),
    mix=((BOTH, D), LOW),
    probs=((MB, PAIRS, 2 * ROWS, ROWS), F32),
    wide=((BOTH, FF), F32),
    mid=((BOTH, D), F32),
    act=((BOTH, FF), LOW),
    narrow=((BOTH, D), LOW),
    result=((BOTH, D), LOW),
    left_a=((BOTH, D), LOW),
    query=((BOTH, D), LOW),
    across=((BOTH, ROWS), F32),
)
BACK = dict(
    hidden=((BOTH, FF), F32),
    across_mid=((BOTH, D), F32),
    left_b=((BOTH, D), LOW),
    right=((BOTH, 2 * D), LOW),
    grad_hidden=((BOTH, FF), LOW),
    gate=((BOTH, D), LOW),
    grad=((BOTH, D), F32),
    grad_low=((BOTH, D), LOW),
)


def shaped(table):
    return [pltpu.VMEM(shape, kind) for shape, kind in table.values()]


def same_shape(arrays):
    return [pltpu.VMEM(value.shape, value.dtype) for value in arrays]


def held(arrays):
    return [pltpu.with_memory_space_constraint(value, pltpu.VMEM) for value in arrays]


def in_place(place):
    return pltpu.with_memory_space_constraint(place, pltpu.SMEM)


def left(arrays):
    return [pltpu.with_memory_space_constraint(value, pltpu.HBM) for value in arrays]


def in_vmem():
    return pl.BlockSpec(memory_space=pltpu.VMEM)


def in_smem():
    return pl.BlockSpec(memory_space=pltpu.SMEM)


def in_hbm():
    return pl.BlockSpec(memory_space=pltpu.HBM)


TOKEN = ((8, LANES), F32)


def mflop(count):
    return count * 1_000_000, 0


def call(
    kernel, name, place, token, reads, keeps, makes, stores=None, scratch=(), cost=(0, 0), patches=None
):
    stores, patches = stores or {}, patches or {}
    out_shape = same_shape(keeps.values()) + shaped(makes) + shaped(dict(token=TOKEN))
    out_shape += [pltpu.HBM(shape, kind) for shape, kind in stores.values()]
    out_shape += [pltpu.HBM(value.shape, value.dtype) for value in patches.values()]
    reads_n, keeps_n, makes_n = len(reads), len(keeps), len(makes)
    stores_n, patches_n = len(stores), len(patches)
    aliases = {2 + reads_n + i: i for i in range(keeps_n)}
    for i in range(patches_n):
        aliases[2 + reads_n + keeps_n + i] = keeps_n + makes_n + 1 + stores_n + i

    def body(place_ref, token_in, *refs):
        del token_in
        refs = list(refs)
        named = dict(zip(reads, refs[:reads_n]))
        refs = refs[reads_n + keeps_n + patches_n :]
        named.update(zip(keeps, refs[:keeps_n]))
        named.update(zip(makes, refs[keeps_n : keeps_n + makes_n]))
        refs = refs[keeps_n + makes_n :]
        refs[0][...] = jnp.zeros(*TOKEN)
        named.update(zip(stores, refs[1 : 1 + stores_n]))
        refs = refs[1 + stores_n :]
        named.update(zip(patches, refs[:patches_n]))
        kernel(place_ref, SimpleNamespace(**named), *refs[patches_n:])

    results = pl.pallas_call(
        body,
        out_shape=out_shape,
        in_specs=[in_smem()] + [in_vmem()] * (1 + reads_n + keeps_n) + [in_hbm()] * patches_n,
        out_specs=[in_vmem()] * (keeps_n + makes_n + 1) + [in_hbm()] * (stores_n + patches_n),
        scratch_shapes=list(scratch),
        input_output_aliases=aliases,
        compiler_params=pltpu.CompilerParams(vmem_limit_bytes=16 * MIB),
        cost_estimate=pl.CostEstimate(flops=cost[0], bytes_accessed=cost[1], transcendentals=0),
        name=name,
    )(
        in_place(place),
        *held([token]),
        *held(reads.values()),
        *held(keeps.values()),
        *left(patches.values()),
    )
    names = list(keeps) + list(makes)
    token = results[len(names)]
    made = dict(zip(names, results))
    made.update(zip(list(stores) + list(patches), results[len(names) + 1 :]))
    return token, made


def forward_step(micro, encoder, lengths_ref, ref, link, gets):
    rows = slice(micro * ROWS, (micro + 1) * ROWS)
    gets.tokens.wait()
    tokens = ref.tokens[rows, :]
    gets.w_qkv[0].wait()
    gets.lengths.wait()
    if encoder:
        mask = segments(lengths_ref, micro, 0, 0) == segments(lengths_ref, micro, 0, 1)
    else:
        seg_tgt = segments(lengths_ref, micro, 1, 1)
        source = segments(lengths_ref, micro, 0, 0)
        ref.across[rows, :] = (source == seg_tgt).astype(F32)
        earlier = lax.broadcasted_iota(jnp.int32, (ROWS, ROWS), 0) <= lax.broadcasted_iota(
            jnp.int32, (ROWS, ROWS), 1
        )
        mask = (segments(lengths_ref, micro, 1, 0) == seg_tgt) & earlier
    for part in range(3):
        cut = slice(part * D, (part + 1) * D)
        if part:
            gets.w_qkv[part].wait()
        ref.proj[rows, cut] = mm(tokens, ref.w_qkv[:, cut]).astype(LOW)

    def write_probs(pair, value):
        ref.probs[micro, pair] = value

    def write_mix(pair, value):
        ref.mix[rows, pair * LANES : (pair + 1) * LANES] = value

    attend(
        columns(ref.proj, rows, 0),
        columns(ref.proj, rows, D),
        columns(ref.proj, rows, 2 * D),
        mask,
        write_probs,
        write_mix,
    )
    gets.w_out.wait()
    mid = tokens.astype(F32) + mm(ref.mix[rows, :], ref.w_out[...])

    if not encoder:
        ref.left_a[rows, :] = mid.astype(LOW)
        ref.mid[rows, :] = mid
        return
    ref.narrow[rows, :] = mid.astype(LOW)
    gets.w_up.wait()
    gets.w_down.wait()
    for part in range(4):
        cut = slice(part * D, (part + 1) * D)
        hidden = mm(ref.narrow[rows, :], ref.w_up[:, cut])
        ref.wide[rows, cut] = hidden
        ref.act[rows, cut] = gelu(hidden).astype(LOW)
    total = mid + mm(ref.act[rows, :], ref.w_down[...])
    ref.result[rows, :] = total.astype(LOW)
    gets.w_cross.wait()
    link[...] = mm(ref.result[rows, :], ref.w_cross[...]).astype(LOW)
    ref.left_a[rows, :] = ref.result[rows, :]


def decoder_ahead(ref, gets):
    gets.w_cross.wait()
    ref.query[...] = mm(ref.left_a[...], ref.w_cross[:, :D]).astype(LOW)
    gets.cotangent.wait()
    gets.w_down.wait()
    for part in range(4):
        cut = slice(part * D, (part + 1) * D)
        ref.wide[:, cut] = mm_nt(ref.cotangent[...], ref.w_down[cut, :])
    gets.w_up.wait()


class Fetch:
    def __init__(self, source, target, sem):
        self.copy = pltpu.make_async_copy(source, target, sem)

    def start(self):
        self.copy.start()

    def wait(self):
        self.copy.wait()


class Arrived:
    def wait(self):
        pass


def fetches(ref, sems, lengths_ref, sources):
    lengths_in, tokens_in, qkv_in, out_in, up_in, down_in, cross_in, cotangent_in = sources
    parts = [pl.ds(part * D, D) for part in range(3)]
    return SimpleNamespace(
        lengths=Fetch(lengths_in, lengths_ref, sems.at[0]),
        tokens=Fetch(tokens_in.at[0], ref.tokens, sems.at[1]),
        w_qkv=[
            Fetch(qkv_in.at[0, :, part], ref.w_qkv.at[:, part], sems.at[2 + at])
            for at, part in enumerate(parts)
        ],
        w_out=Fetch(out_in.at[0], ref.w_out, sems.at[5]),
        w_up=Fetch(up_in.at[0], ref.w_up, sems.at[6]),
        w_down=Fetch(down_in.at[0], ref.w_down, sems.at[7]),
        w_cross=Fetch(cross_in.at[0], ref.w_cross, sems.at[8]),
        cotangent=Fetch(cotangent_in.at[0], ref.cotangent, sems.at[9]),
    )


def start_all(gets):
    order = [gets.lengths, gets.tokens, *gets.w_qkv, gets.w_out, gets.w_up, gets.w_down, gets.w_cross]
    for get in order:
        get.start()


FETCHED = 8
FETCH_SCRATCH = [pltpu.SMEM((MB, 2, SLOTS), jnp.int32), pltpu.SemaphoreType.DMA((FETCHED + 2,))]


def first_stage(given):
    makes = {**WEIGHTS, **HELD, **STATE, **dict(link=((ROWS, 2 * D), LOW), token=TOKEN)}

    def body(*refs):
        place_ref, lengths_ref, sems = refs[FETCHED + len(makes) :]
        ref = SimpleNamespace(**dict(zip(makes, refs[FETCHED:])))
        index = lax.axis_index(DP).astype(jnp.int32)
        section = lax.axis_index(SECTION).astype(jnp.int32)
        place_ref[0] = section
        for bit in range(PLACE - 1):
            place_ref[1 + bit] = (index >> bit) % 2
        ref.token[...] = jnp.zeros(*TOKEN)

        @pl.when(section == 0)
        def _():
            gets = fetches(ref, sems, lengths_ref, refs[:FETCHED])
            start_all(gets)
            forward_step(0, True, lengths_ref, ref, ref.link, gets)

    results = pl.pallas_call(
        body,
        out_shape=shaped(makes) + [pltpu.SMEM((PLACE,), jnp.int32)],
        in_specs=[in_hbm()] * FETCHED,
        out_specs=[in_vmem()] * len(makes) + [in_smem()],
        scratch_shapes=FETCH_SCRATCH,
        compiler_params=pltpu.CompilerParams(vmem_limit_bytes=16 * MIB),
        cost_estimate=pl.CostEstimate(
            flops=2 * ROWS * D * 7168, bytes_accessed=10_000_000, transcendentals=0
        ),
        name="first_stage",
    )(*left(given))
    made = SimpleNamespace(**dict(zip(makes, results)))
    link, token = made.link, made.token
    del made.link, made.token
    return results[-1], token, link, made


def second_stage(place, state, given):
    kept = {**WEIGHTS, **HELD, **STATE}
    keeps = [getattr(state, name) for name in kept]

    def body(place_ref, *refs):
        sources = refs[:FETCHED]
        refs = refs[FETCHED + len(keeps) :]
        ref = SimpleNamespace(**dict(zip(kept, refs)))
        link, lengths_ref, sems = refs[len(keeps) :]
        gets = fetches(ref, sems, lengths_ref, sources)
        here = Arrived()

        @pl.when(place_ref[0] == 0)
        def _():
            gets.lengths.start()
            gets.cotangent.start()
            arrived = SimpleNamespace(
                lengths=gets.lengths,
                tokens=here,
                w_qkv=[here] * 3,
                w_out=here,
                w_up=here,
                w_down=here,
                w_cross=here,
            )
            forward_step(1, True, lengths_ref, ref, link, arrived)
            gets.cotangent.wait()

        @pl.when(place_ref[0] != 0)
        def _():
            start_all(gets)
            gets.cotangent.start()
            forward_step(0, False, lengths_ref, ref, link, gets)
            arrived = SimpleNamespace(lengths=here, tokens=here, w_qkv=[here] * 3, w_out=here)
            forward_step(1, False, lengths_ref, ref, link, arrived)
            decoder_ahead(ref, gets)

    results = pl.pallas_call(
        body,
        out_shape=same_shape(keeps) + [pltpu.VMEM((ROWS, 2 * D), LOW)],
        in_specs=[in_smem()] + [in_hbm()] * FETCHED + [in_vmem()] * len(keeps),
        out_specs=[in_vmem()] * (len(keeps) + 1),
        scratch_shapes=FETCH_SCRATCH,
        input_output_aliases={1 + FETCHED + i: i for i in range(len(keeps))},
        compiler_params=pltpu.CompilerParams(vmem_limit_bytes=16 * MIB),
        cost_estimate=pl.CostEstimate(
            flops=2 * ROWS * D * 7168, bytes_accessed=10_000_000, transcendentals=0
        ),
        name="second_stage",
    )(in_place(place), *left(given), *held(keeps))
    vars(state).update(zip(kept, results))
    return results[-1]


def middle_step(micro, ref):
    rows = slice(micro * ROWS, (micro + 1) * ROWS)
    whole = slice(0, ROWS)

    def write_probs(pair, value):
        ref.link_probs[pair] = value

    def write_mix(pair, value):
        ref.left_b[rows, pair * LANES : (pair + 1) * LANES] = value

    attend(
        columns(ref.query, rows, 0),
        columns(ref.link, whole, 0),
        columns(ref.link, whole, D),
        ref.across[rows, :] != 0.0,
        write_probs,
        write_mix,
    )
    after = ref.mid[rows, :] + mm(ref.left_b[rows, :], ref.w_cross[:, D:])
    ref.across_mid[rows, :] = after
    ref.narrow[rows, :] = after.astype(LOW)
    grad = ref.cotangent[rows, :].astype(F32)
    for part in range(4):
        cut = slice(part * D, (part + 1) * D)
        hidden = mm(ref.narrow[rows, :], ref.w_up[:, cut])
        ref.hidden[rows, cut] = hidden
        grad_hidden = (gelu_slope(hidden) * ref.wide[rows, cut]).astype(LOW)
        ref.grad_hidden[rows, cut] = grad_hidden
        grad = grad + mm_nt(grad_hidden, ref.w_up[:, cut])
    ref.grad[rows, :] = grad
    ref.right[rows, D:] = grad.astype(LOW)
    ref.mixed[...] = mm_nt(ref.right[rows, D:], ref.w_cross[:, D:]).astype(LOW)

    def write(pair, grad_v):
        ref.values_grad[:, pair * LANES : (pair + 1) * LANES] = grad_v.astype(LOW)

    attend_back_values(lambda pair: ref.link_probs[pair], columns(ref.mixed, whole, 0), write)


def middle_keys(micro, ref):
    rows = slice(micro * ROWS, (micro + 1) * ROWS)
    whole = slice(0, ROWS)

    def write(pair, grad_q, grad_k):
        cut = slice(pair * LANES, (pair + 1) * LANES)
        ref.right[rows, cut] = grad_q.astype(LOW)
        ref.keys_grad[:, cut] = grad_k.astype(LOW)

    attend_back_keys(
        columns(ref.query, rows, 0),
        columns(ref.link, whole, 0),
        columns(ref.link, whole, D),
        lambda pair: ref.link_probs[pair],
        columns(ref.mixed, whole, 0),
        write,
    )


def two_sides(link_grad):
    return link_grad.at[pl.ds(0, ROWS)], link_grad.at[pl.ds(ROWS, ROWS)]


LINK_STATE = dict(link_probs=((PAIRS, 2 * ROWS, ROWS), F32), mixed=((ROWS, D), LOW))
SIDE = ((ROWS, D), LOW)


def middle_stage(micro, place, token, state, link):
    reads = dict(
        query=state.query,
        across=state.across,
        mid=state.mid,
        cotangent=state.cotangent,
        w_cross=state.w_cross,
        w_up=state.w_up,
        link=link,
    )
    keeps = dict(narrow=state.narrow, wide=state.wide)
    makes, scratch = {}, ()
    if micro == 0:
        makes.update(link_grad=((2 * ROWS, D), LOW), **BACK)
        scratch = shaped(LINK_STATE)
    else:
        makes.update(values_grad=SIDE, **LINK_STATE)
        keeps.update((name, getattr(state, name)) for name in BACK)

    def kernel(place_ref, ref, *own):
        vars(ref).update(zip(LINK_STATE, own))

        @pl.when(place_ref[0] != 0)
        def _():
            if micro == 0:
                ref.keys_grad, ref.values_grad = two_sides(ref.link_grad)
            middle_step(micro, ref)
            if micro == 0:
                middle_keys(micro, ref)

        @pl.when(place_ref[0] == 0)
        def _():
            rows = slice(micro * ROWS, (micro + 1) * ROWS)
            for part in range(4):
                cut = slice(part * D, (part + 1) * D)
                ref.wide[rows, cut] = gelu_slope(ref.wide[rows, cut])

    cost = (2 * ROWS * D * 10000, 8_000_000)
    token, made = call(
        kernel, "middle_stage", place, token, reads, keeps, makes, scratch=scratch, cost=cost
    )
    vars(state).update(made)
    return token


def middle_keys_stage(micro, place, token, state, link):
    reads = dict(query=state.query, link=link, link_probs=state.link_probs, mixed=state.mixed)

    def kernel(place_ref, ref):
        @pl.when(place_ref[0] != 0)
        def _():
            middle_keys(micro, ref)

    cost = mflop(200)
    keeps, makes = dict(right=state.right), dict(keys_grad=SIDE)
    token, made = call(kernel, "middle_keys", place, token, reads, keeps, makes, cost=cost)
    vars(state).update(made)
    return token


def values_step(micro, first, ref):
    rows = slice(micro * ROWS, (micro + 1) * ROWS)

    @pl.when(first)
    def _():
        cotangent = ref.cotangent[rows, :].astype(F32)
        ref.grad[rows, :] = cotangent + mm_nt(ref.values_grad[...], ref.w_cross[:, D:])
        ref.right[rows, D:] = ref.values_grad[...]


def gate_step(micro, first, ref):
    rows = slice(micro * ROWS, (micro + 1) * ROWS)

    @pl.when(first)
    def _():
        grad = ref.grad[rows, :] + mm_nt(ref.keys_grad[...], ref.w_cross[:, :D])
        ref.grad[rows, :] = grad
        ref.gate[rows, :] = grad.astype(LOW)
        ref.right[rows, :D] = ref.keys_grad[...]
        ref.left_b[rows, :] = ref.left_a[rows, :]

    @pl.when(jnp.logical_not(first))
    def _():
        ref.gate[rows, :] = ref.cotangent[rows, :]
        for part in range(4):
            cut = slice(part * D, (part + 1) * D)
            ref.act[rows, cut] = gelu(ref.hidden[rows, cut]).astype(LOW)


def back_step(micro, first, ref):
    rows = slice(micro * ROWS, (micro + 1) * ROWS)

    @pl.when(first)
    def _():
        grad = ref.grad[rows, :]
        for part in range(4):
            cut = slice(part * D, (part + 1) * D)
            grad_act = mm_nt(ref.gate[rows, :], ref.w_down[cut, :])
            grad_hidden = (ref.wide[rows, cut] * grad_act).astype(LOW)
            ref.grad_hidden[rows, cut] = grad_hidden
            grad = grad + mm_nt(grad_hidden, ref.w_up[:, cut])
        ref.grad[rows, :] = grad
        ref.grad_low[rows, :] = grad.astype(LOW)

    @pl.when(jnp.logical_not(first))
    def _():
        grad = ref.grad[rows, :] + mm_nt(ref.right[rows, :D], ref.w_cross[:, :D])
        ref.grad[rows, :] = grad
        ref.grad_low[rows, :] = grad.astype(LOW)


def back_stage(micro, place, token, state, link_grad, parts, send=(), cost=5000):
    reads = dict(
        cotangent=state.cotangent,
        w_cross=state.w_cross,
        w_up=state.w_up,
        w_down=state.w_down,
        wide=state.wide,
        left_a=state.left_a,
        **link_grad,
        narrow=state.narrow,
        mix=state.mix,
    )
    keeps = {name: getattr(state, name) for name in BACK}
    keeps.update(act=state.act)
    makes = {}
    for at, chunk in enumerate(send):
        makes["send%d" % at] = ((chunk.rows, D), LOW)

    def kernel(place_ref, ref):
        if micro == 0:
            ref.keys_grad, ref.values_grad = two_sides(ref.link_grad)
        for part in parts:
            part(micro, place_ref[0] == 0, ref)
        for at, chunk in enumerate(send):
            put_send(place_ref, ref, chunk, getattr(ref, "send%d" % at))

    token, made = call(kernel, "back_stage", place, token, reads, keeps, makes, cost=mflop(cost))
    sends = [made.pop(name) for name in makes]
    vars(state).update(made)
    return token, sends


def late_kernel(place_ref, ref, mixed_v):
    mixed_v[...] = mm_nt(ref.grad_low[...], ref.w_out[...]).astype(LOW)
    for micro in range(MB):
        rows = slice(micro * ROWS, (micro + 1) * ROWS)

        def write(pair, *grads, rows=rows, first=0):
            for part, value in enumerate(grads):
                at = (first + part) * D + pair * LANES
                rounded, rest = in_two(value)
                ref.grad_proj[rows, at : at + LANES] = rounded
                ref.grad_rest[rows, at : at + LANES] = rest

        def read_probs(pair, micro=micro):
            return ref.probs[micro, pair]

        attend_back_keys(
            columns(ref.proj, rows, 0),
            columns(ref.proj, rows, D),
            columns(ref.proj, rows, 2 * D),
            read_probs,
            columns(mixed_v, rows, 0),
            write,
        )
        attend_back_values(
            read_probs,
            columns(mixed_v, rows, 0),
            lambda pair, value, write=write: write(pair, value, first=2),
        )
    for here, gradient, run in QKV.each():
        value = product_of(gradient, ref, run, 1 - place_ref[1])
        ref.send[here, :], ref.more[here, :] = in_two(value)


def late_stage(place, token, state, cost):
    reads = dict(
        grad_low=state.grad_low,
        w_out=state.w_out,
        proj=state.proj,
        probs=state.probs,
        tokens=state.tokens,
        mix=state.mix,
    )
    wide, side = ((BOTH, 3 * D), LOW), ((QKV.rows, D), LOW)
    makes = dict(grad_proj=wide, grad_rest=wide, send=side, more=side)
    scratch = (pltpu.VMEM((BOTH, D), LOW),)
    token, made = call(
        late_kernel, "late_stage", place, token, reads, {}, makes, None, scratch, mflop(cost)
    )
    sends = made.pop("send"), made.pop("more")
    vars(state).update(made)
    return token, sends


def final_kernel(place_ref, ref, result_v, grad_v, sems):
    @pl.when(place_ref[0] == 0)
    def _():
        result_v[...] = ref.result[...]

    @pl.when(place_ref[0] != 0)
    def _():
        total = ref.across_mid[...]
        for part in range(4):
            cut = slice(part * D, (part + 1) * D)
            total = total + mm(ref.act[:, cut], ref.w_down[cut, :])
        result_v[...] = total.astype(LOW)

    first = fetch(result_v, ref.outputs.at[0], sems.at[0])
    grad_v[...] = (ref.grad[...] + mm_nt(ref.grad_proj[...], ref.w_qkv[...])).astype(LOW)
    second = fetch(grad_v, ref.input_grad.at[0], sems.at[1])
    first.wait()
    second.wait()


def final_stage(place, token, state, cost):
    reads = dict(
        grad=state.grad,
        grad_proj=state.grad_proj,
        w_qkv=state.w_qkv,
        result=state.result,
        across_mid=state.across_mid,
        act=state.act,
        w_down=state.w_down,
    )
    half = ((1, BOTH, D), LOW)
    stores = dict(outputs=half, input_grad=half)
    scratch = [pltpu.VMEM((BOTH, D), LOW)] * 2 + [pltpu.SemaphoreType.DMA((2,))]
    return call(
        final_kernel, "final_stage", place, token, reads, {}, {}, stores, scratch, mflop(cost)
    )


PIECE = HALF // 2
PIECES = 7

Y_FIRST = (1, 2, 3)
Z_FIRST = (2, 1, 3)


def cut_of(part):
    return slice(part * D, (part + 1) * D)


class Gradient:
    def __init__(self, sides, store, down=False):
        self.sides = sides
        self.store = store
        self.down = down

    def rows(self, part, half, first, count):
        start = (part * D if self.down else 0) + first * PIECE
        return pl.ds(pl.multiple_of(start + half * HALF, PIECE), count * PIECE)

    def product(self, ref, part, half, first, count):
        left_ref, right_ref, column, *rest = self.sides(ref, part)
        value = left_ref[:, self.rows(part, half, first, count)]
        total = mm_tn(value, right_ref[:, cut_of(column)])
        for rest_ref in rest:
            total = total + mm_tn(value, rest_ref[:, cut_of(column)])
        return total

    def target(self, array, part, half, first, count):
        column = 0 if self.down else part * D
        return array.at[0, self.rows(part, half, first, count), pl.ds(column, D)]


G_DOWN = Gradient(lambda ref, part: (ref.act, ref.gate, 0), dict(g_down=((1, FF, D), F32)), down=True)
G_UP = Gradient(lambda ref, part: (ref.narrow, ref.grad_hidden, part), dict(g_up=((1, D, FF), F32)))
G_CROSS = Gradient(
    lambda ref, part: ((ref.left_a, ref.left_b)[part], ref.right, part),
    dict(g_cross=((1, D, 2 * D), F32)),
)
G_OUT = Gradient(lambda ref, part: (ref.mix, ref.grad_low, 0), dict(g_out=((1, D, D), F32)))
G_QKV = Gradient(
    lambda ref, part: (ref.tokens, ref.grad_proj, part, ref.grad_rest),
    dict(g_qkv=((1, D, 3 * D), F32)),
)


class Chunk:
    def __init__(self, levels, operands, runs, fine=False):
        self.levels = levels
        self.fine = fine
        self.operands = operands
        self.runs = runs
        self.rows = PIECES * PIECE
        self.stores = {}
        for run in runs:
            self.stores.update(run[0].store)

    def each(self):
        at = 0
        for gradient, part, first, count in self.runs:
            yield slice(at, at + count * PIECE), gradient, (part, first, count)
            at += count * PIECE


def product_of(gradient, ref, run, half):
    part, first, count = run
    return gradient.product(ref, part, half, first, count)


CROSS = Chunk(
    (Y_FIRST, Z_FIRST),
    lambda state: dict(
        left_a=state.left_a,
        left_b=state.left_b,
        right=state.right,
        mix=state.mix,
        grad_low=state.grad_low,
        act=state.act,
        gate=state.gate,
        narrow=state.narrow,
        grad_hidden=state.grad_hidden,
    ),
    [(G_CROSS, 0, 0, 2), (G_CROSS, 1, 0, 2), (G_OUT, 0, 0, 1), (G_DOWN, 3, 1, 1), (G_UP, 3, 1, 1)],
)
DOWN = Chunk(
    (Y_FIRST, Z_FIRST),
    lambda state: dict(act=state.act, gate=state.gate),
    [(G_DOWN, 0, 0, 2), (G_DOWN, 1, 0, 2), (G_DOWN, 2, 0, 2), (G_DOWN, 3, 0, 1)],
)
UP = Chunk(
    (Y_FIRST, Z_FIRST),
    lambda state: dict(narrow=state.narrow, grad_hidden=state.grad_hidden),
    [(G_UP, 0, 0, 2), (G_UP, 1, 0, 2), (G_UP, 2, 0, 2), (G_UP, 3, 0, 1)],
)
QKV = Chunk(
    (Z_FIRST, Y_FIRST),
    lambda state: dict(
        tokens=state.tokens,
        grad_proj=state.grad_proj,
        grad_rest=state.grad_rest,
        mix=state.mix,
        grad_low=state.grad_low,
    ),
    [(G_QKV, 0, 0, 2), (G_QKV, 1, 0, 2), (G_QKV, 2, 0, 2), (G_OUT, 0, 1, 1)],
    fine=True,
)


def put_send(place_ref, ref, chunk, send):
    for here, gradient, run in chunk.each():
        send[here, :] = product_of(gradient, ref, run, 1 - place_ref[1]).astype(LOW)


class Summing:
    def __init__(self, chunk, state, place, count):
        self.chunk = chunk
        self.state = state
        self.place = place
        self.count = count
        self.depth = count.bit_length() - 2
        self.step = 0

    def swap(self, value, level):
        def partner(i):
            bit = self.chunk.levels[i % 2][level - 1] if 0 < level < 4 else level
            return i ^ (1 << bit)

        return lax.ppermute(value, "dp", [(i, partner(i)) for i in range(self.count)])

    def call(self, kernel, token, reads, makes, stores=None, scratch=(), patches=None):
        name = "sum_%d" % self.step
        rest = (stores, scratch, mflop(self.cost), patches)
        return call(kernel, name, self.place, token, reads, {}, makes, *rest)

    def halves(self, place_ref, level, rows):
        first, second = (place_ref[1 + levels[level - 1]] for levels in self.chunk.levels)
        bit = jnp.where(place_ref[1] == 0, first, second)
        half = rows // 2
        own = pl.ds(pl.multiple_of(bit * half, half), half)
        return own, pl.ds(pl.multiple_of((1 - bit) * half, half), half)

    def launch(self, send, *more):
        self.got = self.swap(send, 0)
        self.more = dict(more=self.swap(*more, 0)) if more else {}

    def start(self, token, cost):
        def kernel(place_ref, ref):
            put_send(place_ref, ref, self.chunk, ref.send)

        makes = dict(send=((self.chunk.rows, D), LOW))
        reads = self.chunk.operands(self.state)
        token, made = call(kernel, "product", self.place, token, reads, {}, makes, cost=mflop(cost))
        self.launch(made["send"])
        return token

    def advance(self, token, grads, cost):
        self.cost = cost
        rows = self.chunk.rows
        if self.step == 0:
            token = self.split_first(token, rows)
        elif self.step == 1:
            token = self.split(token, rows // 2)
        elif self.step == 2:
            token = self.round_off(token, rows // 4)
        elif self.step == 3:
            for level in range(4, self.depth + 1):
                token = self.pair_sum(token, rows // 4, level, False)
            token = self.pair_sum(token, rows // 4, 2, True)
        elif self.step == 4:
            token = self.merge(token, rows // 4, 1)
        elif self.step == 5:
            token = self.merge(token, rows // 2, 0)
        else:
            token = self.unpack(token, grads, False, cost)
        self.step += 1
        return token

    def split_first(self, token, rows):
        chunk = self.chunk

        def kernel(place_ref, ref, total):
            for here, gradient, run in chunk.each():
                own = product_of(gradient, ref, run, place_ref[1])
                total[here, :] = own + ref.got[here, :].astype(F32)
                if chunk.fine:
                    total[here, :] = total[here, :] + ref.more[here, :].astype(F32)
            own, other = self.halves(place_ref, 1, rows)
            ref.send[...] = total[other, :].astype(LOW)
            ref.keep[...] = total[own, :]

        reads = dict(got=self.got, **self.more, **chunk.operands(self.state))
        makes = dict(send=((rows // 2, D), LOW), keep=((rows // 2, D), F32))
        scratch = (pltpu.VMEM((rows, D), F32),)
        token, made = self.call(kernel, token, reads, makes, scratch=scratch)
        self.keep = made["keep"]
        self.got = self.swap(made["send"], 1)
        return token

    def split(self, token, rows):
        def kernel(place_ref, ref):
            own, other = self.halves(place_ref, 2, rows)
            ref.send[...] = (ref.keep[other, :] + ref.got[other, :].astype(F32)).astype(LOW)
            ref.kept[...] = ref.keep[own, :] + ref.got[own, :].astype(F32)

        reads = dict(keep=self.keep, got=self.got)
        makes = dict(send=((rows // 2, D), LOW), kept=((rows // 2, D), F32))
        token, made = self.call(kernel, token, reads, makes)
        self.keep = made["kept"]
        self.got = self.swap(made["send"], 2)
        return token

    def round_off(self, token, rows):
        fine = False

        def kernel(place_ref, ref):
            total = ref.keep[...] + ref.got[...].astype(F32)
            if fine:
                ref.piece[...], ref.rest[...] = in_two(total)
            else:
                ref.piece[...] = total.astype(LOW)

        side = ((rows, D), LOW)
        makes = dict(piece=side, rest=side) if fine else dict(piece=side)
        token, made = self.call(kernel, token, dict(keep=self.keep, got=self.got), makes)
        self.spread(made, 3)
        return token

    def spread(self, made, level):
        self.piece = made["piece"]
        self.got = self.swap(self.piece, level)
        self.more = {}
        if "rest" in made:
            self.more = dict(rest=made["rest"], more=self.swap(made["rest"], level))

    def pair_sum(self, token, rows, level, last):
        fine = False

        def kernel(place_ref, ref):
            own, other = ref.held[...].astype(F32), ref.got[...].astype(F32)
            if fine:
                own, other = own + ref.rest[...].astype(F32), other + ref.more[...].astype(F32)
            if fine and not last:
                ref.piece[...], ref.rest_out[...] = in_two(own + other)
            else:
                ref.piece[...] = (own + other).astype(LOW)

        side = ((rows, D), LOW)
        makes = dict(piece=side, rest_out=side) if fine and not last else dict(piece=side)
        reads = dict(held=self.piece, got=self.got, **self.more)
        token, made = self.call(kernel, token, reads, makes)
        if "rest_out" in made:
            made["rest"] = made.pop("rest_out")
        self.spread(made, level)
        return token

    def merge(self, token, rows, level):
        def kernel(place_ref, ref):
            own, other = self.halves(place_ref, level + 1, 2 * rows)
            ref.piece[own, :] = ref.held[...]
            ref.piece[other, :] = ref.got[...]

        makes = dict(piece=((2 * rows, D), LOW))
        token, made = self.call(kernel, token, dict(held=self.piece, got=self.got), makes)
        self.piece = made["piece"]
        self.got = self.swap(self.piece, level)
        return token

    def unpack(self, token, grads, own, cost):
        chunk = self.chunk
        patches = {name: grads[name] for name in chunk.stores if name in grads}
        stores = {name: kind for name, kind in chunk.stores.items() if name not in grads}

        def kernel(place_ref, ref, wide, sems):
            half = place_ref[1] if own else 1 - place_ref[1]
            copies = []
            for index, (here, gradient, (part, first, count)) in enumerate(chunk.each()):
                wide[here, :] = ref.source[here, :].astype(F32)
                array = getattr(ref, list(gradient.store)[0])
                target = gradient.target(array, part, half, first, count)
                rows = pl.ds(here.start, here.stop - here.start)
                copies.append(fetch(wide.at[rows], target, sems.at[index]))
            for copy in copies:
                copy.wait()

        scratch = (pltpu.VMEM((chunk.rows, D), F32), pltpu.SemaphoreType.DMA((len(chunk.runs),)))
        reads = dict(source=self.piece if own else self.got)
        name = "unpack_%d" % own
        token, made = call(
            kernel, name, self.place, token, reads, {}, {}, stores, scratch, mflop(cost), patches
        )
        grads.update(made)
        return token


CHUNKS = (DOWN, CROSS, UP, QKV)
GATE, BACK_ATTN, BACK_FFN, FINAL, MORE, OWN = 10, 11, 12, 13, 14, 20
ORDER = (10, 12, 0, 14, 1, 11, 2, 0, 3, 1, 0, 2, 13, 1, 3, 0, 2, 1, 3, 0, 2, 1, 3, 0, 2, 20, 1, 21, 3, 0, 2, 1, 22, 3, 2, 23, 3)
COSTS = (1000, 1000, 8000, 4000, 8000, 8000, 4000, 8000, 1000, 1000, 1000, 1000, 1000, 1000, 1000, 1000, 1000, 1000, 1000, 1000, 1000, 1000, 1000, 1000, 8000, 8000, 1000, 8000, 1000, 1000, 1000, 1000, 1000, 50, 3000, 1000, 1000)


def on_device(inputs, lengths, w_qkv, w_attn_out, w_cross, w_up, w_down, cotangent):
    count = lax.axis_size("dp")
    given = (lengths, inputs, w_qkv, w_attn_out, w_up, w_down, w_cross, cotangent)
    place, token, link, state = first_stage(given)
    links = [lax.ppermute(link, "section", [(0, 1)])]
    link = second_stage(place, state, given)
    links.append(lax.ppermute(link, "section", [(0, 1)]))

    def to_encoder(side):
        return lax.ppermute(side, "section", [(1, 0)])

    token = middle_stage(0, place, token, state, links[0])
    grads = [dict(link_grad=to_encoder(state.link_grad))]
    token = middle_stage(1, place, token, state, links[1])
    values = to_encoder(state.values_grad)
    token = middle_keys_stage(1, place, token, state, links[1])
    grads.append(dict(keys_grad=to_encoder(state.keys_grad)))
    token, _ = back_stage(0, place, token, state, grads[0], (values_step, gate_step, back_step), cost=900)
    token, _ = back_stage(1, place, token, state, dict(values_grad=values), (values_step,), cost=300)
    chunks = [Summing(chunk, state, place, count) for chunk in CHUNKS]
    made = {}
    for task, cost in zip(ORDER, COSTS):
        if task == GATE:
            token, sends = back_stage(1, place, token, state, grads[1], (gate_step,), [DOWN], cost)
            chunks[0].launch(*sends)
        elif task == BACK_FFN:
            token, sends = back_stage(1, place, token, state, grads[1], (back_step,), [CROSS], cost)
            chunks[1].launch(*sends)
        elif task == MORE:
            token = chunks[2].start(token, cost)
        elif task == BACK_ATTN:
            token, sends = late_stage(place, token, state, cost)
            chunks[3].launch(*sends)
        elif task == FINAL:
            token, ends = final_stage(place, token, state, cost)
            made.update(ends)
        elif task >= OWN:
            token = chunks[task - OWN].unpack(token, made, True, cost)
        else:
            token = chunks[task].advance(token, made, cost)
    done = SimpleNamespace(**made)
    return (
        done.outputs,
        done.input_grad,
        done.g_qkv,
        done.g_out,
        done.g_cross,
        done.g_up,
        done.g_down,
    )


def solution(mesh):
    return jax.shard_map(
        on_device,
        mesh=mesh,
        in_specs=(
            P("section", "dp", None),
            P("dp", None, None),
            P("section", None, None),
            P("section", None, None),
            P("section", None, None),
            P("section", None, None),
            P("section", None, None),
            P("section", "dp", None),
        ),
        out_specs=(
            P("section", "dp", None),
            P("section", "dp", None),
            P("section", None, None),
            P("section", None, None),
            P("section", None, None),
            P("section", None, None),
            P("section", None, None),
        ),
        check_vma=False,
    )
```
